32 devices in a mesh: seq: 8 (over z, core), chan: 4 (over y, x).
Axes of the slice: x: 2, y: 2, z: 4, core: 2. Of those that a mesh axis runs over, the one named last changes fastest.
Arguments:
- values: bfloat16 [2048, 4096], P('seq', 'chan'), may hold values from -6 to 6
- gate_in: bfloat16 [2048, 4096], P('seq', 'chan'), may hold values from -6 to 6
- gate_out: bfloat16 [2048, 4096], P('seq', 'chan'), may hold values from -6 to 6
- spectrum: float32 [2, 2, 1024, 4096], P(None, None, 'seq', 'chan'), may hold values from -6 to 6
- out_weight: bfloat16 [4096, 8192], P('chan'), may hold values from -0.125 to 0.125
Outputs:
- mixed: bfloat16 [2048, 8192], P('seq', 'chan')
The draws below stay inside these ranges and needn't reach their ends.
All inputs are finite; a program needn't handle non-finite values.
Results may differ from the reference program's by a relative error of at most 0.024.
Values may be sent and summed in bfloat16 or wider, within the bound.
No kernel may reach another device: no remote copies, remote signals or barrier semaphores. Data moves between devices by JAX's collectives and lax.ppermute only.
A program may use at most 64 MiB of HBM per device.

```python
import math
import jax
import jax.numpy as jnp
from jax import lax

DIM = 8192
CHANNELS = 4096
BLOCK = 1024
TOKENS = 2048
SPAN = 2
N_CHAN = 4


def raised(values, stream_key, source, target, blocks, factor):
    owner, partner = [(jnp.arange(values.shape[dim]) // (values.shape[dim] // blocks)).reshape([-1 if axis == dim else 1 for axis in range(values.ndim)]) for dim in (source, target)]
    chosen = jax.random.permutation(stream_key, blocks)[partner]
    strong = (owner == chosen) | (owner == (partner + blocks // 2) % blocks)
    return jnp.where(strong, factor * values, values)


def level_of(key, shape, cuts, low, top_value):
    gain = 1.0
    for position, parts in cuts:
        draws = jax.random.uniform(jax.random.fold_in(jax.random.fold_in(key, 6), position), (parts,), jnp.float32, low / len(cuts), top_value / len(cuts))
        gain = gain * jnp.repeat(jnp.exp(draws), shape[position] // parts).reshape((-1,) + (1,) * (len(shape) - 1 - position))
    return gain


def scatter_about(rng, dims, deviation, limit, split=(), kind=jnp.bfloat16):
    loudness = level_of(rng, dims, split, -0.22, 0.18) if split else 1.0
    values = jax.random.normal(rng, dims, jnp.float32) * deviation * loudness
    return jnp.minimum(jnp.maximum(values, -limit), limit).astype(kind)


def bell_draw_with(stream_key, extent, spread, bound, shards, heavy, kind=jnp.bfloat16):
    entries = spread * jax.random.normal(stream_key, extent, jnp.float32)
    if shards:
        entries = entries * level_of(stream_key, extent, shards, -0.22, 0.18)
    return jnp.clip(raised(entries, jax.random.fold_in(stream_key, 3), *heavy), -bound, bound).astype(kind)


def setup_inputs(seed: int = 0) -> dict:
    splits = jax.random.split(jax.random.key(seed), 6)
    return {
        "values": scatter_about(splits[0], (TOKENS, CHANNELS), 1.0, 6.0, ((0, 8), (1, 4))),
        "gate_in": scatter_about(splits[1], (TOKENS, CHANNELS), 1.0, 6.0, ((0, 8), (1, 4))),
        "gate_out": scatter_about(splits[2], (TOKENS, CHANNELS), 1.0, 6.0, ((0, 8), (1, 4))),
        "spectrum": scatter_about(splits[3], (2, SPAN, BLOCK, CHANNELS), 1.0, 6.0, ((2, 8), (3, 4)), jnp.float32),
        "out_weight": bell_draw_with(splits[4], (CHANNELS, DIM), CHANNELS ** -0.5, 0.125, ((0, 4),), (0, 1, 4, 2.0)),
    }


def angle_table(first, second, period):
    product = (first[:, None] * second[None, :]) % period
    return product.astype(jnp.float32) * (2.0 * math.pi / period)


def settle(array):
    return lax.optimization_barrier(array.astype(jnp.bfloat16)).astype(jnp.float32)


def reference(values, gate_in, gate_out, spectrum, out_weight):
    span = TOKENS // BLOCK
    full_block = jnp.arange(BLOCK, dtype=jnp.int32)
    full_span = jnp.arange(span, dtype=jnp.int32)
    block_angle = angle_table(full_block, full_block, BLOCK)
    block_cos = jnp.cos(block_angle).astype(jnp.bfloat16).astype(jnp.float32)
    block_sin = jnp.sin(block_angle).astype(jnp.bfloat16).astype(jnp.float32)
    span_angle = angle_table(full_span, full_span, span)
    span_cos = jnp.cos(span_angle).astype(jnp.bfloat16).astype(jnp.float32)
    span_sin = jnp.sin(span_angle).astype(jnp.bfloat16).astype(jnp.float32)
    source = settle(values.astype(jnp.float32) * gate_in.astype(jnp.float32))
    grid = source.reshape(BLOCK, span, CHANNELS)
    cos_part = jnp.einsum('ac,abh->bch', block_cos, grid)
    sin_part = jnp.einsum('ac,abh->bch', block_sin, grid)
    turn = angle_table(full_span, full_block, TOKENS)
    turn_cos = jnp.cos(turn)[:, :, None]
    turn_sin = jnp.sin(turn)[:, :, None]
    twist_re = cos_part * turn_cos - sin_part * turn_sin
    twist_im = -sin_part * turn_cos - cos_part * turn_sin
    twisted = settle(jnp.stack([twist_re, twist_im]))
    with_cos = jnp.einsum('bd,kbch->kdch', span_cos, twisted)
    with_sin = jnp.einsum('bd,kbch->kdch', span_sin, twisted)
    freq_re = with_cos[0] + with_sin[1]
    freq_im = with_cos[1] - with_sin[0]
    prod_re = freq_re * spectrum[0] - freq_im * spectrum[1]
    prod_im = freq_re * spectrum[1] + freq_im * spectrum[0]
    product = settle(jnp.stack([prod_re, prod_im]))
    back_cos = jnp.einsum('db,kdch->kcbh', span_cos, product)
    back_sin = jnp.einsum('db,kdch->kcbh', span_sin, product)
    back_re = (back_cos[0] - back_sin[1]) / span
    back_im = (back_cos[1] + back_sin[0]) / span
    turn_back = jnp.transpose(turn)
    back_tc = jnp.cos(turn_back)[:, :, None]
    back_ts = jnp.sin(turn_back)[:, :, None]
    rotated_re = settle(back_re * back_tc - back_im * back_ts)
    rotated_im = settle(back_im * back_tc + back_re * back_ts)
    conv = (jnp.einsum('ac,cbh->abh', block_cos, rotated_re) - jnp.einsum('ac,cbh->abh', block_sin, rotated_im)) / BLOCK
    conv = settle(conv.reshape(TOKENS, CHANNELS))
    gated = (conv * gate_out.astype(jnp.float32)).astype(jnp.bfloat16)
    width = CHANNELS // N_CHAN
    total = jnp.zeros((TOKENS, DIM), jnp.float32)
    for group in range(N_CHAN):
        partial_sum = jnp.dot(gated[:, group * width:(group + 1) * width], out_weight[group * width:(group + 1) * width], preferred_element_type=jnp.float32)
        total = total + settle(partial_sum)
    return total.astype(jnp.bfloat16)
```

```python
import functools
import math

import jax
import jax.numpy as jnp
import ml_dtypes
import numpy as np
from jax import lax
from jax.experimental import pallas as pl
from jax.experimental.pallas import tpu as pltpu
from jax.sharding import PartitionSpec as P

BLOCK = 1024
LANES = 128


def angles(first, second, period):
    return (np.arange(first)[:, None] * np.arange(second)[None, :] % period) * (2.0 * math.pi / period)


def rounded(table):
    return jnp.asarray(table.astype(np.float32).astype(ml_dtypes.bfloat16))


def split_rows(rows, span):
    out = lax.broadcasted_iota(jnp.int32, (rows, rows), 0)
    token = lax.broadcasted_iota(jnp.int32, (rows, rows), 1)
    block_rows = rows // span
    return jnp.where(token == (out % block_rows) * span + out // block_rows, 1.0, 0.0).astype(jnp.bfloat16)


def join_rows(rows, span):
    token = lax.broadcasted_iota(jnp.int32, (rows, rows), 0)
    held = lax.broadcasted_iota(jnp.int32, (rows, rows), 1)
    block_rows = rows // span
    return jnp.where(token == (held % block_rows) * span + held // block_rows, 1.0, 0.0).astype(jnp.bfloat16)


def pack_kernel(span, values_ref, gate_ref, spectrum_ref, out_ref):
    rows = values_ref.shape[0]
    block_rows = rows // span
    source = (values_ref[...].astype(jnp.float32) * gate_ref[...].astype(jnp.float32)).astype(jnp.bfloat16)
    source = jnp.dot(split_rows(rows, span), source, preferred_element_type=jnp.float32).astype(jnp.bfloat16)
    for dest in range(out_ref.shape[0]):
        lanes = slice(dest * LANES, (dest + 1) * LANES)
        for part in range(2):
            for d in range(span):
                out_ref[dest, part * span + d] = spectrum_ref[part, d, :, lanes].astype(jnp.bfloat16)
        for b in range(span):
            out_ref[dest, 2 * span + b] = source[b * block_rows:(b + 1) * block_rows, lanes]


def pack(values, gate_in, spectrum, seq_count):
    rows, width = values.shape
    _, span, block_rows, _ = spectrum.shape
    per_step = 2
    cols = per_step * LANES
    return pl.pallas_call(
        functools.partial(pack_kernel, span),
        grid=(seq_count // per_step,),
        in_specs=[
            pl.BlockSpec((rows, cols), lambda i: (0, i)),
            pl.BlockSpec((rows, cols), lambda i: (0, i)),
            pl.BlockSpec((2, span, block_rows, cols), lambda i: (0, 0, 0, i)),
        ],
        out_specs=pl.BlockSpec((per_step, 3 * span, block_rows, LANES), lambda i: (i, 0, 0, 0)),
        out_shape=jax.ShapeDtypeStruct((seq_count, 3 * span, block_rows, LANES), jnp.bfloat16),
        compiler_params=pltpu.CompilerParams(vmem_limit_bytes=16 << 20),
        name="pack",
    )(values, gate_in, spectrum)


def conv_kernel(parts, data_ref, cos_ref, sin_ref, turn_cos_ref, turn_sin_ref, *refs):
    outs, (cols_ref, re_ref, im_ref) = refs[:parts], refs[parts:]
    shares, _, rows, _ = data_ref.shape
    for s in range(shares):
        for b in range(2):
            cols_ref[s * rows:(s + 1) * rows, b * LANES:(b + 1) * LANES] = data_ref[s, 4 + b]
    step = 2 * rows
    for i in range(shares * rows // step):
        at = slice(i * step, (i + 1) * step)
        cols = cols_ref[...]
        first_re = jnp.dot(cos_ref[at, :], cols, preferred_element_type=jnp.float32)
        first_sin = jnp.dot(sin_ref[at, :], cols, preferred_element_type=jnp.float32)
        tc, ts = turn_cos_ref[at, :], turn_sin_ref[at, :]
        re0, im0 = first_re[:, :LANES], -first_sin[:, :LANES]
        re1, im1 = first_re[:, LANES:], -first_sin[:, LANES:]
        re1, im1 = re1 * tc + im1 * ts, im1 * tc - re1 * ts

        def filt(part):
            return jnp.concatenate([data_ref[2 * i, part], data_ref[2 * i + 1, part]], axis=0).astype(jnp.float32)

        f0r, f0i, f1r, f1i = re0 + re1, im0 + im1, re0 - re1, im0 - im1
        s0r, s1r, s0i, s1i = filt(0), filt(1), filt(2), filt(3)
        p0r, p0i = f0r * s0r - f0i * s0i, f0r * s0i + f0i * s0r
        p1r, p1i = f1r * s1r - f1i * s1i, f1r * s1i + f1i * s1r
        b0r, b0i = 0.5 * (p0r + p1r), 0.5 * (p0i + p1i)
        b1r, b1i = 0.5 * (p0r - p1r), 0.5 * (p0i - p1i)
        b1r, b1i = b1r * tc - b1i * ts, b1i * tc + b1r * ts
        re_ref[at, :] = jnp.concatenate([b0r, b1r], axis=1).astype(jnp.bfloat16)
        im_ref[at, :] = jnp.concatenate([b0i, b1i], axis=1).astype(jnp.bfloat16)
    scale = 1.0 / (shares * rows)
    part_rows = rows // parts
    for i in range(shares * rows // step):
        at = slice(i * step, (i + 1) * step)
        conv = jnp.dot(cos_ref[at, :], re_ref[...], preferred_element_type=jnp.float32)
        conv = conv - jnp.dot(sin_ref[at, :], im_ref[...], preferred_element_type=jnp.float32)
        conv = (conv * scale).astype(jnp.bfloat16)
        for s in range(2):
            for p in range(parts):
                begin = s * rows + p * part_rows
                for b in range(2):
                    outs[p][2 * i + s, b] = conv[begin:begin + part_rows, b * LANES:(b + 1) * LANES]


def convolve(data, parts):
    shares, _, rows, _ = data.shape
    block = shares * rows
    angle = angles(block, block, block)
    turn = np.broadcast_to(angles(block, 2, 2 * block)[:, 1:], (block, LANES))
    vmem = pl.BlockSpec(memory_space=pltpu.VMEM)
    return pl.pallas_call(
        functools.partial(conv_kernel, parts),
        in_specs=[vmem] * 5,
        out_specs=[vmem] * parts,
        out_shape=[jax.ShapeDtypeStruct((shares, 2, rows // parts, LANES), jnp.bfloat16)] * parts,
        scratch_shapes=[pltpu.VMEM((block, 2 * LANES), jnp.bfloat16)] * 3,
        compiler_params=pltpu.CompilerParams(vmem_limit_bytes=32 << 20),
        name="convolve",
    )(
        data, rounded(np.cos(angle)), rounded(np.sin(angle)),
        jnp.asarray(np.cos(turn).astype(np.float32)), jnp.asarray(np.sin(turn).astype(np.float32)),
    )


def project_kernel(me_ref, conv_ref, gate_ref, weight_ref, first_ref, second_ref, gated_ref):
    step = pl.program_id(0)

    @pl.when(step == 0)
    def _():
        shares, span, part_rows, _ = conv_ref.shape
        join = join_rows(span * part_rows, span)
        for s in range(shares):
            lanes = slice(s * LANES, (s + 1) * LANES)
            held = conv_ref[s].reshape(span * part_rows, LANES)
            conv = jnp.dot(join, held, preferred_element_type=jnp.float32)
            gated_ref[:, lanes] = (conv * gate_ref[:, lanes].astype(jnp.float32)).astype(jnp.bfloat16)

    partial_sum = jnp.dot(gated_ref[...], weight_ref[...], preferred_element_type=jnp.float32).astype(jnp.bfloat16)

    @pl.when(step < 2)
    def _():
        first_ref[0] = partial_sum

    @pl.when(step >= 2)
    def _():
        second_ref[0] = partial_sum


def project(me, conv, gate, weight, part, blocks):
    shares, span, part_rows, _ = conv.shape
    depth, width = weight.shape
    rows = span * part_rows
    cols = width // 8
    (f0, h0), (f1, h1), (f2, h2), (f3, h3) = blocks

    def column(i, me_ref):
        flip = jnp.where(i == 0, f0, jnp.where(i == 1, f1, jnp.where(i == 2, f2, f3)))
        half = jnp.where(i == 0, h0, jnp.where(i == 1, h1, jnp.where(i == 2, h2, h3)))
        return 0, (me_ref[0] ^ flip) * 2 + half

    shape = jax.ShapeDtypeStruct((2, rows, cols), jnp.bfloat16)
    return pl.pallas_call(
        project_kernel,
        grid_spec=pltpu.PrefetchScalarGridSpec(
            num_scalar_prefetch=1,
            grid=(4,),
            in_specs=[
                pl.BlockSpec((shares, span, part_rows, LANES), lambda i, m: (0, 0, 0, 0)),
                pl.BlockSpec((rows, depth), lambda i, m: (part, 0)),
                pl.BlockSpec((depth, cols), column),
            ],
            out_specs=[
                pl.BlockSpec((1, rows, cols), lambda i, m: (jnp.minimum(i, 1), 0, 0)),
                pl.BlockSpec((1, rows, cols), lambda i, m: (jnp.maximum(i - 2, 0), 0, 0)),
            ],
            scratch_shapes=[pltpu.VMEM((rows, depth), jnp.bfloat16)],
        ),
        out_shape=[shape, shape],
        compiler_params=pltpu.CompilerParams(vmem_limit_bytes=24 << 20),
        cost_estimate=pl.CostEstimate(
            flops=2 * rows * depth * cols * 4, bytes_accessed=2 * depth * cols * 4, transcendentals=0
        ),
        name="project",
    )(me, conv, gate, weight)


def swap(data, axis, flip):
    return lax.ppermute(data, axis, [(i, i ^ flip) for i in range(lax.axis_size(axis))])


def add(first, second):
    return (first.astype(jnp.float32) + second.astype(jnp.float32)).astype(jnp.bfloat16)


def by_channels(values, gate_in, gate_out, spectrum, out_weight):
    seq_count = lax.axis_size("seq")
    me = lax.axis_index("chan").astype(jnp.int32).reshape(1)
    parts = 2
    data = pack(values, gate_in, spectrum, seq_count)
    data = lax.all_to_all(data, "seq", split_axis=0, concat_axis=0, tiled=True)
    convs = convolve(data, parts)
    outs = []
    for part, conv in enumerate(convs):
        conv = lax.all_to_all(conv, "seq", split_axis=0, concat_axis=0, tiled=True)
        send_a, send_b = project(me, conv, gate_out, out_weight, part, ((1, 0), (3, 0), (2, 1), (3, 1)))
        keep_a, keep_b = project(me, conv, gate_out, out_weight, part, ((0, 0), (2, 0), (0, 1), (1, 1)))
        sum_a = add(keep_a, swap(send_a, "chan", 1))
        sum_b = add(keep_b, swap(send_b, "chan", 2))
        out_a = add(sum_a[0], swap(sum_a[1], "chan", 2))
        out_b = add(sum_b[0], swap(sum_b[1], "chan", 1))
        outs.append(jnp.concatenate([out_a, out_b], axis=1))
    return jnp.concatenate(outs, axis=0)


def to_columns(data):
    return lax.all_to_all(data, "seq", split_axis=2, concat_axis=1, tiled=True)


def to_rows(data):
    return lax.all_to_all(data, "seq", split_axis=1, concat_axis=2, tiled=True)


def by_frequencies(values, gate_in, gate_out, spectrum, out_weight):
    seq_count = lax.axis_size("seq")
    seq_index = lax.axis_index("seq")
    tok_rows, chan_width = values.shape
    block_rows = BLOCK // seq_count
    span = tok_rows // block_rows
    tokens_all = BLOCK * span
    col_share = span * chan_width // seq_count
    block_cos = rounded(np.cos(angles(BLOCK, BLOCK, BLOCK)))
    block_sin = rounded(np.sin(angles(BLOCK, BLOCK, BLOCK)))
    span_cos = rounded(np.cos(angles(span, span, span)))
    span_sin = rounded(np.sin(angles(span, span, span)))
    turn_all = angles(BLOCK, span, tokens_all)
    turn_cos_all = jnp.asarray(np.cos(turn_all).astype(np.float32))
    turn_sin_all = jnp.asarray(np.sin(turn_all).astype(np.float32))
    source = (values.astype(jnp.float32) * gate_in.astype(jnp.float32)).astype(jnp.bfloat16)
    spread = to_columns(source.reshape(1, block_rows, seq_count, col_share))
    columns = spread.reshape(BLOCK, col_share)
    cos_part = jnp.dot(jnp.transpose(block_cos), columns, preferred_element_type=jnp.float32)
    sin_part = jnp.dot(jnp.transpose(block_sin), columns, preferred_element_type=jnp.float32)
    col_pos = (seq_index * col_share + jnp.arange(col_share, dtype=jnp.int32)) // chan_width
    turn_cos = jnp.take(turn_cos_all, col_pos, axis=1)
    turn_sin = jnp.take(turn_sin_all, col_pos, axis=1)
    twist_re = cos_part * turn_cos - sin_part * turn_sin
    twist_im = -sin_part * turn_cos - cos_part * turn_sin
    twisted = jnp.stack([twist_re, twist_im]).astype(jnp.bfloat16)
    arranged = to_rows(twisted).reshape(2, block_rows, span, chan_width)
    with_cos = jnp.einsum("bd,kcbh->kdch", span_cos, arranged, preferred_element_type=jnp.float32)
    with_sin = jnp.einsum("bd,kcbh->kdch", span_sin, arranged, preferred_element_type=jnp.float32)
    freq_re = with_cos[0] + with_sin[1]
    freq_im = with_cos[1] - with_sin[0]
    prod_re = freq_re * spectrum[0] - freq_im * spectrum[1]
    prod_im = freq_re * spectrum[1] + freq_im * spectrum[0]
    product = jnp.stack([prod_re, prod_im]).astype(jnp.bfloat16)
    back_cos = jnp.einsum("db,kdch->kcbh", span_cos, product, preferred_element_type=jnp.float32)
    back_sin = jnp.einsum("db,kdch->kcbh", span_sin, product, preferred_element_type=jnp.float32)
    back_re = (back_cos[0] - back_sin[1]) / span
    back_im = (back_cos[1] + back_sin[0]) / span
    back_tc = lax.dynamic_slice_in_dim(turn_cos_all, seq_index * block_rows, block_rows)[:, :, None]
    back_ts = lax.dynamic_slice_in_dim(turn_sin_all, seq_index * block_rows, block_rows)[:, :, None]
    rotated = jnp.stack(
        [back_re * back_tc - back_im * back_ts, back_im * back_tc + back_re * back_ts]
    ).astype(jnp.bfloat16)
    gathered = to_columns(rotated.reshape(2, block_rows, seq_count, col_share)).reshape(2, BLOCK, col_share)
    summed = jnp.dot(block_cos, gathered[0], preferred_element_type=jnp.float32)
    summed = summed - jnp.dot(block_sin, gathered[1], preferred_element_type=jnp.float32)
    ordered = (summed / BLOCK).astype(jnp.bfloat16).reshape(1, BLOCK, col_share)
    conv = to_rows(ordered).reshape(tok_rows, chan_width)
    gated = (conv.astype(jnp.float32) * gate_out.astype(jnp.float32)).astype(jnp.bfloat16)
    partial_sum = jnp.dot(gated, out_weight, preferred_element_type=jnp.float32)
    return lax.psum_scatter(partial_sum.astype(jnp.bfloat16), "chan", scatter_dimension=1, tiled=True)


def shards(values, gate_in, gate_out, spectrum, out_weight):
    seq_count, chan_count = lax.axis_size("seq"), lax.axis_size("chan")
    _, span, block_rows, width = spectrum.shape
    one_lane_block = width == seq_count * LANES and seq_count % 2 == 0 and block_rows % 32 == 0
    if span == 2 and chan_count == 4 and one_lane_block:
        return by_channels(values, gate_in, gate_out, spectrum, out_weight)
    return by_frequencies(values, gate_in, gate_out, spectrum, out_weight)


def solution(mesh):
    placed = (
        P("seq", "chan"),
        P("seq", "chan"),
        P("seq", "chan"),
        P(None, None, "seq", "chan"),
        P("chan", None),
    )
    return jax.shard_map(
        shards, mesh=mesh, in_specs=placed, out_specs=P("seq", "chan"), check_vma=False
    )
```

```python
import functools
import math

import jax
import jax.numpy as jnp
import ml_dtypes
import numpy as np
from jax import lax
from jax.experimental import pallas as pl
from jax.experimental.pallas import tpu as pltpu
from jax.sharding import PartitionSpec as P

BLOCK = 1024
LANES = 128


def angles(first, second, period):
    return (np.arange(first)[:, None] * np.arange(second)[None, :] % period) * (2.0 * math.pi / period)


def rounded(table):
    return jnp.asarray(table.astype(np.float32).astype(ml_dtypes.bfloat16))


def split_rows(rows, span):
    out = lax.broadcasted_iota(jnp.int32, (rows, rows), 0)
    token = lax.broadcasted_iota(jnp.int32, (rows, rows), 1)
    block_rows = rows // span
    return jnp.where(token == (out % block_rows) * span + out // block_rows, 1.0, 0.0).astype(jnp.bfloat16)


def join_rows(rows, span):
    token = lax.broadcasted_iota(jnp.int32, (rows, rows), 0)
    held = lax.broadcasted_iota(jnp.int32, (rows, rows), 1)
    block_rows = rows // span
    return jnp.where(token == (held % block_rows) * span + held // block_rows, 1.0, 0.0).astype(jnp.bfloat16)


def pack_kernel(span, order, me_ref, values_ref, gate_ref, spectrum_ref, *outs):
    step = pl.program_id(0)
    rows = values_ref.shape[0]
    block_rows = rows // span
    source = (values_ref[...].astype(jnp.float32) * gate_ref[...].astype(jnp.float32)).astype(jnp.bfloat16)
    source = jnp.dot(split_rows(rows, span), source, preferred_element_type=jnp.float32).astype(jnp.bfloat16)
    odd = me_ref[0] % 2 == 1

    def fill(out_ref, lanes):
        for part in range(2):
            for d in range(span):
                out_ref[part * span + d] = spectrum_ref[part, d, :, lanes].astype(jnp.bfloat16)
        for b in range(span):
            out_ref[2 * span + b] = source[b * block_rows:(b + 1) * block_rows, lanes]

    for place in range(len(order)):

        @pl.when(step == place)
        def _():
            for core in range(2):
                lanes = slice(core * LANES, (core + 1) * LANES)

                @pl.when(odd)
                def _():
                    fill(outs[2 * place + 1 - core], lanes)

                @pl.when(jnp.logical_not(odd))
                def _():
                    fill(outs[2 * place + core], lanes)


def pack(me, values, gate_in, spectrum, order):
    rows, _ = values.shape
    _, span, block_rows, _ = spectrum.shape
    cols = 2 * LANES

    def column(i, me_ref):
        flip = sum((jnp.where(i == place, chip, 0) for place, chip in enumerate(order)), 0)
        return (me_ref[0] // 2) ^ flip

    shape = (3 * span, block_rows, LANES)
    return pl.pallas_call(
        functools.partial(pack_kernel, span, order),
        grid_spec=pltpu.PrefetchScalarGridSpec(
            num_scalar_prefetch=1,
            grid=(len(order),),
            in_specs=[
                pl.BlockSpec((rows, cols), lambda i, m: (0, column(i, m))),
                pl.BlockSpec((rows, cols), lambda i, m: (0, column(i, m))),
                pl.BlockSpec((2, span, block_rows, cols), lambda i, m: (0, 0, 0, column(i, m))),
            ],
            out_specs=[pl.BlockSpec(shape, lambda i, m: (0, 0, 0))] * (2 * len(order)),
        ),
        out_shape=[jax.ShapeDtypeStruct(shape, jnp.bfloat16)] * (2 * len(order)),
        compiler_params=pltpu.CompilerParams(vmem_limit_bytes=48 << 20),
        name="pack",
    )(me, values, gate_in, spectrum)


def conv_kernel(parts, shares, me_ref, *refs):
    data, (cos_ref, sin_ref, turn_cos_ref, turn_sin_ref) = refs[:shares], refs[shares:shares + 4]
    outs, (cols_ref, fre_ref, fim_ref, re_ref, im_ref) = refs[shares + 4:shares + 4 + parts], refs[shares + 4 + parts:]
    me = me_ref[0]
    rows = data[0].shape[1]
    for m in range(shares):
        at = pl.ds(pl.multiple_of((me ^ m) * rows, rows), rows)
        for b in range(2):
            cols_ref[at, b * LANES:(b + 1) * LANES] = data[m][4 + b]
    step = 2 * rows
    for i in range(shares * rows // step):
        at = slice(i * step, (i + 1) * step)
        fre_ref[at, :] = jnp.dot(cos_ref[at, :], cols_ref[...], preferred_element_type=jnp.float32)
        fim_ref[at, :] = jnp.dot(sin_ref[at, :], cols_ref[...], preferred_element_type=jnp.float32)
    for m in range(shares):
        at = pl.ds(pl.multiple_of((me ^ m) * rows, rows), rows)
        tc, ts = turn_cos_ref[at, :], turn_sin_ref[at, :]
        re0, im0 = fre_ref[at, :LANES], -fim_ref[at, :LANES]
        re1, im1 = fre_ref[at, LANES:], -fim_ref[at, LANES:]
        re1, im1 = re1 * tc + im1 * ts, im1 * tc - re1 * ts
        f0r, f0i, f1r, f1i = re0 + re1, im0 + im1, re0 - re1, im0 - im1
        s0r, s1r, s0i, s1i = (data[m][part].astype(jnp.float32) for part in range(4))
        p0r, p0i = f0r * s0r - f0i * s0i, f0r * s0i + f0i * s0r
        p1r, p1i = f1r * s1r - f1i * s1i, f1r * s1i + f1i * s1r
        b0r, b0i = 0.5 * (p0r + p1r), 0.5 * (p0i + p1i)
        b1r, b1i = 0.5 * (p0r - p1r), 0.5 * (p0i - p1i)
        b1r, b1i = b1r * tc - b1i * ts, b1i * tc + b1r * ts
        re_ref[at, :] = jnp.concatenate([b0r, b1r], axis=1).astype(jnp.bfloat16)
        im_ref[at, :] = jnp.concatenate([b0i, b1i], axis=1).astype(jnp.bfloat16)
    scale = 1.0 / (shares * rows)
    part_rows = rows // parts
    for i in range(shares * rows // step):
        at = slice(i * step, (i + 1) * step)
        conv = jnp.dot(cos_ref[at, :], re_ref[...], preferred_element_type=jnp.float32)
        conv = conv - jnp.dot(sin_ref[at, :], im_ref[...], preferred_element_type=jnp.float32)
        conv = (conv * scale).astype(jnp.bfloat16)
        for s in range(2):
            for p in range(parts):
                begin = s * rows + p * part_rows
                for b in range(2):
                    outs[p][2 * i + s, b] = conv[begin:begin + part_rows, b * LANES:(b + 1) * LANES]


def convolve(me, data, parts):
    shares = len(data)
    rows = data[0].shape[1]
    block = shares * rows
    angle = angles(block, block, block)
    turn = np.broadcast_to(angles(block, 2, 2 * block)[:, 1:], (block, LANES))
    vmem = pl.BlockSpec(memory_space=pltpu.VMEM)
    return pl.pallas_call(
        functools.partial(conv_kernel, parts, shares),
        in_specs=[pl.BlockSpec(memory_space=pltpu.SMEM)] + [vmem] * (shares + 4),
        out_specs=[vmem] * parts,
        out_shape=[jax.ShapeDtypeStruct((shares, 2, rows // parts, LANES), jnp.bfloat16)] * parts,
        scratch_shapes=[pltpu.VMEM((block, 2 * LANES), dtype) for dtype in
                        (jnp.bfloat16, jnp.float32, jnp.float32, jnp.bfloat16, jnp.bfloat16)],
        compiler_params=pltpu.CompilerParams(vmem_limit_bytes=32 << 20),
        name="convolve",
    )(
        me, *data, rounded(np.cos(angle)), rounded(np.sin(angle)),
        jnp.asarray(np.cos(turn).astype(np.float32)), jnp.asarray(np.sin(turn).astype(np.float32)),
    )


def project_kernel(me_ref, conv_ref, gate_ref, weight_ref, first_ref, second_ref, gated_ref):
    step = pl.program_id(0)

    @pl.when(step == 0)
    def _():
        shares, span, part_rows, _ = conv_ref.shape
        join = join_rows(span * part_rows, span)
        for s in range(shares):
            lanes = slice(s * LANES, (s + 1) * LANES)
            held = conv_ref[s].reshape(span * part_rows, LANES)
            conv = jnp.dot(join, held, preferred_element_type=jnp.float32)
            gated_ref[:, lanes] = (conv * gate_ref[:, lanes].astype(jnp.float32)).astype(jnp.bfloat16)

    partial_sum = jnp.dot(gated_ref[...], weight_ref[...], preferred_element_type=jnp.float32).astype(jnp.bfloat16)

    @pl.when(step < 2)
    def _():
        first_ref[0] = partial_sum

    @pl.when(step >= 2)
    def _():
        second_ref[0] = partial_sum


def project(me, conv, gate, weight, part, blocks):
    shares, span, part_rows, _ = conv.shape
    depth, width = weight.shape
    rows = span * part_rows
    cols = width // 8
    (f0, h0), (f1, h1), (f2, h2), (f3, h3) = blocks

    def column(i, me_ref):
        flip = jnp.where(i == 0, f0, jnp.where(i == 1, f1, jnp.where(i == 2, f2, f3)))
        half = jnp.where(i == 0, h0, jnp.where(i == 1, h1, jnp.where(i == 2, h2, h3)))
        return 0, (me_ref[0] ^ flip) * 2 + half

    shape = jax.ShapeDtypeStruct((2, rows, cols), jnp.bfloat16)
    return pl.pallas_call(
        project_kernel,
        grid_spec=pltpu.PrefetchScalarGridSpec(
            num_scalar_prefetch=1,
            grid=(4,),
            in_specs=[
                pl.BlockSpec((shares, span, part_rows, LANES), lambda i, m: (0, 0, 0, 0)),
                pl.BlockSpec((rows, depth), lambda i, m: (part, 0)),
                pl.BlockSpec((depth, cols), column),
            ],
            out_specs=[
                pl.BlockSpec((1, rows, cols), lambda i, m: (jnp.minimum(i, 1), 0, 0)),
                pl.BlockSpec((1, rows, cols), lambda i, m: (jnp.maximum(i - 2, 0), 0, 0)),
            ],
            scratch_shapes=[pltpu.VMEM((rows, depth), jnp.bfloat16)],
        ),
        out_shape=[shape, shape],
        compiler_params=pltpu.CompilerParams(vmem_limit_bytes=52 << 20),
        cost_estimate=pl.CostEstimate(
            flops=2 * rows * depth * cols * 4, bytes_accessed=2 * depth * cols * 4, transcendentals=0
        ),
        name="project",
    )(me, conv, gate, weight)


def swap(data, axis, flip):
    return lax.ppermute(data, axis, [(i, i ^ flip) for i in range(lax.axis_size(axis))])


def add(first, second):
    return (first.astype(jnp.float32) + second.astype(jnp.float32)).astype(jnp.bfloat16)


def by_channels(values, gate_in, gate_out, spectrum, out_weight):
    seq_count = lax.axis_size("seq")
    here = lax.axis_index("seq").astype(jnp.int32).reshape(1)
    me = lax.axis_index("chan").astype(jnp.int32).reshape(1)
    parts = 2
    order = tuple(reversed(range(seq_count // 2)))
    packed = pack(here, values, gate_in, spectrum, order)
    data = [None] * seq_count
    for place, flip in enumerate(order):
        for core in range(2):
            mine = packed[2 * place + core]
            data[2 * flip + core] = swap(mine, "seq", 2 * flip + core) if flip or core else mine
    convs = convolve(here, data, parts)
    outs = []
    for part, conv in enumerate(convs):
        conv = lax.all_to_all(conv, "seq", split_axis=0, concat_axis=0, tiled=True)
        send_a, send_b = project(me, conv, gate_out, out_weight, part, ((1, 0), (3, 0), (2, 1), (3, 1)))
        keep_a, keep_b = project(me, conv, gate_out, out_weight, part, ((0, 0), (2, 0), (0, 1), (1, 1)))
        sum_a = add(keep_a, swap(send_a, "chan", 1))
        sum_b = add(keep_b, swap(send_b, "chan", 2))
        out_a = add(sum_a[0], swap(sum_a[1], "chan", 2))
        out_b = add(sum_b[0], swap(sum_b[1], "chan", 1))
        outs.append(jnp.concatenate([out_a, out_b], axis=1))
    return jnp.concatenate(outs, axis=0)


def to_columns(data):
    return lax.all_to_all(data, "seq", split_axis=2, concat_axis=1, tiled=True)


def to_rows(data):
    return lax.all_to_all(data, "seq", split_axis=1, concat_axis=2, tiled=True)


def by_frequencies(values, gate_in, gate_out, spectrum, out_weight):
    seq_count = lax.axis_size("seq")
    seq_index = lax.axis_index("seq")
    tok_rows, chan_width = values.shape
    block_rows = BLOCK // seq_count
    span = tok_rows // block_rows
    tokens_all = BLOCK * span
    col_share = span * chan_width // seq_count
    block_cos = rounded(np.cos(angles(BLOCK, BLOCK, BLOCK)))
    block_sin = rounded(np.sin(angles(BLOCK, BLOCK, BLOCK)))
    span_cos = rounded(np.cos(angles(span, span, span)))
    span_sin = rounded(np.sin(angles(span, span, span)))
    turn_all = angles(BLOCK, span, tokens_all)
    turn_cos_all = jnp.asarray(np.cos(turn_all).astype(np.float32))
    turn_sin_all = jnp.asarray(np.sin(turn_all).astype(np.float32))
    source = (values.astype(jnp.float32) * gate_in.astype(jnp.float32)).astype(jnp.bfloat16)
    spread = to_columns(source.reshape(1, block_rows, seq_count, col_share))
    columns = spread.reshape(BLOCK, col_share)
    cos_part = jnp.dot(jnp.transpose(block_cos), columns, preferred_element_type=jnp.float32)
    sin_part = jnp.dot(jnp.transpose(block_sin), columns, preferred_element_type=jnp.float32)
    col_pos = (seq_index * col_share + jnp.arange(col_share, dtype=jnp.int32)) // chan_width
    turn_cos = jnp.take(turn_cos_all, col_pos, axis=1)
    turn_sin = jnp.take(turn_sin_all, col_pos, axis=1)
    twist_re = cos_part * turn_cos - sin_part * turn_sin
    twist_im = -sin_part * turn_cos - cos_part * turn_sin
    twisted = jnp.stack([twist_re, twist_im]).astype(jnp.bfloat16)
    arranged = to_rows(twisted).reshape(2, block_rows, span, chan_width)
    with_cos = jnp.einsum("bd,kcbh->kdch", span_cos, arranged, preferred_element_type=jnp.float32)
    with_sin = jnp.einsum("bd,kcbh->kdch", span_sin, arranged, preferred_element_type=jnp.float32)
    freq_re = with_cos[0] + with_sin[1]
    freq_im = with_cos[1] - with_sin[0]
    prod_re = freq_re * spectrum[0] - freq_im * spectrum[1]
    prod_im = freq_re * spectrum[1] + freq_im * spectrum[0]
    product = jnp.stack([prod_re, prod_im]).astype(jnp.bfloat16)
    back_cos = jnp.einsum("db,kdch->kcbh", span_cos, product, preferred_element_type=jnp.float32)
    back_sin = jnp.einsum("db,kdch->kcbh", span_sin, product, preferred_element_type=jnp.float32)
    back_re = (back_cos[0] - back_sin[1]) / span
    back_im = (back_cos[1] + back_sin[0]) / span
    back_tc = lax.dynamic_slice_in_dim(turn_cos_all, seq_index * block_rows, block_rows)[:, :, None]
    back_ts = lax.dynamic_slice_in_dim(turn_sin_all, seq_index * block_rows, block_rows)[:, :, None]
    rotated = jnp.stack(
        [back_re * back_tc - back_im * back_ts, back_im * back_tc + back_re * back_ts]
    ).astype(jnp.bfloat16)
    gathered = to_columns(rotated.reshape(2, block_rows, seq_count, col_share)).reshape(2, BLOCK, col_share)
    summed = jnp.dot(block_cos, gathered[0], preferred_element_type=jnp.float32)
    summed = summed - jnp.dot(block_sin, gathered[1], preferred_element_type=jnp.float32)
    ordered = (summed / BLOCK).astype(jnp.bfloat16).reshape(1, BLOCK, col_share)
    conv = to_rows(ordered).reshape(tok_rows, chan_width)
    gated = (conv.astype(jnp.float32) * gate_out.astype(jnp.float32)).astype(jnp.bfloat16)
    partial_sum = jnp.dot(gated, out_weight, preferred_element_type=jnp.float32)
    return lax.psum_scatter(partial_sum.astype(jnp.bfloat16), "chan", scatter_dimension=1, tiled=True)


def shards(values, gate_in, gate_out, spectrum, out_weight):
    seq_count, chan_count = lax.axis_size("seq"), lax.axis_size("chan")
    _, span, block_rows, width = spectrum.shape
    one_lane_block = width == seq_count * LANES and block_rows % 32 == 0
    if span == 2 and chan_count == 4 and seq_count & (seq_count - 1) == 0 and one_lane_block:
        return by_channels(values, gate_in, gate_out, spectrum, out_weight)
    return by_frequencies(values, gate_in, gate_out, spectrum, out_weight)


def solution(mesh):
    placed = (
        P("seq", "chan"),
        P("seq", "chan"),
        P("seq", "chan"),
        P(None, None, "seq", "chan"),
        P("chan", None),
    )
    return jax.shard_map(
        shards, mesh=mesh, in_specs=placed, out_specs=P("seq", "chan"), check_vma=False
    )
```

```python
import functools
import math

import jax
import jax.numpy as jnp
import ml_dtypes
import numpy as np
from jax import lax
from jax.experimental import pallas as pl
from jax.experimental.pallas import tpu as pltpu
from jax.sharding import PartitionSpec as P

BLOCK = 1024
LANES = 128


def angles(first, second, period):
    return (np.arange(first)[:, None] * np.arange(second)[None, :] % period) * (2.0 * math.pi / period)


def rounded(table):
    return jnp.asarray(table.astype(np.float32).astype(ml_dtypes.bfloat16))


def split_rows(rows, span):
    out = lax.broadcasted_iota(jnp.int32, (rows, rows), 0)
    token = lax.broadcasted_iota(jnp.int32, (rows, rows), 1)
    block_rows = rows // span
    return jnp.where(token == (out % block_rows) * span + out // block_rows, 1.0, 0.0).astype(jnp.bfloat16)


def join_rows(rows, span):
    token = lax.broadcasted_iota(jnp.int32, (rows, rows), 0)
    held = lax.broadcasted_iota(jnp.int32, (rows, rows), 1)
    block_rows = rows // span
    return jnp.where(token == (held % block_rows) * span + held // block_rows, 1.0, 0.0).astype(jnp.bfloat16)


def pack_kernel(span, me_ref, values_hbm, gate_hbm, spectrum_hbm, *refs):
    outs, (values_ref, gate_ref, spectrum_ref, sems) = refs[:-4], refs[-4:]
    copies = [
        pltpu.make_async_copy(values_hbm, values_ref, sems.at[0]),
        pltpu.make_async_copy(gate_hbm, gate_ref, sems.at[1]),
    ]
    for part in range(2):
        for d in range(span):
            copies.append(pltpu.make_async_copy(
                spectrum_hbm.at[part, d], spectrum_ref.at[part * span + d], sems.at[2 + part * span + d]
            ))
    for copy in copies:
        copy.start()
    me = me_ref[0]
    rows = values_ref.shape[0]
    block_rows = rows // span
    copies[0].wait()
    copies[1].wait()
    source = (values_ref[...].astype(jnp.float32) * gate_ref[...].astype(jnp.float32)).astype(jnp.bfloat16)
    values_ref[...] = jnp.dot(
        split_rows(rows, span), source, preferred_element_type=jnp.float32
    ).astype(jnp.bfloat16)

    def lanes_of(m):
        return pl.ds(pl.multiple_of((me ^ m) * LANES, LANES), LANES)

    for m, out_ref in enumerate(outs):
        for b in range(span):
            out_ref[2 * span + b] = values_ref[b * block_rows:(b + 1) * block_rows, lanes_of(m)]
    for part in range(2 * span):
        copies[2 + part].wait()
        for m, out_ref in enumerate(outs):
            out_ref[part] = spectrum_ref[part, :, lanes_of(m)].astype(jnp.bfloat16)


def pack(me, values, gate_in, spectrum, shares):
    rows, width = values.shape
    _, span, block_rows, _ = spectrum.shape
    shape = (3 * span, block_rows, LANES)
    vmem, hbm = pl.BlockSpec(memory_space=pltpu.VMEM), pl.BlockSpec(memory_space=pltpu.HBM)
    return pl.pallas_call(
        functools.partial(pack_kernel, span),
        in_specs=[pl.BlockSpec(memory_space=pltpu.SMEM), hbm, hbm, hbm],
        out_specs=[vmem] * shares,
        out_shape=[jax.ShapeDtypeStruct(shape, jnp.bfloat16)] * shares,
        scratch_shapes=[
            pltpu.VMEM((rows, width), jnp.bfloat16),
            pltpu.VMEM((rows, width), jnp.bfloat16),
            pltpu.VMEM((2 * span, block_rows, width), jnp.float32),
            pltpu.SemaphoreType.DMA((2 + 2 * span,)),
        ],
        compiler_params=pltpu.CompilerParams(vmem_limit_bytes=60 << 20),
        name="pack",
    )(me, values, gate_in, spectrum)


def take_kernel(places_ref, weight_hbm, *refs):
    outs, sems = refs[:-1], refs[-1]
    slabs = sems.shape[1]
    depth, cols = outs[0].shape[0] // slabs, outs[0].shape[1]
    copies = [
        pltpu.make_async_copy(
            weight_hbm.at[i * depth:(i + 1) * depth, pl.ds(pl.multiple_of(places_ref[k] * cols, cols), cols)],
            out_ref.at[i * depth:(i + 1) * depth],
            sems.at[k, i],
        )
        for k, out_ref in enumerate(outs)
        for i in range(slabs)
    ]
    for copy in copies:
        copy.start()
    for copy in copies:
        copy.wait()


def take_blocks(places, weight):
    depth, cols = weight.shape[0], weight.shape[1] // 8
    count, slabs = places.shape[0], 4
    return pl.pallas_call(
        take_kernel,
        in_specs=[pl.BlockSpec(memory_space=pltpu.SMEM), pl.BlockSpec(memory_space=pltpu.HBM)],
        out_specs=[pl.BlockSpec(memory_space=pltpu.VMEM)] * count,
        out_shape=[jax.ShapeDtypeStruct((depth, cols), weight.dtype)] * count,
        scratch_shapes=[pltpu.SemaphoreType.DMA((count, slabs))],
        compiler_params=pltpu.CompilerParams(vmem_limit_bytes=48 << 20),
        cost_estimate=pl.CostEstimate(flops=0, bytes_accessed=128 * depth * cols, transcendentals=0),
        name="take_blocks",
    )(places, weight)


def conv_kernel(parts, order, me_ref, *refs):
    shares = len(order)
    data, (cos_ref, sin_ref, turn_cos_ref, turn_sin_ref) = refs[:shares], refs[shares:shares + 4]
    outs, (cols_ref, filt_ref, re_ref, im_ref) = refs[shares + 4:shares + 4 + parts], refs[shares + 4 + parts:]
    me = me_ref[0]
    rows = data[0].shape[1]
    for m, ref in zip(order, data):
        at = pl.ds(pl.multiple_of((me ^ m) * rows, rows), rows)
        for b in range(2):
            cols_ref[at, b * LANES:(b + 1) * LANES] = ref[4 + b]
        for part in range(4):
            filt_ref[part, at, :] = ref[part]
    step = 2 * rows
    for i in range(shares * rows // step):
        at = slice(i * step, (i + 1) * step)
        first_re = jnp.dot(cos_ref[at, :], cols_ref[...], preferred_element_type=jnp.float32)
        first_sin = jnp.dot(sin_ref[at, :], cols_ref[...], preferred_element_type=jnp.float32)
        tc, ts = turn_cos_ref[at, :], turn_sin_ref[at, :]
        re0, im0 = first_re[:, :LANES], -first_sin[:, :LANES]
        re1, im1 = first_re[:, LANES:], -first_sin[:, LANES:]
        re1, im1 = re1 * tc + im1 * ts, im1 * tc - re1 * ts
        f0r, f0i, f1r, f1i = re0 + re1, im0 + im1, re0 - re1, im0 - im1
        s0r, s1r, s0i, s1i = (filt_ref[part, at, :].astype(jnp.float32) for part in range(4))
        p0r, p0i = f0r * s0r - f0i * s0i, f0r * s0i + f0i * s0r
        p1r, p1i = f1r * s1r - f1i * s1i, f1r * s1i + f1i * s1r
        b0r, b0i = 0.5 * (p0r + p1r), 0.5 * (p0i + p1i)
        b1r, b1i = 0.5 * (p0r - p1r), 0.5 * (p0i - p1i)
        b1r, b1i = b1r * tc - b1i * ts, b1i * tc + b1r * ts
        re_ref[at, :] = jnp.concatenate([b0r, b1r], axis=1).astype(jnp.bfloat16)
        im_ref[at, :] = jnp.concatenate([b0i, b1i], axis=1).astype(jnp.bfloat16)
    scale = 1.0 / (shares * rows)
    part_rows = rows // parts
    for i in range(shares * rows // step):
        at = slice(i * step, (i + 1) * step)
        conv = jnp.dot(cos_ref[at, :], re_ref[...], preferred_element_type=jnp.float32)
        conv = conv - jnp.dot(sin_ref[at, :], im_ref[...], preferred_element_type=jnp.float32)
        conv = (conv * scale).astype(jnp.bfloat16)
        for s in range(2):
            for p in range(parts):
                begin = s * rows + p * part_rows
                for b in range(2):
                    outs[p][2 * i + s, b] = conv[begin:begin + part_rows, b * LANES:(b + 1) * LANES]


def convolve(me, data, order, parts):
    shares = len(data)
    rows = data[0].shape[1]
    block = shares * rows
    angle = angles(block, block, block)
    turn = np.broadcast_to(angles(block, 2, 2 * block)[:, 1:], (block, LANES))
    vmem = pl.BlockSpec(memory_space=pltpu.VMEM)
    columns = pltpu.VMEM((block, 2 * LANES), jnp.bfloat16)
    return pl.pallas_call(
        functools.partial(conv_kernel, parts, order),
        in_specs=[pl.BlockSpec(memory_space=pltpu.SMEM)] + [vmem] * (shares + 4),
        out_specs=[vmem] * parts,
        out_shape=[jax.ShapeDtypeStruct((shares, 2, rows // parts, LANES), jnp.bfloat16)] * parts,
        scratch_shapes=[columns, pltpu.VMEM((4, block, LANES), jnp.bfloat16), columns, columns],
        compiler_params=pltpu.CompilerParams(vmem_limit_bytes=24 << 20),
        cost_estimate=pl.CostEstimate(flops=64 * block * block * LANES, bytes_accessed=8 * block * block, transcendentals=0),
        name="convolve",
    )(
        me, *data, rounded(np.cos(angle)), rounded(np.sin(angle)),
        jnp.asarray(np.cos(turn).astype(np.float32)), jnp.asarray(np.sin(turn).astype(np.float32)),
    )


def gate_kernel(conv_ref, gate_ref, *refs):
    outs, held_ref = refs[:-1], refs[-1]
    shares, span, block_rows, _ = conv_ref.shape
    rows = span * block_rows
    for s in range(shares):
        held_ref[:, s * LANES:(s + 1) * LANES] = conv_ref[s].reshape(rows, LANES)
    conv = jnp.dot(join_rows(rows, span), held_ref[...], preferred_element_type=jnp.float32)
    gated = (conv * gate_ref[...].astype(jnp.float32)).astype(jnp.bfloat16)
    part = rows // len(outs)
    for p, out_ref in enumerate(outs):
        out_ref[...] = gated[p * part:(p + 1) * part]


def gate(conv, gate_out, parts):
    rows, width = gate_out.shape
    vmem = pl.BlockSpec(memory_space=pltpu.VMEM)
    return pl.pallas_call(
        gate_kernel,
        in_specs=[vmem, vmem],
        out_specs=[vmem] * parts,
        out_shape=[jax.ShapeDtypeStruct((rows // parts, width), jnp.bfloat16)] * parts,
        scratch_shapes=[pltpu.VMEM((rows, width), jnp.bfloat16)],
        compiler_params=pltpu.CompilerParams(vmem_limit_bytes=16 << 20),
        name="gate",
    )(conv, gate_out)


def own_kernel(me_ref, *refs):
    parts = (len(refs) - 1) // 2
    gated, slabs, out_ref = refs[:parts], refs[parts:-1], refs[-1]
    rows, depth = gated[0].shape[0], slabs[0].shape[0]
    for p, gated_ref in enumerate(gated):
        out_ref[0, p * rows:(p + 1) * rows] = sum(
            jnp.dot(gated_ref[:, i * depth:(i + 1) * depth], slab[...], preferred_element_type=jnp.float32)
            for i, slab in enumerate(slabs)
        )


def own_part(me, gated, weight, blocks):
    parts = len(gated)
    part_rows, depth = gated[0].shape
    cols = weight.shape[1] // 8

    def column(slab, i, me_ref):
        flip = sum((jnp.where(i == place, f, 0) for place, (f, _) in enumerate(blocks)), 0)
        half = sum((jnp.where(i == place, h, 0) for place, (_, h) in enumerate(blocks)), 0)
        return slab, (me_ref[0] ^ flip) * 2 + half

    return pl.pallas_call(
        own_kernel,
        grid_spec=pltpu.PrefetchScalarGridSpec(
            num_scalar_prefetch=1,
            grid=(len(blocks),),
            in_specs=[pl.BlockSpec((part_rows, depth), lambda i, m: (0, 0))] * parts
            + [pl.BlockSpec((depth // parts, cols), functools.partial(column, slab)) for slab in range(parts)],
            out_specs=pl.BlockSpec((1, parts * part_rows, cols), lambda i, m: (i, 0, 0)),
        ),
        out_shape=jax.ShapeDtypeStruct((len(blocks), parts * part_rows, cols), jnp.float32),
        compiler_params=pltpu.CompilerParams(vmem_limit_bytes=40 << 20),
        cost_estimate=pl.CostEstimate(
            flops=2 * parts * part_rows * depth * cols * len(blocks),
            bytes_accessed=2 * depth * cols * len(blocks), transcendentals=0,
        ),
        name="own_part",
    )(me, *gated, *[weight] * parts)


def add_kernel(parts, kept, core_ref, own_ref, *refs):
    moved, refs = refs[:2 * parts], refs[2 * parts:]
    weights, (a_ref, b_ref, held_ref, sems) = refs[:4], refs[4:]
    slabs = sems.shape[1]
    depth = held_ref.shape[1] // slabs

    def copies(side, take_mine):
        source = weights[2 * side] if take_mine else weights[2 * side + 1]
        return [
            pltpu.make_async_copy(
                source.at[i * depth:(i + 1) * depth], held_ref.at[side, i * depth:(i + 1) * depth], sems.at[side, i]
            )
            for i in range(slabs)
        ]

    mine_core = 0 if kept else 1
    for side in range(2):

        @pl.when(core_ref[0] == mine_core)
        def _():
            for copy in copies(side, True):
                copy.start()

        @pl.when(core_ref[0] != mine_core)
        def _():
            for copy in copies(side, False):
                copy.start()

    rows = moved[0].shape[0]
    for side, out_ref in enumerate((a_ref, b_ref)):
        for i, copy in enumerate(copies(side, True)):
            copy.wait()
        for p in range(parts):
            at = slice(p * rows, (p + 1) * rows)
            total = own_ref[side, at] + jnp.dot(
                moved[side * parts + p][...], held_ref[side], preferred_element_type=jnp.float32
            )
            out_ref[at] = total.astype(out_ref.dtype)


def add_moved(core, own, moved_x, moved_y, weights, first, kept, dtype):
    parts = len(moved_x)
    rows, depth = moved_x[0].shape
    cols = own.shape[2]
    whole = pl.BlockSpec((rows, depth), lambda i: (0, 0))
    shape = jax.ShapeDtypeStruct((parts * rows, cols), dtype)
    out = pl.BlockSpec((parts * rows, cols), lambda i: (0, 0))
    return pl.pallas_call(
        functools.partial(add_kernel, parts, kept),
        grid=(1,),
        in_specs=[
            pl.BlockSpec(memory_space=pltpu.SMEM),
            pl.BlockSpec((2, parts * rows, cols), lambda i: (0, first, 0)),
        ]
        + [whole] * (2 * parts)
        + [pl.BlockSpec(memory_space=pl.ANY)] * 4,
        out_specs=[out, out],
        out_shape=[shape, shape],
        scratch_shapes=[pltpu.VMEM((2, depth, cols), jnp.bfloat16), pltpu.SemaphoreType.DMA((2, 4))],
        compiler_params=pltpu.CompilerParams(vmem_limit_bytes=40 << 20),
        cost_estimate=pl.CostEstimate(
            flops=4 * parts * rows * depth * cols, bytes_accessed=4 * depth * cols, transcendentals=0
        ),
        name="add_kept" if kept else "add_sent",
    )(core, own, *moved_x, *moved_y, *weights)


def swap(data, axis, flip):
    return lax.ppermute(data, axis, [(i, i ^ flip) for i in range(lax.axis_size(axis))])


def by_channels(values, gate_in, gate_out, spectrum, out_weight):
    seq_count = lax.axis_size("seq")
    here = lax.axis_index("seq").astype(jnp.int32)
    me = lax.axis_index("chan").astype(jnp.int32)
    core = here % 2
    parts = 2

    order = tuple(sorted(range(seq_count), key=lambda m: (m == 0, m == 1, m % 2, -m)))
    packed = list(pack(here.reshape(1), values, gate_in, spectrum, seq_count))
    places = jnp.stack([(me ^ (1 + 2 * core)) * 2, (me ^ (2 + core)) * 2 + 1])
    _, places = lax.optimization_barrier((packed, places))
    block_x, block_y = take_blocks(places, out_weight)
    weight_x, weight_y = swap(block_x, "chan", 1), swap(block_y, "chan", 2)
    late = [m for m in order if m % 2]
    held, _ = lax.optimization_barrier(([packed[m] for m in late], block_y))
    for m, mine in zip(late, held):
        packed[m] = mine
    data = [swap(packed[m], "seq", m) if m else packed[m] for m in order]
    (conv,) = convolve(here.reshape(1), data, order, 1)
    conv = lax.all_to_all(conv, "seq", split_axis=0, concat_axis=0, tiled=True)
    gated = gate(conv, gate_out, parts)
    weight_x, weight_y, _ = lax.optimization_barrier((weight_x, weight_y, gated))
    weights = [weight_x, swap(weight_x, "seq", 1), weight_y, swap(weight_y, "seq", 1)]
    own = own_part(me.reshape(1), gated, out_weight, ((2, 0), (1, 1)))
    core = core.reshape(1)
    moved_x, moved_y = [], []
    for p in range(parts):
        mine = gated[p]
        if p:
            mine, _ = lax.optimization_barrier((mine, own))
        moved_x.append(swap(mine, "chan", 1))
        moved_y.append(swap(mine, "chan", 2))
    sums_a, sums_b = [], []
    for p in range(parts):
        sent = add_moved(core, own, moved_x[p:p + 1], moved_y[p:p + 1], weights, p, False, jnp.bfloat16)
        sums_a.append(swap(sent[0], "chan", 2))
        sums_b.append(swap(sent[1], "chan", 1))
    gated, _ = lax.optimization_barrier((gated, sent))
    own = own_part(me.reshape(1), gated, out_weight, ((0, 0), (0, 1)))
    kept_a, kept_b = add_moved(core, own, moved_x, moved_y, weights, 0, True, jnp.float32)
    sums = jnp.concatenate([jnp.concatenate(sums_a, axis=0), jnp.concatenate(sums_b, axis=0)], axis=1)
    return (jnp.concatenate([kept_a, kept_b], axis=1) + sums.astype(jnp.float32)).astype(jnp.bfloat16)


def to_columns(data):
    return lax.all_to_all(data, "seq", split_axis=2, concat_axis=1, tiled=True)


def to_rows(data):
    return lax.all_to_all(data, "seq", split_axis=1, concat_axis=2, tiled=True)


def by_frequencies(values, gate_in, gate_out, spectrum, out_weight):
    seq_count = lax.axis_size("seq")
    seq_index = lax.axis_index("seq")
    tok_rows, chan_width = values.shape
    block_rows = BLOCK // seq_count
    span = tok_rows // block_rows
    tokens_all = BLOCK * span
    col_share = span * chan_width // seq_count
    block_cos = rounded(np.cos(angles(BLOCK, BLOCK, BLOCK)))
    block_sin = rounded(np.sin(angles(BLOCK, BLOCK, BLOCK)))
    span_cos = rounded(np.cos(angles(span, span, span)))
    span_sin = rounded(np.sin(angles(span, span, span)))
    turn_all = angles(BLOCK, span, tokens_all)
    turn_cos_all = jnp.asarray(np.cos(turn_all).astype(np.float32))
    turn_sin_all = jnp.asarray(np.sin(turn_all).astype(np.float32))
    source = (values.astype(jnp.float32) * gate_in.astype(jnp.float32)).astype(jnp.bfloat16)
    spread = to_columns(source.reshape(1, block_rows, seq_count, col_share))
    columns = spread.reshape(BLOCK, col_share)
    cos_part = jnp.dot(jnp.transpose(block_cos), columns, preferred_element_type=jnp.float32)
    sin_part = jnp.dot(jnp.transpose(block_sin), columns, preferred_element_type=jnp.float32)
    col_pos = (seq_index * col_share + jnp.arange(col_share, dtype=jnp.int32)) // chan_width
    turn_cos = jnp.take(turn_cos_all, col_pos, axis=1)
    turn_sin = jnp.take(turn_sin_all, col_pos, axis=1)
    twist_re = cos_part * turn_cos - sin_part * turn_sin
    twist_im = -sin_part * turn_cos - cos_part * turn_sin
    twisted = jnp.stack([twist_re, twist_im]).astype(jnp.bfloat16)
    arranged = to_rows(twisted).reshape(2, block_rows, span, chan_width)
    with_cos = jnp.einsum("bd,kcbh->kdch", span_cos, arranged, preferred_element_type=jnp.float32)
    with_sin = jnp.einsum("bd,kcbh->kdch", span_sin, arranged, preferred_element_type=jnp.float32)
    freq_re = with_cos[0] + with_sin[1]
    freq_im = with_cos[1] - with_sin[0]
    prod_re = freq_re * spectrum[0] - freq_im * spectrum[1]
    prod_im = freq_re * spectrum[1] + freq_im * spectrum[0]
    product = jnp.stack([prod_re, prod_im]).astype(jnp.bfloat16)
    back_cos = jnp.einsum("db,kdch->kcbh", span_cos, product, preferred_element_type=jnp.float32)
    back_sin = jnp.einsum("db,kdch->kcbh", span_sin, product, preferred_element_type=jnp.float32)
    back_re = (back_cos[0] - back_sin[1]) / span
    back_im = (back_cos[1] + back_sin[0]) / span
    back_tc = lax.dynamic_slice_in_dim(turn_cos_all, seq_index * block_rows, block_rows)[:, :, None]
    back_ts = lax.dynamic_slice_in_dim(turn_sin_all, seq_index * block_rows, block_rows)[:, :, None]
    rotated = jnp.stack(
        [back_re * back_tc - back_im * back_ts, back_im * back_tc + back_re * back_ts]
    ).astype(jnp.bfloat16)
    gathered = to_columns(rotated.reshape(2, block_rows, seq_count, col_share)).reshape(2, BLOCK, col_share)
    summed = jnp.dot(block_cos, gathered[0], preferred_element_type=jnp.float32)
    summed = summed - jnp.dot(block_sin, gathered[1], preferred_element_type=jnp.float32)
    ordered = (summed / BLOCK).astype(jnp.bfloat16).reshape(1, BLOCK, col_share)
    conv = to_rows(ordered).reshape(tok_rows, chan_width)
    gated = (conv.astype(jnp.float32) * gate_out.astype(jnp.float32)).astype(jnp.bfloat16)
    partial_sum = jnp.dot(gated, out_weight, preferred_element_type=jnp.float32)
    return lax.psum_scatter(partial_sum.astype(jnp.bfloat16), "chan", scatter_dimension=1, tiled=True)


def shards(values, gate_in, gate_out, spectrum, out_weight):
    seq_count, chan_count = lax.axis_size("seq"), lax.axis_size("chan")
    _, span, block_rows, width = spectrum.shape
    one_lane_block = width == seq_count * LANES and block_rows % 32 == 0
    if span == 2 and chan_count == 4 and seq_count & (seq_count - 1) == 0 and one_lane_block:
        return by_channels(values, gate_in, gate_out, spectrum, out_weight)
    return by_frequencies(values, gate_in, gate_out, spectrum, out_weight)


def solution(mesh):
    placed = (
        P("seq", "chan"),
        P("seq", "chan"),
        P("seq", "chan"),
        P(None, None, "seq", "chan"),
        P("chan", None),
    )
    return jax.shard_map(
        shards, mesh=mesh, in_specs=placed, out_specs=P("seq", "chan"), check_vma=False
    )
```

```python
import functools
import math

import jax
import jax.numpy as jnp
import ml_dtypes
import numpy as np
from jax import lax
from jax.experimental import pallas as pl
from jax.experimental.pallas import tpu as pltpu
from jax.sharding import PartitionSpec as P

BLOCK = 1024
LANES = 128


def angles(first, second, period):
    return (np.arange(first)[:, None] * np.arange(second)[None, :] % period) * (2.0 * math.pi / period)


def rounded(table):
    return jnp.asarray(table.astype(np.float32).astype(ml_dtypes.bfloat16))


def split_rows(rows, span):
    out = lax.broadcasted_iota(jnp.int32, (rows, rows), 0)
    token = lax.broadcasted_iota(jnp.int32, (rows, rows), 1)
    block_rows = rows // span
    return jnp.where(token == (out % block_rows) * span + out // block_rows, 1.0, 0.0).astype(jnp.bfloat16)


def join_rows(rows, span):
    token = lax.broadcasted_iota(jnp.int32, (rows, rows), 0)
    held = lax.broadcasted_iota(jnp.int32, (rows, rows), 1)
    block_rows = rows // span
    return jnp.where(token == (held % block_rows) * span + held // block_rows, 1.0, 0.0).astype(jnp.bfloat16)


def pack_kernel(span, me_ref, values_hbm, gate_hbm, spectrum_hbm, *refs):
    outs, (values_ref, gate_ref, spectrum_ref, sems) = refs[:-4], refs[-4:]
    copies = [
        pltpu.make_async_copy(values_hbm, values_ref, sems.at[0]),
        pltpu.make_async_copy(gate_hbm, gate_ref, sems.at[1]),
    ]
    for part in range(2):
        for d in range(span):
            copies.append(pltpu.make_async_copy(
                spectrum_hbm.at[part, d], spectrum_ref.at[part * span + d], sems.at[2 + part * span + d]
            ))
    for copy in copies:
        copy.start()
    me = me_ref[0]
    rows = values_ref.shape[0]
    block_rows = rows // span
    copies[0].wait()
    copies[1].wait()
    source = (values_ref[...].astype(jnp.float32) * gate_ref[...].astype(jnp.float32)).astype(jnp.bfloat16)
    values_ref[...] = jnp.dot(
        split_rows(rows, span), source, preferred_element_type=jnp.float32
    ).astype(jnp.bfloat16)

    def lanes_of(m):
        return pl.ds(pl.multiple_of((me ^ m) * LANES, LANES), LANES)

    for m, out_ref in enumerate(outs):
        for b in range(span):
            out_ref[2 * span + b] = values_ref[b * block_rows:(b + 1) * block_rows, lanes_of(m)]
    for part in range(2 * span):
        copies[2 + part].wait()
        for m, out_ref in enumerate(outs):
            out_ref[part] = spectrum_ref[part, :, lanes_of(m)].astype(jnp.bfloat16)


def pack(me, values, gate_in, spectrum, shares):
    rows, width = values.shape
    _, span, block_rows, _ = spectrum.shape
    shape = (3 * span, block_rows, LANES)
    vmem, hbm = pl.BlockSpec(memory_space=pltpu.VMEM), pl.BlockSpec(memory_space=pltpu.HBM)
    return pl.pallas_call(
        functools.partial(pack_kernel, span),
        in_specs=[pl.BlockSpec(memory_space=pltpu.SMEM), hbm, hbm, hbm],
        out_specs=[vmem] * shares,
        out_shape=[jax.ShapeDtypeStruct(shape, jnp.bfloat16)] * shares,
        scratch_shapes=[
            pltpu.VMEM((rows, width), jnp.bfloat16),
            pltpu.VMEM((rows, width), jnp.bfloat16),
            pltpu.VMEM((2 * span, block_rows, width), jnp.float32),
            pltpu.SemaphoreType.DMA((2 + 2 * span,)),
        ],
        compiler_params=pltpu.CompilerParams(vmem_limit_bytes=60 << 20),
        name="pack",
    )(me, values, gate_in, spectrum)


def take_kernel(places_ref, weight_hbm, *refs):
    outs, sems = refs[:-1], refs[-1]
    slabs = sems.shape[1]
    depth, cols = outs[0].shape[0] // slabs, outs[0].shape[1]
    copies = [
        pltpu.make_async_copy(
            weight_hbm.at[i * depth:(i + 1) * depth, pl.ds(pl.multiple_of(places_ref[k] * cols, cols), cols)],
            out_ref.at[i * depth:(i + 1) * depth],
            sems.at[k, i],
        )
        for k, out_ref in enumerate(outs)
        for i in range(slabs)
    ]
    for copy in copies:
        copy.start()
    for copy in copies:
        copy.wait()


def take_blocks(places, weight):
    depth, cols = weight.shape[0], weight.shape[1] // 8
    count, slabs = places.shape[0], 4
    return pl.pallas_call(
        take_kernel,
        in_specs=[pl.BlockSpec(memory_space=pltpu.SMEM), pl.BlockSpec(memory_space=pltpu.HBM)],
        out_specs=[pl.BlockSpec(memory_space=pltpu.VMEM)] * count,
        out_shape=[jax.ShapeDtypeStruct((depth, cols), weight.dtype)] * count,
        scratch_shapes=[pltpu.SemaphoreType.DMA((count, slabs))],
        compiler_params=pltpu.CompilerParams(vmem_limit_bytes=48 << 20),
        cost_estimate=pl.CostEstimate(flops=0, bytes_accessed=128 * depth * cols, transcendentals=0),
        name="take_blocks",
    )(places, weight)


def conv_kernel(parts, order, me_ref, *refs):
    shares = len(order)
    data, (cos_ref, sin_ref, turn_cos_ref, turn_sin_ref) = refs[:shares], refs[shares:shares + 4]
    outs, (cols_ref, filt_ref, re_ref, im_ref) = refs[shares + 4:shares + 4 + parts], refs[shares + 4 + parts:]
    me = me_ref[0]
    rows = data[0].shape[1]
    for m, ref in zip(order, data):
        at = pl.ds(pl.multiple_of((me ^ m) * rows, rows), rows)
        for b in range(2):
            cols_ref[at, b * LANES:(b + 1) * LANES] = ref[4 + b]
        for part in range(4):
            filt_ref[part, at, :] = ref[part]
    step = 2 * rows
    for i in range(shares * rows // step):
        at = slice(i * step, (i + 1) * step)
        first_re = jnp.dot(cos_ref[at, :], cols_ref[...], preferred_element_type=jnp.float32)
        first_sin = jnp.dot(sin_ref[at, :], cols_ref[...], preferred_element_type=jnp.float32)
        tc, ts = turn_cos_ref[at, :], turn_sin_ref[at, :]
        re0, im0 = first_re[:, :LANES], -first_sin[:, :LANES]
        re1, im1 = first_re[:, LANES:], -first_sin[:, LANES:]
        re1, im1 = re1 * tc + im1 * ts, im1 * tc - re1 * ts
        f0r, f0i, f1r, f1i = re0 + re1, im0 + im1, re0 - re1, im0 - im1
        s0r, s1r, s0i, s1i = (filt_ref[part, at, :].astype(jnp.float32) for part in range(4))
        p0r, p0i = f0r * s0r - f0i * s0i, f0r * s0i + f0i * s0r
        p1r, p1i = f1r * s1r - f1i * s1i, f1r * s1i + f1i * s1r
        b0r, b0i = 0.5 * (p0r + p1r), 0.5 * (p0i + p1i)
        b1r, b1i = 0.5 * (p0r - p1r), 0.5 * (p0i - p1i)
        b1r, b1i = b1r * tc - b1i * ts, b1i * tc + b1r * ts
        re_ref[at, :] = jnp.concatenate([b0r, b1r], axis=1).astype(jnp.bfloat16)
        im_ref[at, :] = jnp.concatenate([b0i, b1i], axis=1).astype(jnp.bfloat16)
    scale = 1.0 / (shares * rows)
    part_rows = rows // parts
    for i in range(shares * rows // step):
        at = slice(i * step, (i + 1) * step)
        conv = jnp.dot(cos_ref[at, :], re_ref[...], preferred_element_type=jnp.float32)
        conv = conv - jnp.dot(sin_ref[at, :], im_ref[...], preferred_element_type=jnp.float32)
        conv = (conv * scale).astype(jnp.bfloat16)
        for s in range(2):
            for p in range(parts):
                begin = s * rows + p * part_rows
                for b in range(2):
                    outs[p][2 * i + s, b] = conv[begin:begin + part_rows, b * LANES:(b + 1) * LANES]


def convolve(me, data, order, parts):
    shares = len(data)
    rows = data[0].shape[1]
    block = shares * rows
    angle = angles(block, block, block)
    turn = np.broadcast_to(angles(block, 2, 2 * block)[:, 1:], (block, LANES))
    vmem = pl.BlockSpec(memory_space=pltpu.VMEM)
    columns = pltpu.VMEM((block, 2 * LANES), jnp.bfloat16)
    return pl.pallas_call(
        functools.partial(conv_kernel, parts, order),
        in_specs=[pl.BlockSpec(memory_space=pltpu.SMEM)] + [vmem] * (shares + 4),
        out_specs=[vmem] * parts,
        out_shape=[jax.ShapeDtypeStruct((shares, 2, rows // parts, LANES), jnp.bfloat16)] * parts,
        scratch_shapes=[columns, pltpu.VMEM((4, block, LANES), jnp.bfloat16), columns, columns],
        compiler_params=pltpu.CompilerParams(vmem_limit_bytes=24 << 20),
        cost_estimate=pl.CostEstimate(flops=50 * block * block * LANES, bytes_accessed=8 * block * block, transcendentals=0),
        name="convolve",
    )(
        me, *data, rounded(np.cos(angle)), rounded(np.sin(angle)),
        jnp.asarray(np.cos(turn).astype(np.float32)), jnp.asarray(np.sin(turn).astype(np.float32)),
    )


def gate_kernel(conv_ref, gate_ref, *refs):
    outs, held_ref = refs[:-1], refs[-1]
    shares, span, block_rows, _ = conv_ref.shape
    rows = span * block_rows
    for s in range(shares):
        held_ref[:, s * LANES:(s + 1) * LANES] = conv_ref[s].reshape(rows, LANES)
    conv = jnp.dot(join_rows(rows, span), held_ref[...], preferred_element_type=jnp.float32)
    gated = (conv * gate_ref[...].astype(jnp.float32)).astype(jnp.bfloat16)
    part = rows // len(outs)
    for p, out_ref in enumerate(outs):
        out_ref[...] = gated[p * part:(p + 1) * part]


def gate(conv, gate_out, parts):
    rows, width = gate_out.shape
    vmem = pl.BlockSpec(memory_space=pltpu.VMEM)
    return pl.pallas_call(
        gate_kernel,
        in_specs=[vmem, vmem],
        out_specs=[vmem] * parts,
        out_shape=[jax.ShapeDtypeStruct((rows // parts, width), jnp.bfloat16)] * parts,
        scratch_shapes=[pltpu.VMEM((rows, width), jnp.bfloat16)],
        compiler_params=pltpu.CompilerParams(vmem_limit_bytes=16 << 20),
        name="gate",
    )(conv, gate_out)


def own_kernel(me_ref, *refs):
    parts = (len(refs) - 1) // 2
    gated, slabs, out_ref = refs[:parts], refs[parts:-1], refs[-1]
    rows, depth = gated[0].shape[0], slabs[0].shape[0]
    for p, gated_ref in enumerate(gated):
        out_ref[0, p * rows:(p + 1) * rows] = sum(
            jnp.dot(gated_ref[:, i * depth:(i + 1) * depth], slab[...], preferred_element_type=jnp.float32)
            for i, slab in enumerate(slabs)
        )


def own_part(me, gated, weight, blocks):
    parts = len(gated)
    part_rows, depth = gated[0].shape
    cols = weight.shape[1] // 8

    def column(slab, i, me_ref):
        flip = sum((jnp.where(i == place, f, 0) for place, (f, _) in enumerate(blocks)), 0)
        half = sum((jnp.where(i == place, h, 0) for place, (_, h) in enumerate(blocks)), 0)
        return slab, (me_ref[0] ^ flip) * 2 + half

    return pl.pallas_call(
        own_kernel,
        grid_spec=pltpu.PrefetchScalarGridSpec(
            num_scalar_prefetch=1,
            grid=(len(blocks),),
            in_specs=[pl.BlockSpec((part_rows, depth), lambda i, m: (0, 0))] * parts
            + [pl.BlockSpec((depth // parts, cols), functools.partial(column, slab)) for slab in range(parts)],
            out_specs=pl.BlockSpec((1, parts * part_rows, cols), lambda i, m: (i, 0, 0)),
        ),
        out_shape=jax.ShapeDtypeStruct((len(blocks), parts * part_rows, cols), jnp.float32),
        compiler_params=pltpu.CompilerParams(vmem_limit_bytes=40 << 20),
        cost_estimate=pl.CostEstimate(
            flops=2 * parts * part_rows * depth * cols * len(blocks),
            bytes_accessed=2 * depth * cols * len(blocks), transcendentals=0,
        ),
        name="own_part",
    )(me, *gated, *[weight] * parts)


def add_kernel(parts, kept, core_ref, own_ref, *refs):
    moved, refs = refs[:2 * parts], refs[2 * parts:]
    weights, (a_ref, b_ref, held_ref, sems) = refs[:4], refs[4:]
    slabs = sems.shape[1]
    depth = held_ref.shape[1] // slabs

    def copies(side, take_mine):
        source = weights[2 * side] if take_mine else weights[2 * side + 1]
        return [
            pltpu.make_async_copy(
                source.at[i * depth:(i + 1) * depth], held_ref.at[side, i * depth:(i + 1) * depth], sems.at[side, i]
            )
            for i in range(slabs)
        ]

    mine_core = 0 if kept else 1
    for side in range(2):

        @pl.when(core_ref[0] == mine_core)
        def _():
            for copy in copies(side, True):
                copy.start()

        @pl.when(core_ref[0] != mine_core)
        def _():
            for copy in copies(side, False):
                copy.start()

    rows = moved[0].shape[0]
    for side, out_ref in enumerate((a_ref, b_ref)):
        for i, copy in enumerate(copies(side, True)):
            copy.wait()
        for p in range(parts):
            at = slice(p * rows, (p + 1) * rows)
            total = own_ref[side, at] + jnp.dot(
                moved[side * parts + p][...], held_ref[side], preferred_element_type=jnp.float32
            )
            out_ref[at] = total.astype(out_ref.dtype)


def add_moved(core, own, moved_x, moved_y, weights, first, kept, dtype):
    parts = len(moved_x)
    rows, depth = moved_x[0].shape
    cols = own.shape[2]
    whole = pl.BlockSpec((rows, depth), lambda i: (0, 0))
    shape = jax.ShapeDtypeStruct((parts * rows, cols), dtype)
    out = pl.BlockSpec((parts * rows, cols), lambda i: (0, 0))
    return pl.pallas_call(
        functools.partial(add_kernel, parts, kept),
        grid=(1,),
        in_specs=[
            pl.BlockSpec(memory_space=pltpu.SMEM),
            pl.BlockSpec((2, parts * rows, cols), lambda i: (0, first, 0)),
        ]
        + [whole] * (2 * parts)
        + [pl.BlockSpec(memory_space=pl.ANY)] * 4,
        out_specs=[out, out],
        out_shape=[shape, shape],
        scratch_shapes=[pltpu.VMEM((2, depth, cols), jnp.bfloat16), pltpu.SemaphoreType.DMA((2, 4))],
        compiler_params=pltpu.CompilerParams(vmem_limit_bytes=40 << 20),
        cost_estimate=pl.CostEstimate(
            flops=4 * parts * rows * depth * cols, bytes_accessed=4 * depth * cols, transcendentals=0
        ),
        name="add_kept" if kept else "add_sent",
    )(core, own, *moved_x, *moved_y, *weights)


def swap(data, axis, flip):
    return lax.ppermute(data, axis, [(i, i ^ flip) for i in range(lax.axis_size(axis))])


def by_channels(values, gate_in, gate_out, spectrum, out_weight):
    seq_count = lax.axis_size("seq")
    here = lax.axis_index("seq").astype(jnp.int32)
    me = lax.axis_index("chan").astype(jnp.int32)
    core = here % 2
    parts = 2

    order = tuple(sorted(range(seq_count), key=lambda m: (m == 0, m == 1, m % 2, -m)))
    packed = list(pack(here.reshape(1), values, gate_in, spectrum, seq_count))
    places = jnp.stack([(me ^ (1 + 2 * core)) * 2, (me ^ (2 + core)) * 2 + 1])
    _, places = lax.optimization_barrier((packed, places))
    block_x, block_y = take_blocks(places, out_weight)
    late = [m for m in order if m % 2]
    held, block_x, block_y = lax.optimization_barrier(([packed[m] for m in late], block_x, block_y))
    weight_x, weight_y = swap(block_x, "chan", 1), swap(block_y, "chan", 2)
    for m, mine in zip(late, held):
        packed[m] = mine
    data = [swap(packed[m], "seq", m) if m else packed[m] for m in order]
    (conv,) = convolve(here.reshape(1), data, order, 1)
    conv = lax.all_to_all(conv, "seq", split_axis=0, concat_axis=0, tiled=True)
    gated = gate(conv, gate_out, parts)
    weight_x, weight_y, _ = lax.optimization_barrier((weight_x, weight_y, gated))
    weights = [weight_x, swap(weight_x, "seq", 1), weight_y, swap(weight_y, "seq", 1)]
    own = own_part(me.reshape(1), gated, out_weight, ((2, 0), (1, 1)))
    core = core.reshape(1)
    moved_x, moved_y = [], []
    for p in range(parts):
        mine = gated[p]
        if p:
            mine, _ = lax.optimization_barrier((mine, own))
        moved_x.append(swap(mine, "chan", 1))
        moved_y.append(swap(mine, "chan", 2))
    sums_a, sums_b = [], []
    for p in range(parts):
        sent = add_moved(core, own, moved_x[p:p + 1], moved_y[p:p + 1], weights, p, False, jnp.bfloat16)
        sums_a.append(swap(sent[0], "chan", 2))
        sums_b.append(swap(sent[1], "chan", 1))
    gated, _ = lax.optimization_barrier((gated, sent))
    own = own_part(me.reshape(1), gated, out_weight, ((0, 0), (0, 1)))
    kept_a, kept_b = add_moved(core, own, moved_x, moved_y, weights, 0, True, jnp.float32)
    sums = jnp.concatenate([jnp.concatenate(sums_a, axis=0), jnp.concatenate(sums_b, axis=0)], axis=1)
    return (jnp.concatenate([kept_a, kept_b], axis=1) + sums.astype(jnp.float32)).astype(jnp.bfloat16)


def to_columns(data):
    return lax.all_to_all(data, "seq", split_axis=2, concat_axis=1, tiled=True)


def to_rows(data):
    return lax.all_to_all(data, "seq", split_axis=1, concat_axis=2, tiled=True)


def by_frequencies(values, gate_in, gate_out, spectrum, out_weight):
    seq_count = lax.axis_size("seq")
    seq_index = lax.axis_index("seq")
    tok_rows, chan_width = values.shape
    block_rows = BLOCK // seq_count
    span = tok_rows // block_rows
    tokens_all = BLOCK * span
    col_share = span * chan_width // seq_count
    block_cos = rounded(np.cos(angles(BLOCK, BLOCK, BLOCK)))
    block_sin = rounded(np.sin(angles(BLOCK, BLOCK, BLOCK)))
    span_cos = rounded(np.cos(angles(span, span, span)))
    span_sin = rounded(np.sin(angles(span, span, span)))
    turn_all = angles(BLOCK, span, tokens_all)
    turn_cos_all = jnp.asarray(np.cos(turn_all).astype(np.float32))
    turn_sin_all = jnp.asarray(np.sin(turn_all).astype(np.float32))
    source = (values.astype(jnp.float32) * gate_in.astype(jnp.float32)).astype(jnp.bfloat16)
    spread = to_columns(source.reshape(1, block_rows, seq_count, col_share))
    columns = spread.reshape(BLOCK, col_share)
    cos_part = jnp.dot(jnp.transpose(block_cos), columns, preferred_element_type=jnp.float32)
    sin_part = jnp.dot(jnp.transpose(block_sin), columns, preferred_element_type=jnp.float32)
    col_pos = (seq_index * col_share + jnp.arange(col_share, dtype=jnp.int32)) // chan_width
    turn_cos = jnp.take(turn_cos_all, col_pos, axis=1)
    turn_sin = jnp.take(turn_sin_all, col_pos, axis=1)
    twist_re = cos_part * turn_cos - sin_part * turn_sin
    twist_im = -sin_part * turn_cos - cos_part * turn_sin
    twisted = jnp.stack([twist_re, twist_im]).astype(jnp.bfloat16)
    arranged = to_rows(twisted).reshape(2, block_rows, span, chan_width)
    with_cos = jnp.einsum("bd,kcbh->kdch", span_cos, arranged, preferred_element_type=jnp.float32)
    with_sin = jnp.einsum("bd,kcbh->kdch", span_sin, arranged, preferred_element_type=jnp.float32)
    freq_re = with_cos[0] + with_sin[1]
    freq_im = with_cos[1] - with_sin[0]
    prod_re = freq_re * spectrum[0] - freq_im * spectrum[1]
    prod_im = freq_re * spectrum[1] + freq_im * spectrum[0]
    product = jnp.stack([prod_re, prod_im]).astype(jnp.bfloat16)
    back_cos = jnp.einsum("db,kdch->kcbh", span_cos, product, preferred_element_type=jnp.float32)
    back_sin = jnp.einsum("db,kdch->kcbh", span_sin, product, preferred_element_type=jnp.float32)
    back_re = (back_cos[0] - back_sin[1]) / span
    back_im = (back_cos[1] + back_sin[0]) / span
    back_tc = lax.dynamic_slice_in_dim(turn_cos_all, seq_index * block_rows, block_rows)[:, :, None]
    back_ts = lax.dynamic_slice_in_dim(turn_sin_all, seq_index * block_rows, block_rows)[:, :, None]
    rotated = jnp.stack(
        [back_re * back_tc - back_im * back_ts, back_im * back_tc + back_re * back_ts]
    ).astype(jnp.bfloat16)
    gathered = to_columns(rotated.reshape(2, block_rows, seq_count, col_share)).reshape(2, BLOCK, col_share)
    summed = jnp.dot(block_cos, gathered[0], preferred_element_type=jnp.float32)
    summed = summed - jnp.dot(block_sin, gathered[1], preferred_element_type=jnp.float32)
    ordered = (summed / BLOCK).astype(jnp.bfloat16).reshape(1, BLOCK, col_share)
    conv = to_rows(ordered).reshape(tok_rows, chan_width)
    gated = (conv.astype(jnp.float32) * gate_out.astype(jnp.float32)).astype(jnp.bfloat16)
    partial_sum = jnp.dot(gated, out_weight, preferred_element_type=jnp.float32)
    return lax.psum_scatter(partial_sum.astype(jnp.bfloat16), "chan", scatter_dimension=1, tiled=True)


def shards(values, gate_in, gate_out, spectrum, out_weight):
    seq_count, chan_count = lax.axis_size("seq"), lax.axis_size("chan")
    _, span, block_rows, width = spectrum.shape
    one_lane_block = width == seq_count * LANES and block_rows % 32 == 0
    if span == 2 and chan_count == 4 and seq_count & (seq_count - 1) == 0 and one_lane_block:
        return by_channels(values, gate_in, gate_out, spectrum, out_weight)
    return by_frequencies(values, gate_in, gate_out, spectrum, out_weight)


def solution(mesh):
    placed = (
        P("seq", "chan"),
        P("seq", "chan"),
        P("seq", "chan"),
        P(None, None, "seq", "chan"),
        P("chan", None),
    )
    return jax.shard_map(
        shards, mesh=mesh, in_specs=placed, out_specs=P("seq", "chan"), check_vma=False
    )
```

```python
import functools
import math

import jax
import jax.numpy as jnp
import ml_dtypes
import numpy as np
from jax import lax
from jax.experimental import pallas as pl
from jax.experimental.pallas import tpu as pltpu
from jax.sharding import PartitionSpec as P

BLOCK = 1024
LANES = 128


def angles(first, second, period):
    return (np.arange(first)[:, None] * np.arange(second)[None, :] % period) * (2.0 * math.pi / period)


def rounded(table):
    return jnp.asarray(table.astype(np.float32).astype(ml_dtypes.bfloat16))


def split_rows(rows, span):
    out = lax.broadcasted_iota(jnp.int32, (rows, rows), 0)
    token = lax.broadcasted_iota(jnp.int32, (rows, rows), 1)
    block_rows = rows // span
    return jnp.where(token == (out % block_rows) * span + out // block_rows, 1.0, 0.0).astype(jnp.bfloat16)


def join_rows(rows, span):
    token = lax.broadcasted_iota(jnp.int32, (rows, rows), 0)
    held = lax.broadcasted_iota(jnp.int32, (rows, rows), 1)
    block_rows = rows // span
    return jnp.where(token == (held % block_rows) * span + held // block_rows, 1.0, 0.0).astype(jnp.bfloat16)


def pack_kernel(span, me_ref, values_hbm, gate_hbm, spectrum_hbm, *refs):
    outs, (values_ref, gate_ref, spectrum_ref, sems) = refs[:-4], refs[-4:]
    copies = [
        pltpu.make_async_copy(values_hbm, values_ref, sems.at[0]),
        pltpu.make_async_copy(gate_hbm, gate_ref, sems.at[1]),
    ]
    for part in range(2):
        for d in range(span):
            copies.append(pltpu.make_async_copy(
                spectrum_hbm.at[part, d], spectrum_ref.at[part * span + d], sems.at[2 + part * span + d]
            ))
    for copy in copies:
        copy.start()
    me = me_ref[0]
    rows = values_ref.shape[0]
    block_rows = rows // span
    copies[0].wait()
    copies[1].wait()
    source = (values_ref[...].astype(jnp.float32) * gate_ref[...].astype(jnp.float32)).astype(jnp.bfloat16)
    values_ref[...] = jnp.dot(
        split_rows(rows, span), source, preferred_element_type=jnp.float32
    ).astype(jnp.bfloat16)

    def lanes_of(m):
        return pl.ds(pl.multiple_of((me ^ m) * LANES, LANES), LANES)

    for m, out_ref in enumerate(outs):
        for b in range(span):
            out_ref[2 * span + b] = values_ref[b * block_rows:(b + 1) * block_rows, lanes_of(m)]
    for part in range(2 * span):
        copies[2 + part].wait()
        for m, out_ref in enumerate(outs):
            out_ref[part] = spectrum_ref[part, :, lanes_of(m)].astype(jnp.bfloat16)


def pack(me, values, gate_in, spectrum, shares):
    rows, width = values.shape
    _, span, block_rows, _ = spectrum.shape
    shape = (3 * span, block_rows, LANES)
    vmem, hbm = pl.BlockSpec(memory_space=pltpu.VMEM), pl.BlockSpec(memory_space=pltpu.HBM)
    return pl.pallas_call(
        functools.partial(pack_kernel, span),
        in_specs=[pl.BlockSpec(memory_space=pltpu.SMEM), hbm, hbm, hbm],
        out_specs=[vmem] * shares,
        out_shape=[jax.ShapeDtypeStruct(shape, jnp.bfloat16)] * shares,
        scratch_shapes=[
            pltpu.VMEM((rows, width), jnp.bfloat16),
            pltpu.VMEM((rows, width), jnp.bfloat16),
            pltpu.VMEM((2 * span, block_rows, width), jnp.float32),
            pltpu.SemaphoreType.DMA((2 + 2 * span,)),
        ],
        compiler_params=pltpu.CompilerParams(vmem_limit_bytes=60 << 20),
        name="pack",
    )(me, values, gate_in, spectrum)


def take_kernel(places_ref, weight_hbm, *refs):
    outs, sems = refs[:-1], refs[-1]
    slabs = sems.shape[1]
    depth, cols = outs[0].shape[0] // slabs, outs[0].shape[1]
    copies = [
        pltpu.make_async_copy(
            weight_hbm.at[i * depth:(i + 1) * depth, pl.ds(pl.multiple_of(places_ref[k] * cols, cols), cols)],
            out_ref.at[i * depth:(i + 1) * depth],
            sems.at[k, i],
        )
        for k, out_ref in enumerate(outs)
        for i in range(slabs)
    ]
    for copy in copies:
        copy.start()
    for copy in copies:
        copy.wait()


def take_blocks(places, weight):
    depth, cols = weight.shape[0], weight.shape[1] // 8
    count, slabs = places.shape[0], 4
    return pl.pallas_call(
        take_kernel,
        in_specs=[pl.BlockSpec(memory_space=pltpu.SMEM), pl.BlockSpec(memory_space=pltpu.HBM)],
        out_specs=[pl.BlockSpec(memory_space=pltpu.VMEM)] * count,
        out_shape=[jax.ShapeDtypeStruct((depth, cols), weight.dtype)] * count,
        scratch_shapes=[pltpu.SemaphoreType.DMA((count, slabs))],
        compiler_params=pltpu.CompilerParams(vmem_limit_bytes=48 << 20),
        cost_estimate=pl.CostEstimate(flops=0, bytes_accessed=128 * depth * cols, transcendentals=0),
        name="take_blocks",
    )(places, weight)


def conv_kernel(parts, order, me_ref, *refs):
    shares = len(order)
    data, (cos_ref, sin_ref, turn_cos_ref, turn_sin_ref) = refs[:shares], refs[shares:shares + 4]
    outs, (cols_ref, filt_ref, re_ref, im_ref) = refs[shares + 4:shares + 4 + parts], refs[shares + 4 + parts:]
    me = me_ref[0]
    rows = data[0].shape[1]
    for m, ref in zip(order, data):
        at = pl.ds(pl.multiple_of((me ^ m) * rows, rows), rows)
        for b in range(2):
            cols_ref[at, b * LANES:(b + 1) * LANES] = ref[4 + b]
        for part in range(4):
            filt_ref[part, at, :] = ref[part]
    step = 2 * rows
    for i in range(shares * rows // step):
        at = slice(i * step, (i + 1) * step)
        first_re = jnp.dot(cos_ref[at, :], cols_ref[...], preferred_element_type=jnp.float32)
        first_sin = jnp.dot(sin_ref[at, :], cols_ref[...], preferred_element_type=jnp.float32)
        tc, ts = turn_cos_ref[at, :], turn_sin_ref[at, :]
        re0, im0 = first_re[:, :LANES], -first_sin[:, :LANES]
        re1, im1 = first_re[:, LANES:], -first_sin[:, LANES:]
        re1, im1 = re1 * tc + im1 * ts, im1 * tc - re1 * ts
        f0r, f0i, f1r, f1i = re0 + re1, im0 + im1, re0 - re1, im0 - im1
        s0r, s1r, s0i, s1i = (filt_ref[part, at, :].astype(jnp.float32) for part in range(4))
        p0r, p0i = f0r * s0r - f0i * s0i, f0r * s0i + f0i * s0r
        p1r, p1i = f1r * s1r - f1i * s1i, f1r * s1i + f1i * s1r
        b0r, b0i = 0.5 * (p0r + p1r), 0.5 * (p0i + p1i)
        b1r, b1i = 0.5 * (p0r - p1r), 0.5 * (p0i - p1i)
        b1r, b1i = b1r * tc - b1i * ts, b1i * tc + b1r * ts
        re_ref[at, :] = jnp.concatenate([b0r, b1r], axis=1).astype(jnp.bfloat16)
        im_ref[at, :] = jnp.concatenate([b0i, b1i], axis=1).astype(jnp.bfloat16)
    scale = 1.0 / (shares * rows)
    part_rows = rows // parts
    for i in range(shares * rows // step):
        at = slice(i * step, (i + 1) * step)
        conv = jnp.dot(cos_ref[at, :], re_ref[...], preferred_element_type=jnp.float32)
        conv = conv - jnp.dot(sin_ref[at, :], im_ref[...], preferred_element_type=jnp.float32)
        conv = (conv * scale).astype(jnp.bfloat16)
        for s in range(2):
            for p in range(parts):
                begin = s * rows + p * part_rows
                for b in range(2):
                    outs[p][2 * i + s, b] = conv[begin:begin + part_rows, b * LANES:(b + 1) * LANES]


def convolve(me, data, order, parts):
    shares = len(data)
    rows = data[0].shape[1]
    block = shares * rows
    angle = angles(block, block, block)
    turn = np.broadcast_to(angles(block, 2, 2 * block)[:, 1:], (block, LANES))
    vmem = pl.BlockSpec(memory_space=pltpu.VMEM)
    columns = pltpu.VMEM((block, 2 * LANES), jnp.bfloat16)
    return pl.pallas_call(
        functools.partial(conv_kernel, parts, order),
        in_specs=[pl.BlockSpec(memory_space=pltpu.SMEM)] + [vmem] * (shares + 4),
        out_specs=[vmem] * parts,
        out_shape=[jax.ShapeDtypeStruct((shares, 2, rows // parts, LANES), jnp.bfloat16)] * parts,
        scratch_shapes=[columns, pltpu.VMEM((4, block, LANES), jnp.bfloat16), columns, columns],
        compiler_params=pltpu.CompilerParams(vmem_limit_bytes=24 << 20),
        cost_estimate=pl.CostEstimate(flops=50 * block * block * LANES, bytes_accessed=8 * block * block, transcendentals=0),
        name="convolve",
    )(
        me, *data, rounded(np.cos(angle)), rounded(np.sin(angle)),
        jnp.asarray(np.cos(turn).astype(np.float32)), jnp.asarray(np.sin(turn).astype(np.float32)),
    )


def gate_kernel(conv_ref, gate_ref, *refs):
    outs, held_ref = refs[:-1], refs[-1]
    shares, span, block_rows, _ = conv_ref.shape
    rows = span * block_rows
    for s in range(shares):
        held_ref[:, s * LANES:(s + 1) * LANES] = conv_ref[s].reshape(rows, LANES)
    conv = jnp.dot(join_rows(rows, span), held_ref[...], preferred_element_type=jnp.float32)
    gated = (conv * gate_ref[...].astype(jnp.float32)).astype(jnp.bfloat16)
    part = rows // len(outs)
    for p, out_ref in enumerate(outs):
        out_ref[...] = gated[p * part:(p + 1) * part]


def gate(conv, gate_out, parts):
    rows, width = gate_out.shape
    vmem = pl.BlockSpec(memory_space=pltpu.VMEM)
    return pl.pallas_call(
        gate_kernel,
        in_specs=[vmem, vmem],
        out_specs=[vmem] * parts,
        out_shape=[jax.ShapeDtypeStruct((rows // parts, width), jnp.bfloat16)] * parts,
        scratch_shapes=[pltpu.VMEM((rows, width), jnp.bfloat16)],
        compiler_params=pltpu.CompilerParams(vmem_limit_bytes=16 << 20),
        name="gate",
    )(conv, gate_out)


def own_kernel(me_ref, *refs):
    parts = (len(refs) - 1) // 2
    gated, slabs, out_ref = refs[:parts], refs[parts:-1], refs[-1]
    rows, depth = gated[0].shape[0], slabs[0].shape[0]
    for p, gated_ref in enumerate(gated):
        out_ref[0, p * rows:(p + 1) * rows] = sum(
            jnp.dot(gated_ref[:, i * depth:(i + 1) * depth], slab[...], preferred_element_type=jnp.float32)
            for i, slab in enumerate(slabs)
        )


def own_part(me, gated, weight, blocks):
    parts = len(gated)
    part_rows, depth = gated[0].shape
    cols = weight.shape[1] // 8

    def column(slab, i, me_ref):
        flip = sum((jnp.where(i == place, f, 0) for place, (f, _) in enumerate(blocks)), 0)
        half = sum((jnp.where(i == place, h, 0) for place, (_, h) in enumerate(blocks)), 0)
        return slab, (me_ref[0] ^ flip) * 2 + half

    return pl.pallas_call(
        own_kernel,
        grid_spec=pltpu.PrefetchScalarGridSpec(
            num_scalar_prefetch=1,
            grid=(len(blocks),),
            in_specs=[pl.BlockSpec((part_rows, depth), lambda i, m: (0, 0))] * parts
            + [pl.BlockSpec((depth // parts, cols), functools.partial(column, slab)) for slab in range(parts)],
            out_specs=pl.BlockSpec((1, parts * part_rows, cols), lambda i, m: (i, 0, 0)),
        ),
        out_shape=jax.ShapeDtypeStruct((len(blocks), parts * part_rows, cols), jnp.float32),
        compiler_params=pltpu.CompilerParams(vmem_limit_bytes=40 << 20),
        cost_estimate=pl.CostEstimate(
            flops=2 * parts * part_rows * depth * cols * len(blocks),
            bytes_accessed=2 * depth * cols * len(blocks), transcendentals=0,
        ),
        name="own_part",
    )(me, *gated, *[weight] * parts)


def add_kernel(parts, kept, core_ref, own_ref, *refs):
    moved, refs = refs[:2 * parts], refs[2 * parts:]
    weights, (a_ref, b_ref, held_ref, sems) = refs[:4], refs[4:]
    slabs = sems.shape[1]
    depth = held_ref.shape[1] // slabs

    def copies(side, take_mine):
        source = weights[2 * side] if take_mine else weights[2 * side + 1]
        return [
            pltpu.make_async_copy(
                source.at[i * depth:(i + 1) * depth], held_ref.at[side, i * depth:(i + 1) * depth], sems.at[side, i]
            )
            for i in range(slabs)
        ]

    mine_core = 0 if kept else 1
    for side in range(2):

        @pl.when(core_ref[0] == mine_core)
        def _():
            for copy in copies(side, True):
                copy.start()

        @pl.when(core_ref[0] != mine_core)
        def _():
            for copy in copies(side, False):
                copy.start()

    rows = moved[0].shape[0]
    for side, out_ref in enumerate((a_ref, b_ref)):
        for i, copy in enumerate(copies(side, True)):
            copy.wait()
        for p in range(parts):
            at = slice(p * rows, (p + 1) * rows)
            total = own_ref[side, at] + jnp.dot(
                moved[side * parts + p][...], held_ref[side], preferred_element_type=jnp.float32
            )
            out_ref[at] = total.astype(out_ref.dtype)


def add_moved(core, own, moved_x, moved_y, weights, first, kept, dtype):
    parts = len(moved_x)
    rows, depth = moved_x[0].shape
    cols = own.shape[2]
    whole = pl.BlockSpec((rows, depth), lambda i: (0, 0))
    shape = jax.ShapeDtypeStruct((parts * rows, cols), dtype)
    out = pl.BlockSpec((parts * rows, cols), lambda i: (0, 0))
    return pl.pallas_call(
        functools.partial(add_kernel, parts, kept),
        grid=(1,),
        in_specs=[
            pl.BlockSpec(memory_space=pltpu.SMEM),
            pl.BlockSpec((2, parts * rows, cols), lambda i: (0, first, 0)),
        ]
        + [whole] * (2 * parts)
        + [pl.BlockSpec(memory_space=pl.ANY)] * 4,
        out_specs=[out, out],
        out_shape=[shape, shape],
        scratch_shapes=[pltpu.VMEM((2, depth, cols), jnp.bfloat16), pltpu.SemaphoreType.DMA((2, 4))],
        compiler_params=pltpu.CompilerParams(vmem_limit_bytes=40 << 20),
        cost_estimate=pl.CostEstimate(
            flops=4 * parts * rows * depth * cols, bytes_accessed=4 * depth * cols, transcendentals=0
        ),
        name="add_kept" if kept else "add_sent",
    )(core, own, *moved_x, *moved_y, *weights)


def swap(data, axis, flip):
    return lax.ppermute(data, axis, [(i, i ^ flip) for i in range(lax.axis_size(axis))])


def by_channels(values, gate_in, gate_out, spectrum, out_weight):
    seq_count = lax.axis_size("seq")
    here = lax.axis_index("seq").astype(jnp.int32)
    me = lax.axis_index("chan").astype(jnp.int32)
    core = here % 2
    parts = 2

    order = tuple(sorted(range(seq_count), key=lambda m: (m == 0, m == 1, m % 2, -m)))
    packed = list(pack(here.reshape(1), values, gate_in, spectrum, seq_count))
    places = jnp.stack([(me ^ (1 + 2 * core)) * 2, (me ^ (2 + core)) * 2 + 1])
    _, places = lax.optimization_barrier((packed, places))
    block_x, block_y = take_blocks(places, out_weight)
    late = [m for m in order if m % 2]
    weight_x, weight_y = swap(block_x, "chan", 1), swap(block_y, "chan", 2)
    data = {m: swap(packed[m], "seq", m) if m else packed[m] for m in order if m % 2 == 0}
    held, data[order[0]] = lax.optimization_barrier(([packed[m] for m in late], data[order[0]]))
    data.update({m: swap(mine, "seq", m) for m, mine in zip(late, held)})
    (conv,) = convolve(here.reshape(1), [data[m] for m in order], order, 1)
    conv = lax.all_to_all(conv, "seq", split_axis=0, concat_axis=0, tiled=True)
    gated = gate(conv, gate_out, parts)
    weight_x, weight_y, _ = lax.optimization_barrier((weight_x, weight_y, gated))
    weights = [weight_x, swap(weight_x, "seq", 1), weight_y, swap(weight_y, "seq", 1)]
    own = own_part(me.reshape(1), gated, out_weight, ((2, 0), (1, 1)))
    core = core.reshape(1)
    moved_x, moved_y = [], []
    for p in range(parts):
        mine = gated[p]
        if p:
            mine, own, weights[1] = lax.optimization_barrier((mine, own, weights[1]))
        moved_x.append(swap(mine, "chan", 1))
        moved_y.append(swap(mine, "chan", 2))
    sums_a, sums_b = [], []
    for p in range(parts):
        if p == parts - 1:
            own_kept = own_part(me.reshape(1), gated, out_weight, ((0, 0), (0, 1)))
            own, own_kept = lax.optimization_barrier((own, own_kept))
        sent = add_moved(core, own, moved_x[p:p + 1], moved_y[p:p + 1], weights, p, False, jnp.bfloat16)
        sums_a.append(swap(sent[0], "chan", 2))
        sums_b.append(swap(sent[1], "chan", 1))
    kept_a, kept_b = add_moved(core, own_kept, moved_x, moved_y, weights, 0, True, jnp.float32)
    sums = jnp.concatenate([jnp.concatenate(sums_a, axis=0), jnp.concatenate(sums_b, axis=0)], axis=1)
    return (jnp.concatenate([kept_a, kept_b], axis=1) + sums.astype(jnp.float32)).astype(jnp.bfloat16)


def to_columns(data):
    return lax.all_to_all(data, "seq", split_axis=2, concat_axis=1, tiled=True)


def to_rows(data):
    return lax.all_to_all(data, "seq", split_axis=1, concat_axis=2, tiled=True)


def by_frequencies(values, gate_in, gate_out, spectrum, out_weight):
    seq_count = lax.axis_size("seq")
    seq_index = lax.axis_index("seq")
    tok_rows, chan_width = values.shape
    block_rows = BLOCK // seq_count
    span = tok_rows // block_rows
    tokens_all = BLOCK * span
    col_share = span * chan_width // seq_count
    block_cos = rounded(np.cos(angles(BLOCK, BLOCK, BLOCK)))
    block_sin = rounded(np.sin(angles(BLOCK, BLOCK, BLOCK)))
    span_cos = rounded(np.cos(angles(span, span, span)))
    span_sin = rounded(np.sin(angles(span, span, span)))
    turn_all = angles(BLOCK, span, tokens_all)
    turn_cos_all = jnp.asarray(np.cos(turn_all).astype(np.float32))
    turn_sin_all = jnp.asarray(np.sin(turn_all).astype(np.float32))
    source = (values.astype(jnp.float32) * gate_in.astype(jnp.float32)).astype(jnp.bfloat16)
    spread = to_columns(source.reshape(1, block_rows, seq_count, col_share))
    columns = spread.reshape(BLOCK, col_share)
    cos_part = jnp.dot(jnp.transpose(block_cos), columns, preferred_element_type=jnp.float32)
    sin_part = jnp.dot(jnp.transpose(block_sin), columns, preferred_element_type=jnp.float32)
    col_pos = (seq_index * col_share + jnp.arange(col_share, dtype=jnp.int32)) // chan_width
    turn_cos = jnp.take(turn_cos_all, col_pos, axis=1)
    turn_sin = jnp.take(turn_sin_all, col_pos, axis=1)
    twist_re = cos_part * turn_cos - sin_part * turn_sin
    twist_im = -sin_part * turn_cos - cos_part * turn_sin
    twisted = jnp.stack([twist_re, twist_im]).astype(jnp.bfloat16)
    arranged = to_rows(twisted).reshape(2, block_rows, span, chan_width)
    with_cos = jnp.einsum("bd,kcbh->kdch", span_cos, arranged, preferred_element_type=jnp.float32)
    with_sin = jnp.einsum("bd,kcbh->kdch", span_sin, arranged, preferred_element_type=jnp.float32)
    freq_re = with_cos[0] + with_sin[1]
    freq_im = with_cos[1] - with_sin[0]
    prod_re = freq_re * spectrum[0] - freq_im * spectrum[1]
    prod_im = freq_re * spectrum[1] + freq_im * spectrum[0]
    product = jnp.stack([prod_re, prod_im]).astype(jnp.bfloat16)
    back_cos = jnp.einsum("db,kdch->kcbh", span_cos, product, preferred_element_type=jnp.float32)
    back_sin = jnp.einsum("db,kdch->kcbh", span_sin, product, preferred_element_type=jnp.float32)
    back_re = (back_cos[0] - back_sin[1]) / span
    back_im = (back_cos[1] + back_sin[0]) / span
    back_tc = lax.dynamic_slice_in_dim(turn_cos_all, seq_index * block_rows, block_rows)[:, :, None]
    back_ts = lax.dynamic_slice_in_dim(turn_sin_all, seq_index * block_rows, block_rows)[:, :, None]
    rotated = jnp.stack(
        [back_re * back_tc - back_im * back_ts, back_im * back_tc + back_re * back_ts]
    ).astype(jnp.bfloat16)
    gathered = to_columns(rotated.reshape(2, block_rows, seq_count, col_share)).reshape(2, BLOCK, col_share)
    summed = jnp.dot(block_cos, gathered[0], preferred_element_type=jnp.float32)
    summed = summed - jnp.dot(block_sin, gathered[1], preferred_element_type=jnp.float32)
    ordered = (summed / BLOCK).astype(jnp.bfloat16).reshape(1, BLOCK, col_share)
    conv = to_rows(ordered).reshape(tok_rows, chan_width)
    gated = (conv.astype(jnp.float32) * gate_out.astype(jnp.float32)).astype(jnp.bfloat16)
    partial_sum = jnp.dot(gated, out_weight, preferred_element_type=jnp.float32)
    return lax.psum_scatter(partial_sum.astype(jnp.bfloat16), "chan", scatter_dimension=1, tiled=True)


def shards(values, gate_in, gate_out, spectrum, out_weight):
    seq_count, chan_count = lax.axis_size("seq"), lax.axis_size("chan")
    _, span, block_rows, width = spectrum.shape
    one_lane_block = width == seq_count * LANES and block_rows % 32 == 0
    if span == 2 and chan_count == 4 and seq_count & (seq_count - 1) == 0 and one_lane_block:
        return by_channels(values, gate_in, gate_out, spectrum, out_weight)
    return by_frequencies(values, gate_in, gate_out, spectrum, out_weight)


def solution(mesh):
    placed = (
        P("seq", "chan"),
        P("seq", "chan"),
        P("seq", "chan"),
        P(None, None, "seq", "chan"),
        P("chan", None),
    )
    return jax.shard_map(
        shards, mesh=mesh, in_specs=placed, out_specs=P("seq", "chan"), check_vma=False
    )
```

```python
import functools
import math

import jax
import jax.numpy as jnp
import ml_dtypes
import numpy as np
from jax import lax
from jax.experimental import pallas as pl
from jax.experimental.pallas import tpu as pltpu
from jax.sharding import PartitionSpec as P

BLOCK = 1024
LANES = 128


def angles(first, second, period):
    return (np.arange(first)[:, None] * np.arange(second)[None, :] % period) * (2.0 * math.pi / period)


def rounded(table):
    return jnp.asarray(table.astype(np.float32).astype(ml_dtypes.bfloat16))


def split_rows(rows, span):
    out = lax.broadcasted_iota(jnp.int32, (rows, rows), 0)
    token = lax.broadcasted_iota(jnp.int32, (rows, rows), 1)
    block_rows = rows // span
    return jnp.where(token == (out % block_rows) * span + out // block_rows, 1.0, 0.0).astype(jnp.bfloat16)


def join_rows(rows, span):
    token = lax.broadcasted_iota(jnp.int32, (rows, rows), 0)
    held = lax.broadcasted_iota(jnp.int32, (rows, rows), 1)
    block_rows = rows // span
    return jnp.where(token == (held % block_rows) * span + held // block_rows, 1.0, 0.0).astype(jnp.bfloat16)


def pack_kernel(span, me_ref, values_hbm, gate_hbm, spectrum_hbm, *refs):
    outs, (values_ref, gate_ref, spectrum_ref, sems) = refs[:-4], refs[-4:]
    copies = [
        pltpu.make_async_copy(values_hbm, values_ref, sems.at[0]),
        pltpu.make_async_copy(gate_hbm, gate_ref, sems.at[1]),
    ]
    for part in range(2):
        for d in range(span):
            copies.append(pltpu.make_async_copy(
                spectrum_hbm.at[part, d], spectrum_ref.at[part * span + d], sems.at[2 + part * span + d]
            ))
    for copy in copies:
        copy.start()
    me = me_ref[0]
    rows = values_ref.shape[0]
    block_rows = rows // span
    copies[0].wait()
    copies[1].wait()
    source = (values_ref[...].astype(jnp.float32) * gate_ref[...].astype(jnp.float32)).astype(jnp.bfloat16)
    values_ref[...] = jnp.dot(
        split_rows(rows, span), source, preferred_element_type=jnp.float32
    ).astype(jnp.bfloat16)

    def lanes_of(m):
        return pl.ds(pl.multiple_of((me ^ m) * LANES, LANES), LANES)

    for m, out_ref in enumerate(outs):
        for b in range(span):
            out_ref[2 * span + b] = values_ref[b * block_rows:(b + 1) * block_rows, lanes_of(m)]
    for part in range(2 * span):
        copies[2 + part].wait()
        for m, out_ref in enumerate(outs):
            out_ref[part] = spectrum_ref[part, :, lanes_of(m)].astype(jnp.bfloat16)


def pack(me, values, gate_in, spectrum, shares):
    rows, width = values.shape
    _, span, block_rows, _ = spectrum.shape
    shape = (3 * span, block_rows, LANES)
    vmem, hbm = pl.BlockSpec(memory_space=pltpu.VMEM), pl.BlockSpec(memory_space=pltpu.HBM)
    return pl.pallas_call(
        functools.partial(pack_kernel, span),
        in_specs=[pl.BlockSpec(memory_space=pltpu.SMEM), hbm, hbm, hbm],
        out_specs=[vmem] * shares,
        out_shape=[jax.ShapeDtypeStruct(shape, jnp.bfloat16)] * shares,
        scratch_shapes=[
            pltpu.VMEM((rows, width), jnp.bfloat16),
            pltpu.VMEM((rows, width), jnp.bfloat16),
            pltpu.VMEM((2 * span, block_rows, width), jnp.float32),
            pltpu.SemaphoreType.DMA((2 + 2 * span,)),
        ],
        compiler_params=pltpu.CompilerParams(vmem_limit_bytes=60 << 20),
        name="pack",
    )(me, values, gate_in, spectrum)


def take_kernel(places_ref, weight_hbm, *refs):
    outs, sems = refs[:-1], refs[-1]
    slabs = sems.shape[1]
    depth, cols = outs[0].shape[0] // slabs, outs[0].shape[1]
    copies = [
        pltpu.make_async_copy(
            weight_hbm.at[i * depth:(i + 1) * depth, pl.ds(pl.multiple_of(places_ref[k] * cols, cols), cols)],
            out_ref.at[i * depth:(i + 1) * depth],
            sems.at[k, i],
        )
        for k, out_ref in enumerate(outs)
        for i in range(slabs)
    ]
    for copy in copies:
        copy.start()
    for copy in copies:
        copy.wait()


def take_blocks(places, weight):
    depth, cols = weight.shape[0], weight.shape[1] // 8
    count, slabs = places.shape[0], 4
    return pl.pallas_call(
        take_kernel,
        in_specs=[pl.BlockSpec(memory_space=pltpu.SMEM), pl.BlockSpec(memory_space=pltpu.HBM)],
        out_specs=[pl.BlockSpec(memory_space=pltpu.VMEM)] * count,
        out_shape=[jax.ShapeDtypeStruct((depth, cols), weight.dtype)] * count,
        scratch_shapes=[pltpu.SemaphoreType.DMA((count, slabs))],
        compiler_params=pltpu.CompilerParams(vmem_limit_bytes=48 << 20),
        cost_estimate=pl.CostEstimate(flops=0, bytes_accessed=128 * depth * cols, transcendentals=0),
        name="take_blocks",
    )(places, weight)


def conv_kernel(order, me_ref, *refs):
    shares = len(order)
    data, (cos_ref, sin_ref, turn_cos_ref, turn_sin_ref) = refs[:shares], refs[shares:shares + 4]
    mine_ref, other_ref, cols_ref, filt_ref, re_ref, im_ref = refs[shares + 4:]
    me = me_ref[0]
    chip, core = me // 2, me % 2
    rows = data[0].shape[1]
    for m, ref in zip(order, data):
        at = pl.ds(pl.multiple_of((me ^ m) * rows, rows), rows)
        for b in range(2):
            cols_ref[at, b * LANES:(b + 1) * LANES] = ref[4 + b]
        for part in range(4):
            filt_ref[part, at, :] = ref[part]
    step = 2 * rows
    for i in range(shares * rows // step):
        at = slice(i * step, (i + 1) * step)
        first_re = jnp.dot(cos_ref[at, :], cols_ref[...], preferred_element_type=jnp.float32)
        first_sin = jnp.dot(sin_ref[at, :], cols_ref[...], preferred_element_type=jnp.float32)
        tc, ts = turn_cos_ref[at, :], turn_sin_ref[at, :]
        re0, im0 = first_re[:, :LANES], -first_sin[:, :LANES]
        re1, im1 = first_re[:, LANES:], -first_sin[:, LANES:]
        re1, im1 = re1 * tc + im1 * ts, im1 * tc - re1 * ts
        f0r, f0i, f1r, f1i = re0 + re1, im0 + im1, re0 - re1, im0 - im1
        s0r, s1r, s0i, s1i = (filt_ref[part, at, :].astype(jnp.float32) for part in range(4))
        p0r, p0i = f0r * s0r - f0i * s0i, f0r * s0i + f0i * s0r
        p1r, p1i = f1r * s1r - f1i * s1i, f1r * s1i + f1i * s1r
        b0r, b0i = 0.5 * (p0r + p1r), 0.5 * (p0i + p1i)
        b1r, b1i = 0.5 * (p0r - p1r), 0.5 * (p0i - p1i)
        b1r, b1i = b1r * tc - b1i * ts, b1i * tc + b1r * ts
        re_ref[at, :] = jnp.concatenate([b0r, b1r], axis=1).astype(jnp.bfloat16)
        im_ref[at, :] = jnp.concatenate([b0i, b1i], axis=1).astype(jnp.bfloat16)
    scale = 1.0 / (shares * rows)
    for i in range(shares * rows // step):
        at = slice(i * step, (i + 1) * step)
        conv = jnp.dot(cos_ref[at, :], re_ref[...], preferred_element_type=jnp.float32)
        conv = conv - jnp.dot(sin_ref[at, :], im_ref[...], preferred_element_type=jnp.float32)
        conv = (conv * scale).astype(jnp.bfloat16)
        for b in range(2):
            lanes = slice(b * LANES, (b + 1) * LANES)
            low, high = conv[:rows, lanes], conv[rows:, lanes]
            mine_ref[i ^ chip, b] = jnp.where(core == 0, low, high)
            other_ref[i ^ chip, b] = jnp.where(core == 0, high, low)


def convolve(me, data, order):
    shares = len(data)
    rows = data[0].shape[1]
    block = shares * rows
    angle = angles(block, block, block)
    turn = np.broadcast_to(angles(block, 2, 2 * block)[:, 1:], (block, LANES))
    vmem = pl.BlockSpec(memory_space=pltpu.VMEM)
    columns = pltpu.VMEM((block, 2 * LANES), jnp.bfloat16)
    return pl.pallas_call(
        functools.partial(conv_kernel, order),
        in_specs=[pl.BlockSpec(memory_space=pltpu.SMEM)] + [vmem] * (shares + 4),
        out_specs=[vmem] * 2,
        out_shape=[jax.ShapeDtypeStruct((shares // 2, 2, rows, LANES), jnp.bfloat16)] * 2,
        scratch_shapes=[columns, pltpu.VMEM((4, block, LANES), jnp.bfloat16), columns, columns],
        compiler_params=pltpu.CompilerParams(vmem_limit_bytes=24 << 20),
        cost_estimate=pl.CostEstimate(flops=50 * block * block * LANES, bytes_accessed=8 * block * block, transcendentals=0),
        name="convolve",
    )(
        me, *data, rounded(np.cos(angle)), rounded(np.sin(angle)),
        jnp.asarray(np.cos(turn).astype(np.float32)), jnp.asarray(np.sin(turn).astype(np.float32)),
    )


def gate_kernel(chips, me_ref, *refs):
    held, gate_ref, outs, conv_ref = refs[:chips], refs[chips], refs[chips + 1:-1], refs[-1]
    _, span, block_rows, _ = held[0].shape
    rows = span * block_rows
    for flip, ref in enumerate(held):
        for core in range(2):
            share = me_ref[0] ^ (2 * flip + core)
            conv_ref[:, pl.ds(pl.multiple_of(share * LANES, LANES), LANES)] = ref[core].reshape(rows, LANES)
    conv = jnp.dot(join_rows(rows, span), conv_ref[...], preferred_element_type=jnp.float32)
    gated = (conv * gate_ref[...].astype(jnp.float32)).astype(jnp.bfloat16)
    part = rows // len(outs)
    for p, out_ref in enumerate(outs):
        out_ref[...] = gated[p * part:(p + 1) * part]


def gate(me, held, gate_out, parts):
    rows, width = gate_out.shape
    vmem = pl.BlockSpec(memory_space=pltpu.VMEM)
    return pl.pallas_call(
        functools.partial(gate_kernel, len(held)),
        in_specs=[pl.BlockSpec(memory_space=pltpu.SMEM)] + [vmem] * (len(held) + 1),
        out_specs=[vmem] * parts,
        out_shape=[jax.ShapeDtypeStruct((rows // parts, width), jnp.bfloat16)] * parts,
        scratch_shapes=[pltpu.VMEM((rows, width), jnp.bfloat16)],
        compiler_params=pltpu.CompilerParams(vmem_limit_bytes=16 << 20),
        name="gate",
    )(me, *held, gate_out)


def own_kernel(me_ref, *refs):
    parts = (len(refs) - 1) // 2
    gated, slabs, out_ref = refs[:parts], refs[parts:-1], refs[-1]
    rows, depth = gated[0].shape[0], slabs[0].shape[0]
    for p, gated_ref in enumerate(gated):
        out_ref[0, p * rows:(p + 1) * rows] = sum(
            jnp.dot(gated_ref[:, i * depth:(i + 1) * depth], slab[...], preferred_element_type=jnp.float32)
            for i, slab in enumerate(slabs)
        )


def own_part(me, gated, weight, blocks):
    parts = len(gated)
    part_rows, depth = gated[0].shape
    cols = weight.shape[1] // 8

    def column(slab, i, me_ref):
        flip = sum((jnp.where(i == place, f, 0) for place, (f, _) in enumerate(blocks)), 0)
        half = sum((jnp.where(i == place, h, 0) for place, (_, h) in enumerate(blocks)), 0)
        return slab, (me_ref[0] ^ flip) * 2 + half

    return pl.pallas_call(
        own_kernel,
        grid_spec=pltpu.PrefetchScalarGridSpec(
            num_scalar_prefetch=1,
            grid=(len(blocks),),
            in_specs=[pl.BlockSpec((part_rows, depth), lambda i, m: (0, 0))] * parts
            + [pl.BlockSpec((depth // parts, cols), functools.partial(column, slab)) for slab in range(parts)],
            out_specs=pl.BlockSpec((1, parts * part_rows, cols), lambda i, m: (i, 0, 0)),
        ),
        out_shape=jax.ShapeDtypeStruct((len(blocks), parts * part_rows, cols), jnp.float32),
        compiler_params=pltpu.CompilerParams(vmem_limit_bytes=40 << 20),
        cost_estimate=pl.CostEstimate(
            flops=2 * parts * part_rows * depth * cols * len(blocks),
            bytes_accessed=2 * depth * cols * len(blocks), transcendentals=0,
        ),
        name="own_part",
    )(me, *gated, *[weight] * parts)


def add_kernel(parts, kept, core_ref, own_ref, *refs):
    moved, refs = refs[:2 * parts], refs[2 * parts:]
    weights, (a_ref, b_ref, held_ref, sems) = refs[:4], refs[4:]
    slabs = sems.shape[1]
    depth = held_ref.shape[1] // slabs

    def copies(side, take_mine):
        source = weights[2 * side] if take_mine else weights[2 * side + 1]
        return [
            pltpu.make_async_copy(
                source.at[i * depth:(i + 1) * depth], held_ref.at[side, i * depth:(i + 1) * depth], sems.at[side, i]
            )
            for i in range(slabs)
        ]

    mine_core = 0 if kept else 1
    for side in range(2):

        @pl.when(core_ref[0] == mine_core)
        def _():
            for copy in copies(side, True):
                copy.start()

        @pl.when(core_ref[0] != mine_core)
        def _():
            for copy in copies(side, False):
                copy.start()

    rows = moved[0].shape[0]
    for side, out_ref in enumerate((a_ref, b_ref)):
        for i, copy in enumerate(copies(side, True)):
            copy.wait()
        for p in range(parts):
            at = slice(p * rows, (p + 1) * rows)
            total = own_ref[side, at] + jnp.dot(
                moved[side * parts + p][...], held_ref[side], preferred_element_type=jnp.float32
            )
            out_ref[at] = total.astype(out_ref.dtype)


def add_moved(core, own, moved_x, moved_y, weights, first, kept, dtype):
    parts = len(moved_x)
    rows, depth = moved_x[0].shape
    cols = own.shape[2]
    whole = pl.BlockSpec((rows, depth), lambda i: (0, 0))
    shape = jax.ShapeDtypeStruct((parts * rows, cols), dtype)
    out = pl.BlockSpec((parts * rows, cols), lambda i: (0, 0))
    return pl.pallas_call(
        functools.partial(add_kernel, parts, kept),
        grid=(1,),
        in_specs=[
            pl.BlockSpec(memory_space=pltpu.SMEM),
            pl.BlockSpec((2, parts * rows, cols), lambda i: (0, first, 0)),
        ]
        + [whole] * (2 * parts)
        + [pl.BlockSpec(memory_space=pl.ANY)] * 4,
        out_specs=[out, out],
        out_shape=[shape, shape],
        scratch_shapes=[pltpu.VMEM((2, depth, cols), jnp.bfloat16), pltpu.SemaphoreType.DMA((2, 4))],
        compiler_params=pltpu.CompilerParams(vmem_limit_bytes=40 << 20),
        cost_estimate=pl.CostEstimate(
            flops=4 * parts * rows * depth * cols, bytes_accessed=4 * depth * cols, transcendentals=0
        ),
        name="add_kept" if kept else "add_sent",
    )(core, own, *moved_x, *moved_y, *weights)


def swap(data, axis, flip):
    return lax.ppermute(data, axis, [(i, i ^ flip) for i in range(lax.axis_size(axis))])


def by_channels(values, gate_in, gate_out, spectrum, out_weight):
    seq_count = lax.axis_size("seq")
    here = lax.axis_index("seq").astype(jnp.int32)
    me = lax.axis_index("chan").astype(jnp.int32)
    core = here % 2
    parts = 2

    order = tuple(sorted(range(seq_count), key=lambda m: (m == 0, m == 1, m % 2, -m)))
    packed = list(pack(here.reshape(1), values, gate_in, spectrum, seq_count))
    places = jnp.stack([(me ^ (1 + 2 * core)) * 2, (me ^ (2 + core)) * 2 + 1])
    _, places = lax.optimization_barrier((packed, places))
    block_x, block_y = take_blocks(places, out_weight)
    late = [m for m in order if m % 2]
    weight_x, weight_y = swap(block_x, "chan", 1), swap(block_y, "chan", 2)
    data = {m: swap(packed[m], "seq", m) if m else packed[m] for m in order if m % 2 == 0}
    held, data[order[0]] = lax.optimization_barrier(([packed[m] for m in late], data[order[0]]))
    data.update({m: swap(mine, "seq", m) for m, mine in zip(late, held)})
    mine, other = convolve(here.reshape(1), [data[m] for m in order], order)
    other = swap(other, "seq", 1)
    held = [jnp.stack([mine[flip], other[flip]]) for flip in range(seq_count // 2)]
    held = [swap(both, "seq", 2 * flip) if flip else both for flip, both in enumerate(held)]
    gated = gate(here.reshape(1), held, gate_out, parts)
    weight_x, weight_y, _ = lax.optimization_barrier((weight_x, weight_y, gated))
    weights = [weight_x, swap(weight_x, "seq", 1), weight_y, swap(weight_y, "seq", 1)]
    own = own_part(me.reshape(1), gated, out_weight, ((2, 0), (1, 1)))
    core = core.reshape(1)
    moved_x, moved_y = [], []
    for p in range(parts):
        mine = gated[p]
        if p:
            mine, own, weights[1] = lax.optimization_barrier((mine, own, weights[1]))
        moved_x.append(swap(mine, "chan", 1))
        moved_y.append(swap(mine, "chan", 2))
    sums_a, sums_b = [], []
    for p in range(parts):
        if p == parts - 1:
            own_kept = own_part(me.reshape(1), gated, out_weight, ((0, 0), (0, 1)))
            own, own_kept = lax.optimization_barrier((own, own_kept))
        sent = add_moved(core, own, moved_x[p:p + 1], moved_y[p:p + 1], weights, p, False, jnp.bfloat16)
        sums_a.append(swap(sent[0], "chan", 2))
        sums_b.append(swap(sent[1], "chan", 1))
    kept_a, kept_b = add_moved(core, own_kept, moved_x, moved_y, weights, 0, True, jnp.float32)
    sums = jnp.concatenate([jnp.concatenate(sums_a, axis=0), jnp.concatenate(sums_b, axis=0)], axis=1)
    return (jnp.concatenate([kept_a, kept_b], axis=1) + sums.astype(jnp.float32)).astype(jnp.bfloat16)


def to_columns(data):
    return lax.all_to_all(data, "seq", split_axis=2, concat_axis=1, tiled=True)


def to_rows(data):
    return lax.all_to_all(data, "seq", split_axis=1, concat_axis=2, tiled=True)


def by_frequencies(values, gate_in, gate_out, spectrum, out_weight):
    seq_count = lax.axis_size("seq")
    seq_index = lax.axis_index("seq")
    tok_rows, chan_width = values.shape
    block_rows = BLOCK // seq_count
    span = tok_rows // block_rows
    tokens_all = BLOCK * span
    col_share = span * chan_width // seq_count
    block_cos = rounded(np.cos(angles(BLOCK, BLOCK, BLOCK)))
    block_sin = rounded(np.sin(angles(BLOCK, BLOCK, BLOCK)))
    span_cos = rounded(np.cos(angles(span, span, span)))
    span_sin = rounded(np.sin(angles(span, span, span)))
    turn_all = angles(BLOCK, span, tokens_all)
    turn_cos_all = jnp.asarray(np.cos(turn_all).astype(np.float32))
    turn_sin_all = jnp.asarray(np.sin(turn_all).astype(np.float32))
    source = (values.astype(jnp.float32) * gate_in.astype(jnp.float32)).astype(jnp.bfloat16)
    spread = to_columns(source.reshape(1, block_rows, seq_count, col_share))
    columns = spread.reshape(BLOCK, col_share)
    cos_part = jnp.dot(jnp.transpose(block_cos), columns, preferred_element_type=jnp.float32)
    sin_part = jnp.dot(jnp.transpose(block_sin), columns, preferred_element_type=jnp.float32)
    col_pos = (seq_index * col_share + jnp.arange(col_share, dtype=jnp.int32)) // chan_width
    turn_cos = jnp.take(turn_cos_all, col_pos, axis=1)
    turn_sin = jnp.take(turn_sin_all, col_pos, axis=1)
    twist_re = cos_part * turn_cos - sin_part * turn_sin
    twist_im = -sin_part * turn_cos - cos_part * turn_sin
    twisted = jnp.stack([twist_re, twist_im]).astype(jnp.bfloat16)
    arranged = to_rows(twisted).reshape(2, block_rows, span, chan_width)
    with_cos = jnp.einsum("bd,kcbh->kdch", span_cos, arranged, preferred_element_type=jnp.float32)
    with_sin = jnp.einsum("bd,kcbh->kdch", span_sin, arranged, preferred_element_type=jnp.float32)
    freq_re = with_cos[0] + with_sin[1]
    freq_im = with_cos[1] - with_sin[0]
    prod_re = freq_re * spectrum[0] - freq_im * spectrum[1]
    prod_im = freq_re * spectrum[1] + freq_im * spectrum[0]
    product = jnp.stack([prod_re, prod_im]).astype(jnp.bfloat16)
    back_cos = jnp.einsum("db,kdch->kcbh", span_cos, product, preferred_element_type=jnp.float32)
    back_sin = jnp.einsum("db,kdch->kcbh", span_sin, product, preferred_element_type=jnp.float32)
    back_re = (back_cos[0] - back_sin[1]) / span
    back_im = (back_cos[1] + back_sin[0]) / span
    back_tc = lax.dynamic_slice_in_dim(turn_cos_all, seq_index * block_rows, block_rows)[:, :, None]
    back_ts = lax.dynamic_slice_in_dim(turn_sin_all, seq_index * block_rows, block_rows)[:, :, None]
    rotated = jnp.stack(
        [back_re * back_tc - back_im * back_ts, back_im * back_tc + back_re * back_ts]
    ).astype(jnp.bfloat16)
    gathered = to_columns(rotated.reshape(2, block_rows, seq_count, col_share)).reshape(2, BLOCK, col_share)
    summed = jnp.dot(block_cos, gathered[0], preferred_element_type=jnp.float32)
    summed = summed - jnp.dot(block_sin, gathered[1], preferred_element_type=jnp.float32)
    ordered = (summed / BLOCK).astype(jnp.bfloat16).reshape(1, BLOCK, col_share)
    conv = to_rows(ordered).reshape(tok_rows, chan_width)
    gated = (conv.astype(jnp.float32) * gate_out.astype(jnp.float32)).astype(jnp.bfloat16)
    partial_sum = jnp.dot(gated, out_weight, preferred_element_type=jnp.float32)
    return lax.psum_scatter(partial_sum.astype(jnp.bfloat16), "chan", scatter_dimension=1, tiled=True)


def shards(values, gate_in, gate_out, spectrum, out_weight):
    seq_count, chan_count = lax.axis_size("seq"), lax.axis_size("chan")
    _, span, block_rows, width = spectrum.shape
    one_lane_block = width == seq_count * LANES and block_rows % 32 == 0
    if span == 2 and chan_count == 4 and seq_count & (seq_count - 1) == 0 and one_lane_block:
        return by_channels(values, gate_in, gate_out, spectrum, out_weight)
    return by_frequencies(values, gate_in, gate_out, spectrum, out_weight)


def solution(mesh):
    placed = (
        P("seq", "chan"),
        P("seq", "chan"),
        P("seq", "chan"),
        P(None, None, "seq", "chan"),
        P("chan", None),
    )
    return jax.shard_map(
        shards, mesh=mesh, in_specs=placed, out_specs=P("seq", "chan"), check_vma=False
    )
```

```python
import functools
import math

import jax
import jax.numpy as jnp
import ml_dtypes
import numpy as np
from jax import lax
from jax.experimental import pallas as pl
from jax.experimental.pallas import tpu as pltpu
from jax.sharding import PartitionSpec as P

BLOCK = 1024
LANES = 128


def angles(first, second, period):
    return (np.arange(first)[:, None] * np.arange(second)[None, :] % period) * (2.0 * math.pi / period)


def rounded(table):
    return jnp.asarray(table.astype(np.float32).astype(ml_dtypes.bfloat16))


def split_rows(rows, span):
    out = lax.broadcasted_iota(jnp.int32, (rows, rows), 0)
    token = lax.broadcasted_iota(jnp.int32, (rows, rows), 1)
    block_rows = rows // span
    return jnp.where(token == (out % block_rows) * span + out // block_rows, 1.0, 0.0).astype(jnp.bfloat16)


def join_rows(rows, span):
    token = lax.broadcasted_iota(jnp.int32, (rows, rows), 0)
    held = lax.broadcasted_iota(jnp.int32, (rows, rows), 1)
    block_rows = rows // span
    return jnp.where(token == (held % block_rows) * span + held // block_rows, 1.0, 0.0).astype(jnp.bfloat16)


def pack_kernel(span, me_ref, values_hbm, gate_hbm, spectrum_hbm, *refs):
    outs, (values_ref, gate_ref, spectrum_ref, sems) = refs[:-4], refs[-4:]
    copies = [
        pltpu.make_async_copy(values_hbm, values_ref, sems.at[0]),
        pltpu.make_async_copy(gate_hbm, gate_ref, sems.at[1]),
    ]
    for part in range(2):
        for d in range(span):
            copies.append(pltpu.make_async_copy(
                spectrum_hbm.at[part, d], spectrum_ref.at[part * span + d], sems.at[2 + part * span + d]
            ))
    for copy in copies:
        copy.start()
    me = me_ref[0]
    rows = values_ref.shape[0]
    block_rows = rows // span
    copies[0].wait()
    copies[1].wait()
    source = (values_ref[...].astype(jnp.float32) * gate_ref[...].astype(jnp.float32)).astype(jnp.bfloat16)
    values_ref[...] = jnp.dot(
        split_rows(rows, span), source, preferred_element_type=jnp.float32
    ).astype(jnp.bfloat16)

    def lanes_of(m):
        return pl.ds(pl.multiple_of((me ^ m) * LANES, LANES), LANES)

    for m, out_ref in enumerate(outs):
        for b in range(span):
            out_ref[2 * span + b] = values_ref[b * block_rows:(b + 1) * block_rows, lanes_of(m)]
    for part in range(2 * span):
        copies[2 + part].wait()
        for m, out_ref in enumerate(outs):
            out_ref[part] = spectrum_ref[part, :, lanes_of(m)].astype(jnp.bfloat16)


def pack(me, values, gate_in, spectrum, shares):
    rows, width = values.shape
    _, span, block_rows, _ = spectrum.shape
    shape = (3 * span, block_rows, LANES)
    vmem, hbm = pl.BlockSpec(memory_space=pltpu.VMEM), pl.BlockSpec(memory_space=pltpu.HBM)
    return pl.pallas_call(
        functools.partial(pack_kernel, span),
        in_specs=[pl.BlockSpec(memory_space=pltpu.SMEM), hbm, hbm, hbm],
        out_specs=[vmem] * shares,
        out_shape=[jax.ShapeDtypeStruct(shape, jnp.bfloat16)] * shares,
        scratch_shapes=[
            pltpu.VMEM((rows, width), jnp.bfloat16),
            pltpu.VMEM((rows, width), jnp.bfloat16),
            pltpu.VMEM((2 * span, block_rows, width), jnp.float32),
            pltpu.SemaphoreType.DMA((2 + 2 * span,)),
        ],
        compiler_params=pltpu.CompilerParams(vmem_limit_bytes=60 << 20),
        name="pack",
    )(me, values, gate_in, spectrum)


def take_kernel(places_ref, weight_hbm, *refs):
    outs, sems = refs[:-1], refs[-1]
    slabs = sems.shape[1]
    depth, cols = outs[0].shape[0] // slabs, outs[0].shape[1]
    copies = [
        pltpu.make_async_copy(
            weight_hbm.at[i * depth:(i + 1) * depth, pl.ds(pl.multiple_of(places_ref[k] * cols, cols), cols)],
            out_ref.at[i * depth:(i + 1) * depth],
            sems.at[k, i],
        )
        for k, out_ref in enumerate(outs)
        for i in range(slabs)
    ]
    for copy in copies:
        copy.start()
    for copy in copies:
        copy.wait()


def take_blocks(places, weight):
    depth, cols = weight.shape[0], weight.shape[1] // 8
    count, slabs = places.shape[0], 4
    return pl.pallas_call(
        take_kernel,
        in_specs=[pl.BlockSpec(memory_space=pltpu.SMEM), pl.BlockSpec(memory_space=pltpu.HBM)],
        out_specs=[pl.BlockSpec(memory_space=pltpu.VMEM)] * count,
        out_shape=[jax.ShapeDtypeStruct((depth, cols), weight.dtype)] * count,
        scratch_shapes=[pltpu.SemaphoreType.DMA((count, slabs))],
        compiler_params=pltpu.CompilerParams(vmem_limit_bytes=48 << 20),
        cost_estimate=pl.CostEstimate(flops=0, bytes_accessed=128 * depth * cols, transcendentals=0),
        name="take_blocks",
    )(places, weight)


def conv_kernel(order, me_ref, *refs):
    shares = len(order)
    data, (cos_ref, sin_ref, turn_cos_ref, turn_sin_ref) = refs[:shares], refs[shares:shares + 4]
    mine_ref, other_ref, cols_ref, filt_ref, re_ref, im_ref = refs[shares + 4:]
    me = me_ref[0]
    chip, core = me // 2, me % 2
    rows = data[0].shape[1]
    for m, ref in zip(order, data):
        at = pl.ds(pl.multiple_of((me ^ m) * rows, rows), rows)
        for b in range(2):
            cols_ref[at, b * LANES:(b + 1) * LANES] = ref[4 + b]
        for part in range(4):
            filt_ref[part, at, :] = ref[part]
    step = 2 * rows
    for i in range(shares * rows // step):
        at = slice(i * step, (i + 1) * step)
        first_re = jnp.dot(cos_ref[at, :], cols_ref[...], preferred_element_type=jnp.float32)
        first_sin = jnp.dot(sin_ref[at, :], cols_ref[...], preferred_element_type=jnp.float32)
        tc, ts = turn_cos_ref[at, :], turn_sin_ref[at, :]
        re0, im0 = first_re[:, :LANES], -first_sin[:, :LANES]
        re1, im1 = first_re[:, LANES:], -first_sin[:, LANES:]
        re1, im1 = re1 * tc + im1 * ts, im1 * tc - re1 * ts
        f0r, f0i, f1r, f1i = re0 + re1, im0 + im1, re0 - re1, im0 - im1
        s0r, s1r, s0i, s1i = (filt_ref[part, at, :].astype(jnp.float32) for part in range(4))
        p0r, p0i = f0r * s0r - f0i * s0i, f0r * s0i + f0i * s0r
        p1r, p1i = f1r * s1r - f1i * s1i, f1r * s1i + f1i * s1r
        b0r, b0i = 0.5 * (p0r + p1r), 0.5 * (p0i + p1i)
        b1r, b1i = 0.5 * (p0r - p1r), 0.5 * (p0i - p1i)
        b1r, b1i = b1r * tc - b1i * ts, b1i * tc + b1r * ts
        re_ref[at, :] = jnp.concatenate([b0r, b1r], axis=1).astype(jnp.bfloat16)
        im_ref[at, :] = jnp.concatenate([b0i, b1i], axis=1).astype(jnp.bfloat16)
    scale = 1.0 / (shares * rows)
    for i in range(shares * rows // step):
        at = slice(i * step, (i + 1) * step)
        conv = jnp.dot(cos_ref[at, :], re_ref[...], preferred_element_type=jnp.float32)
        conv = conv - jnp.dot(sin_ref[at, :], im_ref[...], preferred_element_type=jnp.float32)
        conv = (conv * scale).astype(jnp.bfloat16)
        for b in range(2):
            lanes = slice(b * LANES, (b + 1) * LANES)
            low, high = conv[:rows, lanes], conv[rows:, lanes]
            mine_ref[i ^ chip, b] = jnp.where(core == 0, low, high)
            other_ref[i ^ chip, b] = jnp.where(core == 0, high, low)


def convolve(me, data, order):
    shares = len(data)
    rows = data[0].shape[1]
    block = shares * rows
    angle = angles(block, block, block)
    turn = np.broadcast_to(angles(block, 2, 2 * block)[:, 1:], (block, LANES))
    vmem = pl.BlockSpec(memory_space=pltpu.VMEM)
    columns = pltpu.VMEM((block, 2 * LANES), jnp.bfloat16)
    return pl.pallas_call(
        functools.partial(conv_kernel, order),
        in_specs=[pl.BlockSpec(memory_space=pltpu.SMEM)] + [vmem] * (shares + 4),
        out_specs=[vmem] * 2,
        out_shape=[jax.ShapeDtypeStruct((shares // 2, 2, rows, LANES), jnp.bfloat16)] * 2,
        scratch_shapes=[columns, pltpu.VMEM((4, block, LANES), jnp.bfloat16), columns, columns],
        compiler_params=pltpu.CompilerParams(vmem_limit_bytes=24 << 20),
        cost_estimate=pl.CostEstimate(flops=50 * block * block * LANES, bytes_accessed=8 * block * block, transcendentals=0),
        name="convolve",
    )(
        me, *data, rounded(np.cos(angle)), rounded(np.sin(angle)),
        jnp.asarray(np.cos(turn).astype(np.float32)), jnp.asarray(np.sin(turn).astype(np.float32)),
    )


def gate_kernel(chips, me_ref, *refs):
    held, (gate_ref, *outs, conv_ref) = refs[:len(chips)], refs[len(chips):]
    _, span, block_rows, _ = held[0].shape
    rows = span * block_rows
    for flip, ref in zip(chips, held):
        for core in range(2):
            share = me_ref[0] ^ (2 * flip + core)
            conv_ref[:, pl.ds(pl.multiple_of(share * LANES, LANES), LANES)] = ref[core].reshape(rows, LANES)
    conv = jnp.dot(join_rows(rows, span), conv_ref[...], preferred_element_type=jnp.float32)
    gated = (conv * gate_ref[...].astype(jnp.float32)).astype(jnp.bfloat16)
    part = rows // len(outs)
    for p, out_ref in enumerate(outs):
        out_ref[...] = gated[p * part:(p + 1) * part]


def gate(me, held, chips, gate_out, parts):
    rows, width = gate_out.shape
    vmem = pl.BlockSpec(memory_space=pltpu.VMEM)
    return pl.pallas_call(
        functools.partial(gate_kernel, chips),
        in_specs=[pl.BlockSpec(memory_space=pltpu.SMEM)] + [vmem] * (len(held) + 1),
        out_specs=[vmem] * parts,
        out_shape=[jax.ShapeDtypeStruct((rows // parts, width), jnp.bfloat16)] * parts,
        scratch_shapes=[pltpu.VMEM((rows, width), jnp.bfloat16)],
        compiler_params=pltpu.CompilerParams(vmem_limit_bytes=16 << 20),
        name="gate",
    )(me, *held, gate_out)


def own_kernel(me_ref, *refs):
    parts = (len(refs) - 1) // 2
    gated, slabs, out_ref = refs[:parts], refs[parts:-1], refs[-1]
    rows, depth = gated[0].shape[0], slabs[0].shape[0]
    for p, gated_ref in enumerate(gated):
        out_ref[0, p * rows:(p + 1) * rows] = sum(
            jnp.dot(gated_ref[:, i * depth:(i + 1) * depth], slab[...], preferred_element_type=jnp.float32)
            for i, slab in enumerate(slabs)
        )


def own_part(me, gated, weight, blocks):
    parts = len(gated)
    part_rows, depth = gated[0].shape
    cols = weight.shape[1] // 8

    def column(slab, i, me_ref):
        flip = sum((jnp.where(i == place, f, 0) for place, (f, _) in enumerate(blocks)), 0)
        half = sum((jnp.where(i == place, h, 0) for place, (_, h) in enumerate(blocks)), 0)
        return slab, (me_ref[0] ^ flip) * 2 + half

    return pl.pallas_call(
        own_kernel,
        grid_spec=pltpu.PrefetchScalarGridSpec(
            num_scalar_prefetch=1,
            grid=(len(blocks),),
            in_specs=[pl.BlockSpec((part_rows, depth), lambda i, m: (0, 0))] * parts
            + [pl.BlockSpec((depth // parts, cols), functools.partial(column, slab)) for slab in range(parts)],
            out_specs=pl.BlockSpec((1, parts * part_rows, cols), lambda i, m: (i, 0, 0)),
        ),
        out_shape=jax.ShapeDtypeStruct((len(blocks), parts * part_rows, cols), jnp.float32),
        compiler_params=pltpu.CompilerParams(vmem_limit_bytes=40 << 20),
        cost_estimate=pl.CostEstimate(
            flops=2 * parts * part_rows * depth * cols * len(blocks),
            bytes_accessed=2 * depth * cols * len(blocks), transcendentals=0,
        ),
        name="own_part",
    )(me, *gated, *[weight] * parts)


def add_kernel(parts, kept, core_ref, own_ref, *refs):
    moved, refs = refs[:2 * parts], refs[2 * parts:]
    weights, (a_ref, b_ref, held_ref, sems) = refs[:4], refs[4:]
    slabs = sems.shape[1]
    depth = held_ref.shape[1] // slabs

    def copies(side, take_mine):
        source = weights[2 * side] if take_mine else weights[2 * side + 1]
        return [
            pltpu.make_async_copy(
                source.at[i * depth:(i + 1) * depth], held_ref.at[side, i * depth:(i + 1) * depth], sems.at[side, i]
            )
            for i in range(slabs)
        ]

    mine_core = 0 if kept else 1
    for side in range(2):

        @pl.when(core_ref[0] == mine_core)
        def _():
            for copy in copies(side, True):
                copy.start()

        @pl.when(core_ref[0] != mine_core)
        def _():
            for copy in copies(side, False):
                copy.start()

    rows = moved[0].shape[0]
    for side, out_ref in enumerate((a_ref, b_ref)):
        for i, copy in enumerate(copies(side, True)):
            copy.wait()
        for p in range(parts):
            at = slice(p * rows, (p + 1) * rows)
            total = own_ref[side, at] + jnp.dot(
                moved[side * parts + p][...], held_ref[side], preferred_element_type=jnp.float32
            )
            out_ref[at] = total.astype(out_ref.dtype)


def add_moved(core, own, moved_x, moved_y, weights, first, kept, dtype):
    parts = len(moved_x)
    rows, depth = moved_x[0].shape
    cols = own.shape[2]
    whole = pl.BlockSpec((rows, depth), lambda i: (0, 0))
    shape = jax.ShapeDtypeStruct((parts * rows, cols), dtype)
    out = pl.BlockSpec((parts * rows, cols), lambda i: (0, 0))
    return pl.pallas_call(
        functools.partial(add_kernel, parts, kept),
        grid=(1,),
        in_specs=[
            pl.BlockSpec(memory_space=pltpu.SMEM),
            pl.BlockSpec((2, parts * rows, cols), lambda i: (0, first, 0)),
        ]
        + [whole] * (2 * parts)
        + [pl.BlockSpec(memory_space=pl.ANY)] * 4,
        out_specs=[out, out],
        out_shape=[shape, shape],
        scratch_shapes=[pltpu.VMEM((2, depth, cols), jnp.bfloat16), pltpu.SemaphoreType.DMA((2, 4))],
        compiler_params=pltpu.CompilerParams(vmem_limit_bytes=40 << 20),
        cost_estimate=pl.CostEstimate(
            flops=4 * parts * rows * depth * cols, bytes_accessed=4 * depth * cols, transcendentals=0
        ),
        name="add_kept" if kept else "add_sent",
    )(core, own, *moved_x, *moved_y, *weights)


def finish_kernel(kept_a_ref, kept_b_ref, sum_a_ref, sum_b_ref, *refs):
    out_ref = refs[-1]
    cols = kept_a_ref.shape[1]
    out_ref[:, :cols] = (kept_a_ref[...] + sum_a_ref[...].astype(jnp.float32)).astype(out_ref.dtype)
    out_ref[:, cols:] = (kept_b_ref[...] + sum_b_ref[...].astype(jnp.float32)).astype(out_ref.dtype)


def finish(kept_a, kept_b, sum_a, sum_b, part, before):
    rows, cols = sum_a.shape
    total = kept_a.shape[0]
    kept = pl.BlockSpec((rows, cols), lambda i: (part, 0))
    sums = pl.BlockSpec((rows, cols), lambda i: (0, 0))
    earlier = [] if before is None else [before]
    return pl.pallas_call(
        finish_kernel,
        grid=(1,),
        in_specs=[kept, kept, sums, sums] + [pl.BlockSpec(memory_space=pl.ANY)] * len(earlier),
        out_specs=pl.BlockSpec((rows, 2 * cols), lambda i: (part, 0)),
        out_shape=jax.ShapeDtypeStruct((total, 2 * cols), jnp.bfloat16),
        input_output_aliases={4: 0} if earlier else {},
        compiler_params=pltpu.CompilerParams(vmem_limit_bytes=16 << 20),
        name="finish",
    )(kept_a, kept_b, sum_a, sum_b, *earlier)


def swap(data, axis, flip):
    return lax.ppermute(data, axis, [(i, i ^ flip) for i in range(lax.axis_size(axis))])


def by_channels(values, gate_in, gate_out, spectrum, out_weight):
    seq_count = lax.axis_size("seq")
    here = lax.axis_index("seq").astype(jnp.int32)
    me = lax.axis_index("chan").astype(jnp.int32)
    core = here % 2
    parts = 2

    order = tuple(sorted(range(seq_count), key=lambda m: (m == 0, m == 1, m % 2, -m)))
    packed = list(pack(here.reshape(1), values, gate_in, spectrum, seq_count))
    places = jnp.stack([(me ^ (1 + 2 * core)) * 2, (me ^ (2 + core)) * 2 + 1])
    _, places = lax.optimization_barrier((packed, places))
    block_x, block_y = take_blocks(places, out_weight)
    late = [m for m in order if m % 2]
    weight_x, weight_y = swap(block_x, "chan", 1), swap(block_y, "chan", 2)
    data = {m: swap(packed[m], "seq", m) if m else packed[m] for m in order if m % 2 == 0}
    held, data[order[0]] = lax.optimization_barrier(([packed[m] for m in late], data[order[0]]))
    data.update({m: swap(mine, "seq", m) for m, mine in zip(late, held)})
    mine, other = convolve(here.reshape(1), [data[m] for m in order], order)
    other = swap(other, "seq", 1)
    held = [jnp.stack([mine[flip], other[flip]]) for flip in range(seq_count // 2)]
    chips = tuple(reversed(range(seq_count // 2)))
    held = [swap(held[flip], "seq", 2 * flip) if flip else held[flip] for flip in chips]
    gated = gate(here.reshape(1), held, chips, gate_out, parts)
    weight_x, weight_y, _ = lax.optimization_barrier((weight_x, weight_y, gated))
    weights = [weight_x, swap(weight_x, "seq", 1), weight_y, swap(weight_y, "seq", 1)]
    own = own_part(me.reshape(1), gated, out_weight, ((2, 0), (1, 1)))
    core = core.reshape(1)
    moved_x, moved_y = [], []
    for p in range(parts):
        mine = gated[p]
        if p:
            mine, own, weights[1] = lax.optimization_barrier((mine, own, weights[1]))
        moved_x.append(swap(mine, "chan", 1))
        moved_y.append(swap(mine, "chan", 2))
    sums_a, sums_b = [], []
    for p in range(parts):
        if p == parts - 1:
            own_kept = own_part(me.reshape(1), gated, out_weight, ((0, 0), (0, 1)))
            own, own_kept = lax.optimization_barrier((own, own_kept))
        sent = add_moved(core, own, moved_x[p:p + 1], moved_y[p:p + 1], weights, p, False, jnp.bfloat16)
        sums_a.append(swap(sent[0], "chan", 2))
        sums_b.append(swap(sent[1], "chan", 1))
    kept_a, kept_b = add_moved(core, own_kept, moved_x, moved_y, weights, 0, True, jnp.float32)
    mixed = None
    for p in range(parts):
        mixed = finish(kept_a, kept_b, sums_a[p], sums_b[p], p, mixed)
    return mixed


def to_columns(data):
    return lax.all_to_all(data, "seq", split_axis=2, concat_axis=1, tiled=True)


def to_rows(data):
    return lax.all_to_all(data, "seq", split_axis=1, concat_axis=2, tiled=True)


def by_frequencies(values, gate_in, gate_out, spectrum, out_weight):
    seq_count = lax.axis_size("seq")
    seq_index = lax.axis_index("seq")
    tok_rows, chan_width = values.shape
    block_rows = BLOCK // seq_count
    span = tok_rows // block_rows
    tokens_all = BLOCK * span
    col_share = span * chan_width // seq_count
    block_cos = rounded(np.cos(angles(BLOCK, BLOCK, BLOCK)))
    block_sin = rounded(np.sin(angles(BLOCK, BLOCK, BLOCK)))
    span_cos = rounded(np.cos(angles(span, span, span)))
    span_sin = rounded(np.sin(angles(span, span, span)))
    turn_all = angles(BLOCK, span, tokens_all)
    turn_cos_all = jnp.asarray(np.cos(turn_all).astype(np.float32))
    turn_sin_all = jnp.asarray(np.sin(turn_all).astype(np.float32))
    source = (values.astype(jnp.float32) * gate_in.astype(jnp.float32)).astype(jnp.bfloat16)
    spread = to_columns(source.reshape(1, block_rows, seq_count, col_share))
    columns = spread.reshape(BLOCK, col_share)
    cos_part = jnp.dot(jnp.transpose(block_cos), columns, preferred_element_type=jnp.float32)
    sin_part = jnp.dot(jnp.transpose(block_sin), columns, preferred_element_type=jnp.float32)
    col_pos = (seq_index * col_share + jnp.arange(col_share, dtype=jnp.int32)) // chan_width
    turn_cos = jnp.take(turn_cos_all, col_pos, axis=1)
    turn_sin = jnp.take(turn_sin_all, col_pos, axis=1)
    twist_re = cos_part * turn_cos - sin_part * turn_sin
    twist_im = -sin_part * turn_cos - cos_part * turn_sin
    twisted = jnp.stack([twist_re, twist_im]).astype(jnp.bfloat16)
    arranged = to_rows(twisted).reshape(2, block_rows, span, chan_width)
    with_cos = jnp.einsum("bd,kcbh->kdch", span_cos, arranged, preferred_element_type=jnp.float32)
    with_sin = jnp.einsum("bd,kcbh->kdch", span_sin, arranged, preferred_element_type=jnp.float32)
    freq_re = with_cos[0] + with_sin[1]
    freq_im = with_cos[1] - with_sin[0]
    prod_re = freq_re * spectrum[0] - freq_im * spectrum[1]
    prod_im = freq_re * spectrum[1] + freq_im * spectrum[0]
    product = jnp.stack([prod_re, prod_im]).astype(jnp.bfloat16)
    back_cos = jnp.einsum("db,kdch->kcbh", span_cos, product, preferred_element_type=jnp.float32)
    back_sin = jnp.einsum("db,kdch->kcbh", span_sin, product, preferred_element_type=jnp.float32)
    back_re = (back_cos[0] - back_sin[1]) / span
    back_im = (back_cos[1] + back_sin[0]) / span
    back_tc = lax.dynamic_slice_in_dim(turn_cos_all, seq_index * block_rows, block_rows)[:, :, None]
    back_ts = lax.dynamic_slice_in_dim(turn_sin_all, seq_index * block_rows, block_rows)[:, :, None]
    rotated = jnp.stack(
        [back_re * back_tc - back_im * back_ts, back_im * back_tc + back_re * back_ts]
    ).astype(jnp.bfloat16)
    gathered = to_columns(rotated.reshape(2, block_rows, seq_count, col_share)).reshape(2, BLOCK, col_share)
    summed = jnp.dot(block_cos, gathered[0], preferred_element_type=jnp.float32)
    summed = summed - jnp.dot(block_sin, gathered[1], preferred_element_type=jnp.float32)
    ordered = (summed / BLOCK).astype(jnp.bfloat16).reshape(1, BLOCK, col_share)
    conv = to_rows(ordered).reshape(tok_rows, chan_width)
    gated = (conv.astype(jnp.float32) * gate_out.astype(jnp.float32)).astype(jnp.bfloat16)
    partial_sum = jnp.dot(gated, out_weight, preferred_element_type=jnp.float32)
    return lax.psum_scatter(partial_sum.astype(jnp.bfloat16), "chan", scatter_dimension=1, tiled=True)


def shards(values, gate_in, gate_out, spectrum, out_weight):
    seq_count, chan_count = lax.axis_size("seq"), lax.axis_size("chan")
    _, span, block_rows, width = spectrum.shape
    one_lane_block = width == seq_count * LANES and block_rows % 32 == 0
    if span == 2 and chan_count == 4 and seq_count & (seq_count - 1) == 0 and one_lane_block:
        return by_channels(values, gate_in, gate_out, spectrum, out_weight)
    return by_frequencies(values, gate_in, gate_out, spectrum, out_weight)


def solution(mesh):
    placed = (
        P("seq", "chan"),
        P("seq", "chan"),
        P("seq", "chan"),
        P(None, None, "seq", "chan"),
        P("chan", None),
    )
    return jax.shard_map(
        shards, mesh=mesh, in_specs=placed, out_specs=P("seq", "chan"), check_vma=False
    )
```

```python
import functools
import math

import jax
import jax.numpy as jnp
import ml_dtypes
import numpy as np
from jax import lax
from jax.experimental import pallas as pl
from jax.experimental.pallas import tpu as pltpu
from jax.sharding import PartitionSpec as P

BLOCK = 1024
LANES = 128


def angles(first, second, period):
    return (np.arange(first)[:, None] * np.arange(second)[None, :] % period) * (2.0 * math.pi / period)


def rounded(table):
    return jnp.asarray(table.astype(np.float32).astype(ml_dtypes.bfloat16))


def split_rows(rows, span):
    out = lax.broadcasted_iota(jnp.int32, (rows, rows), 0)
    token = lax.broadcasted_iota(jnp.int32, (rows, rows), 1)
    block_rows = rows // span
    return jnp.where(token == (out % block_rows) * span + out // block_rows, 1.0, 0.0).astype(jnp.bfloat16)


def join_rows(rows, span):
    token = lax.broadcasted_iota(jnp.int32, (rows, rows), 0)
    held = lax.broadcasted_iota(jnp.int32, (rows, rows), 1)
    block_rows = rows // span
    return jnp.where(token == (held % block_rows) * span + held // block_rows, 1.0, 0.0).astype(jnp.bfloat16)


def pack_kernel(span, me_ref, values_hbm, gate_hbm, spectrum_hbm, *refs):
    outs, (values_ref, gate_ref, spectrum_ref, sems) = refs[:-4], refs[-4:]
    copies = [
        pltpu.make_async_copy(values_hbm, values_ref, sems.at[0]),
        pltpu.make_async_copy(gate_hbm, gate_ref, sems.at[1]),
    ]
    for part in range(2):
        for d in range(span):
            copies.append(pltpu.make_async_copy(
                spectrum_hbm.at[part, d], spectrum_ref.at[part * span + d], sems.at[2 + part * span + d]
            ))
    for copy in copies:
        copy.start()
    me = me_ref[0]
    rows = values_ref.shape[0]
    block_rows = rows // span
    copies[0].wait()
    copies[1].wait()
    source = (values_ref[...].astype(jnp.float32) * gate_ref[...].astype(jnp.float32)).astype(jnp.bfloat16)
    values_ref[...] = jnp.dot(
        split_rows(rows, span), source, preferred_element_type=jnp.float32
    ).astype(jnp.bfloat16)

    def lanes_of(m):
        return pl.ds(pl.multiple_of((me ^ m) * LANES, LANES), LANES)

    for m, out_ref in enumerate(outs):
        for b in range(span):
            out_ref[2 * span + b] = values_ref[b * block_rows:(b + 1) * block_rows, lanes_of(m)]
    for part in range(2 * span):
        copies[2 + part].wait()
        for m, out_ref in enumerate(outs):
            out_ref[part] = spectrum_ref[part, :, lanes_of(m)].astype(jnp.bfloat16)


def pack(me, values, gate_in, spectrum, shares):
    rows, width = values.shape
    _, span, block_rows, _ = spectrum.shape
    shape = (3 * span, block_rows, LANES)
    vmem, hbm = pl.BlockSpec(memory_space=pltpu.VMEM), pl.BlockSpec(memory_space=pltpu.HBM)
    return pl.pallas_call(
        functools.partial(pack_kernel, span),
        in_specs=[pl.BlockSpec(memory_space=pltpu.SMEM), hbm, hbm, hbm],
        out_specs=[vmem] * shares,
        out_shape=[jax.ShapeDtypeStruct(shape, jnp.bfloat16)] * shares,
        scratch_shapes=[
            pltpu.VMEM((rows, width), jnp.bfloat16),
            pltpu.VMEM((rows, width), jnp.bfloat16),
            pltpu.VMEM((2 * span, block_rows, width), jnp.float32),
            pltpu.SemaphoreType.DMA((2 + 2 * span,)),
        ],
        compiler_params=pltpu.CompilerParams(vmem_limit_bytes=60 << 20),
        name="pack",
    )(me, values, gate_in, spectrum)


def take_kernel(places_ref, weight_hbm, *refs):
    outs, sems = refs[:-1], refs[-1]
    slabs = sems.shape[1]
    depth, cols = outs[0].shape[0] // slabs, outs[0].shape[1]
    copies = [
        pltpu.make_async_copy(
            weight_hbm.at[i * depth:(i + 1) * depth, pl.ds(pl.multiple_of(places_ref[k] * cols, cols), cols)],
            out_ref.at[i * depth:(i + 1) * depth],
            sems.at[k, i],
        )
        for k, out_ref in enumerate(outs)
        for i in range(slabs)
    ]
    for copy in copies:
        copy.start()
    for copy in copies:
        copy.wait()


def take_blocks(places, weight):
    depth, cols = weight.shape[0], weight.shape[1] // 8
    count, slabs = places.shape[0], 4
    return pl.pallas_call(
        take_kernel,
        in_specs=[pl.BlockSpec(memory_space=pltpu.SMEM), pl.BlockSpec(memory_space=pltpu.HBM)],
        out_specs=[pl.BlockSpec(memory_space=pltpu.VMEM)] * count,
        out_shape=[jax.ShapeDtypeStruct((depth, cols), weight.dtype)] * count,
        scratch_shapes=[pltpu.SemaphoreType.DMA((count, slabs))],
        compiler_params=pltpu.CompilerParams(vmem_limit_bytes=48 << 20),
        cost_estimate=pl.CostEstimate(flops=0, bytes_accessed=128 * depth * cols, transcendentals=0),
        name="take_blocks",
    )(places, weight)


def conv_kernel(order, me_ref, *refs):
    shares = len(order)
    data, (cos_ref, sin_ref, turn_cos_ref, turn_sin_ref) = refs[:shares], refs[shares:shares + 4]
    other_ref, re_ref, im_ref, cols_ref, filt_ref = refs[shares + 4:]
    me = me_ref[0]
    rows = data[0].shape[1]
    for m, ref in zip(order, data):
        at = pl.ds(pl.multiple_of((me ^ m) * rows, rows), rows)
        for b in range(2):
            cols_ref[at, b * LANES:(b + 1) * LANES] = ref[4 + b]
        for part in range(4):
            filt_ref[part, at, :] = ref[part]
    step = 2 * rows
    for i in range(shares * rows // step):
        at = slice(i * step, (i + 1) * step)
        first_re = jnp.dot(cos_ref[at, :], cols_ref[...], preferred_element_type=jnp.float32)
        first_sin = jnp.dot(sin_ref[at, :], cols_ref[...], preferred_element_type=jnp.float32)
        tc, ts = turn_cos_ref[at, :], turn_sin_ref[at, :]
        re0, im0 = first_re[:, :LANES], -first_sin[:, :LANES]
        re1, im1 = first_re[:, LANES:], -first_sin[:, LANES:]
        re1, im1 = re1 * tc + im1 * ts, im1 * tc - re1 * ts
        f0r, f0i, f1r, f1i = re0 + re1, im0 + im1, re0 - re1, im0 - im1
        s0r, s1r, s0i, s1i = (filt_ref[part, at, :].astype(jnp.float32) for part in range(4))
        p0r, p0i = f0r * s0r - f0i * s0i, f0r * s0i + f0i * s0r
        p1r, p1i = f1r * s1r - f1i * s1i, f1r * s1i + f1i * s1r
        b0r, b0i = 0.5 * (p0r + p1r), 0.5 * (p0i + p1i)
        b1r, b1i = 0.5 * (p0r - p1r), 0.5 * (p0i - p1i)
        b1r, b1i = b1r * tc - b1i * ts, b1i * tc + b1r * ts
        re_ref[at, :] = jnp.concatenate([b0r, b1r], axis=1).astype(jnp.bfloat16)
        im_ref[at, :] = jnp.concatenate([b0i, b1i], axis=1).astype(jnp.bfloat16)
    invert(me, 1, cos_ref, sin_ref, re_ref, im_ref, other_ref)


def invert(me, flip, cos_ref, sin_ref, re_ref, im_ref, out_ref):
    chips, _, rows, _ = out_ref.shape
    scale = 1.0 / (2 * chips * rows)
    for i in range(chips):
        at = pl.ds(pl.multiple_of((me ^ (2 * i + flip)) * rows, rows), rows)
        conv = jnp.dot(cos_ref[at, :], re_ref[...], preferred_element_type=jnp.float32)
        conv = conv - jnp.dot(sin_ref[at, :], im_ref[...], preferred_element_type=jnp.float32)
        conv = (conv * scale).astype(jnp.bfloat16)
        for b in range(2):
            out_ref[i, b] = conv[:, b * LANES:(b + 1) * LANES]


def rest_kernel(me_ref, re_ref, im_ref, cos_ref, sin_ref, out_ref):
    invert(me_ref[0], 0, cos_ref, sin_ref, re_ref, im_ref, out_ref)


def convolve(me, data, order):
    shares = len(data)
    rows = data[0].shape[1]
    block = shares * rows
    angle = angles(block, block, block)
    turn = np.broadcast_to(angles(block, 2, 2 * block)[:, 1:], (block, LANES))
    vmem, smem = pl.BlockSpec(memory_space=pltpu.VMEM), pl.BlockSpec(memory_space=pltpu.SMEM)
    share = jax.ShapeDtypeStruct((shares // 2, 2, rows, LANES), jnp.bfloat16)
    columns = jax.ShapeDtypeStruct((block, 2 * LANES), jnp.bfloat16)
    block_cos, block_sin = rounded(np.cos(angle)), rounded(np.sin(angle))
    other, rotated_re, rotated_im = pl.pallas_call(
        functools.partial(conv_kernel, order),
        in_specs=[smem] + [vmem] * (shares + 4),
        out_specs=[vmem] * 3,
        out_shape=[share, columns, columns],
        scratch_shapes=[
            pltpu.VMEM((block, 2 * LANES), jnp.bfloat16),
            pltpu.VMEM((4, block, LANES), jnp.bfloat16),
        ],
        compiler_params=pltpu.CompilerParams(vmem_limit_bytes=24 << 20),
        cost_estimate=pl.CostEstimate(flops=50 * block * block * LANES, bytes_accessed=8 * block * block, transcendentals=0),
        name="convolve",
    )(
        me, *data, block_cos, block_sin,
        jnp.asarray(np.cos(turn).astype(np.float32)), jnp.asarray(np.sin(turn).astype(np.float32)),
    )
    other = swap(other, "seq", 1)
    mine = pl.pallas_call(
        rest_kernel,
        in_specs=[smem] + [vmem] * 4,
        out_specs=vmem,
        out_shape=share,
        compiler_params=pltpu.CompilerParams(vmem_limit_bytes=24 << 20),
        cost_estimate=pl.CostEstimate(flops=4 * block * block * LANES, bytes_accessed=4 * block * block, transcendentals=0),
        name="convolve_rest",
    )(me, rotated_re, rotated_im, block_cos, block_sin)
    return mine, other


def gate_kernel(chips, me_ref, *refs):
    held, (gate_ref, *outs, conv_ref) = refs[:len(chips)], refs[len(chips):]
    _, span, block_rows, _ = held[0].shape
    rows = span * block_rows
    for flip, ref in zip(chips, held):
        for core in range(2):
            share = me_ref[0] ^ (2 * flip + core)
            conv_ref[:, pl.ds(pl.multiple_of(share * LANES, LANES), LANES)] = ref[core].reshape(rows, LANES)
    conv = jnp.dot(join_rows(rows, span), conv_ref[...], preferred_element_type=jnp.float32)
    gated = (conv * gate_ref[...].astype(jnp.float32)).astype(jnp.bfloat16)
    part = rows // len(outs)
    for p, out_ref in enumerate(outs):
        out_ref[...] = gated[p * part:(p + 1) * part]


def gate(me, held, chips, gate_out, parts):
    rows, width = gate_out.shape
    vmem = pl.BlockSpec(memory_space=pltpu.VMEM)
    return pl.pallas_call(
        functools.partial(gate_kernel, chips),
        in_specs=[pl.BlockSpec(memory_space=pltpu.SMEM)] + [vmem] * (len(held) + 1),
        out_specs=[vmem] * parts,
        out_shape=[jax.ShapeDtypeStruct((rows // parts, width), jnp.bfloat16)] * parts,
        scratch_shapes=[pltpu.VMEM((rows, width), jnp.bfloat16)],
        compiler_params=pltpu.CompilerParams(vmem_limit_bytes=16 << 20),
        name="gate",
    )(me, *held, gate_out)


def own_kernel(me_ref, *refs):
    parts = (len(refs) - 1) // 2
    gated, slabs, out_ref = refs[:parts], refs[parts:-1], refs[-1]
    rows, depth = gated[0].shape[0], slabs[0].shape[0]
    for p, gated_ref in enumerate(gated):
        out_ref[0, p * rows:(p + 1) * rows] = sum(
            jnp.dot(gated_ref[:, i * depth:(i + 1) * depth], slab[...], preferred_element_type=jnp.float32)
            for i, slab in enumerate(slabs)
        )


def own_part(me, gated, weight, blocks):
    parts = len(gated)
    part_rows, depth = gated[0].shape
    cols = weight.shape[1] // 8

    def column(slab, i, me_ref):
        flip = sum((jnp.where(i == place, f, 0) for place, (f, _) in enumerate(blocks)), 0)
        half = sum((jnp.where(i == place, h, 0) for place, (_, h) in enumerate(blocks)), 0)
        return slab, (me_ref[0] ^ flip) * 2 + half

    return pl.pallas_call(
        own_kernel,
        grid_spec=pltpu.PrefetchScalarGridSpec(
            num_scalar_prefetch=1,
            grid=(len(blocks),),
            in_specs=[pl.BlockSpec((part_rows, depth), lambda i, m: (0, 0))] * parts
            + [pl.BlockSpec((depth // parts, cols), functools.partial(column, slab)) for slab in range(parts)],
            out_specs=pl.BlockSpec((1, parts * part_rows, cols), lambda i, m: (i, 0, 0)),
        ),
        out_shape=jax.ShapeDtypeStruct((len(blocks), parts * part_rows, cols), jnp.float32),
        compiler_params=pltpu.CompilerParams(vmem_limit_bytes=40 << 20),
        cost_estimate=pl.CostEstimate(
            flops=2 * parts * part_rows * depth * cols * len(blocks),
            bytes_accessed=2 * depth * cols * len(blocks), transcendentals=0,
        ),
        name="own_part",
    )(me, *gated, *[weight] * parts)


def add_kernel(parts, kept, core_ref, own_ref, *refs):
    moved, refs = refs[:2 * parts], refs[2 * parts:]
    weights, (a_ref, b_ref, held_ref, sems) = refs[:4], refs[4:]
    slabs = sems.shape[1]
    depth = held_ref.shape[1] // slabs

    def copies(side, take_mine):
        source = weights[2 * side] if take_mine else weights[2 * side + 1]
        return [
            pltpu.make_async_copy(
                source.at[i * depth:(i + 1) * depth], held_ref.at[side, i * depth:(i + 1) * depth], sems.at[side, i]
            )
            for i in range(slabs)
        ]

    mine_core = 0 if kept else 1
    for side in range(2):

        @pl.when(core_ref[0] == mine_core)
        def _():
            for copy in copies(side, True):
                copy.start()

        @pl.when(core_ref[0] != mine_core)
        def _():
            for copy in copies(side, False):
                copy.start()

    rows = moved[0].shape[0]
    for side, out_ref in enumerate((a_ref, b_ref)):
        for i, copy in enumerate(copies(side, True)):
            copy.wait()
        for p in range(parts):
            at = slice(p * rows, (p + 1) * rows)
            total = own_ref[side, at] + jnp.dot(
                moved[side * parts + p][...], held_ref[side], preferred_element_type=jnp.float32
            )
            out_ref[at] = total.astype(out_ref.dtype)


def add_moved(core, own, moved_x, moved_y, weights, first, kept, dtype):
    parts = len(moved_x)
    rows, depth = moved_x[0].shape
    cols = own.shape[2]
    whole = pl.BlockSpec((rows, depth), lambda i: (0, 0))
    shape = jax.ShapeDtypeStruct((parts * rows, cols), dtype)
    out = pl.BlockSpec((parts * rows, cols), lambda i: (0, 0))
    return pl.pallas_call(
        functools.partial(add_kernel, parts, kept),
        grid=(1,),
        in_specs=[
            pl.BlockSpec(memory_space=pltpu.SMEM),
            pl.BlockSpec((2, parts * rows, cols), lambda i: (0, first, 0)),
        ]
        + [whole] * (2 * parts)
        + [pl.BlockSpec(memory_space=pl.ANY)] * 4,
        out_specs=[out, out],
        out_shape=[shape, shape],
        scratch_shapes=[pltpu.VMEM((2, depth, cols), jnp.bfloat16), pltpu.SemaphoreType.DMA((2, 4))],
        compiler_params=pltpu.CompilerParams(vmem_limit_bytes=40 << 20),
        cost_estimate=pl.CostEstimate(
            flops=4 * parts * rows * depth * cols, bytes_accessed=4 * depth * cols, transcendentals=0
        ),
        name="add_kept" if kept else "add_sent",
    )(core, own, *moved_x, *moved_y, *weights)


def finish_kernel(kept_a_ref, kept_b_ref, sum_a_ref, sum_b_ref, *refs):
    out_ref = refs[-1]
    cols = kept_a_ref.shape[1]
    out_ref[:, :cols] = (kept_a_ref[...] + sum_a_ref[...].astype(jnp.float32)).astype(out_ref.dtype)
    out_ref[:, cols:] = (kept_b_ref[...] + sum_b_ref[...].astype(jnp.float32)).astype(out_ref.dtype)


def finish(kept_a, kept_b, sum_a, sum_b, part, before):
    rows, cols = sum_a.shape
    total = kept_a.shape[0]
    kept = pl.BlockSpec((rows, cols), lambda i: (part, 0))
    sums = pl.BlockSpec((rows, cols), lambda i: (0, 0))
    earlier = [] if before is None else [before]
    return pl.pallas_call(
        finish_kernel,
        grid=(1,),
        in_specs=[kept, kept, sums, sums] + [pl.BlockSpec(memory_space=pl.ANY)] * len(earlier),
        out_specs=pl.BlockSpec((rows, 2 * cols), lambda i: (part, 0)),
        out_shape=jax.ShapeDtypeStruct((total, 2 * cols), jnp.bfloat16),
        input_output_aliases={4: 0} if earlier else {},
        compiler_params=pltpu.CompilerParams(vmem_limit_bytes=16 << 20),
        name="finish",
    )(kept_a, kept_b, sum_a, sum_b, *earlier)


def swap(data, axis, flip):
    return lax.ppermute(data, axis, [(i, i ^ flip) for i in range(lax.axis_size(axis))])


def by_channels(values, gate_in, gate_out, spectrum, out_weight):
    seq_count = lax.axis_size("seq")
    here = lax.axis_index("seq").astype(jnp.int32)
    me = lax.axis_index("chan").astype(jnp.int32)
    core = here % 2
    parts = 2

    order = tuple(sorted(range(seq_count), key=lambda m: (m == 0, m == 1, m % 2, -m)))
    packed = list(pack(here.reshape(1), values, gate_in, spectrum, seq_count))
    places = jnp.stack([(me ^ (1 + 2 * core)) * 2, (me ^ (2 + core)) * 2 + 1])
    _, places = lax.optimization_barrier((packed, places))
    block_x, block_y = take_blocks(places, out_weight)
    late = [m for m in order if m % 2]
    weight_x, weight_y = swap(block_x, "chan", 1), swap(block_y, "chan", 2)
    data = {m: swap(packed[m], "seq", m) if m else packed[m] for m in order if m % 2 == 0}
    held, data[order[0]] = lax.optimization_barrier(([packed[m] for m in late], data[order[0]]))
    data.update({m: swap(mine, "seq", m) for m, mine in zip(late, held)})
    mine, other = convolve(here.reshape(1), [data[m] for m in order], order)
    held = [jnp.stack([mine[flip], other[flip]]) for flip in range(seq_count // 2)]
    chips = tuple(reversed(range(seq_count // 2)))
    held = [swap(held[flip], "seq", 2 * flip) if flip else held[flip] for flip in chips]
    gated = gate(here.reshape(1), held, chips, gate_out, parts)
    weight_x, weight_y, _ = lax.optimization_barrier((weight_x, weight_y, gated))
    weights = [weight_x, swap(weight_x, "seq", 1), weight_y, swap(weight_y, "seq", 1)]
    own = own_part(me.reshape(1), gated, out_weight, ((2, 0), (1, 1)))
    core = core.reshape(1)
    moved_x, moved_y = [], []
    for p in range(parts):
        mine = gated[p]
        if p:
            mine, own, weights[1] = lax.optimization_barrier((mine, own, weights[1]))
        moved_x.append(swap(mine, "chan", 1))
        moved_y.append(swap(mine, "chan", 2))
    sums_a, sums_b = [], []
    for p in range(parts):
        if p == parts - 1:
            own_kept = own_part(me.reshape(1), gated, out_weight, ((0, 0), (0, 1)))
            own, own_kept = lax.optimization_barrier((own, own_kept))
        sent = add_moved(core, own, moved_x[p:p + 1], moved_y[p:p + 1], weights, p, False, jnp.bfloat16)
        sums_a.append(swap(sent[0], "chan", 2))
        sums_b.append(swap(sent[1], "chan", 1))
    kept_a, kept_b = add_moved(core, own_kept, moved_x, moved_y, weights, 0, True, jnp.float32)
    mixed = None
    for p in range(parts):
        mixed = finish(kept_a, kept_b, sums_a[p], sums_b[p], p, mixed)
    return mixed


def to_columns(data):
    return lax.all_to_all(data, "seq", split_axis=2, concat_axis=1, tiled=True)


def to_rows(data):
    return lax.all_to_all(data, "seq", split_axis=1, concat_axis=2, tiled=True)


def by_frequencies(values, gate_in, gate_out, spectrum, out_weight):
    seq_count = lax.axis_size("seq")
    seq_index = lax.axis_index("seq")
    tok_rows, chan_width = values.shape
    block_rows = BLOCK // seq_count
    span = tok_rows // block_rows
    tokens_all = BLOCK * span
    col_share = span * chan_width // seq_count
    block_cos = rounded(np.cos(angles(BLOCK, BLOCK, BLOCK)))
    block_sin = rounded(np.sin(angles(BLOCK, BLOCK, BLOCK)))
    span_cos = rounded(np.cos(angles(span, span, span)))
    span_sin = rounded(np.sin(angles(span, span, span)))
    turn_all = angles(BLOCK, span, tokens_all)
    turn_cos_all = jnp.asarray(np.cos(turn_all).astype(np.float32))
    turn_sin_all = jnp.asarray(np.sin(turn_all).astype(np.float32))
    source = (values.astype(jnp.float32) * gate_in.astype(jnp.float32)).astype(jnp.bfloat16)
    spread = to_columns(source.reshape(1, block_rows, seq_count, col_share))
    columns = spread.reshape(BLOCK, col_share)
    cos_part = jnp.dot(jnp.transpose(block_cos), columns, preferred_element_type=jnp.float32)
    sin_part = jnp.dot(jnp.transpose(block_sin), columns, preferred_element_type=jnp.float32)
    col_pos = (seq_index * col_share + jnp.arange(col_share, dtype=jnp.int32)) // chan_width
    turn_cos = jnp.take(turn_cos_all, col_pos, axis=1)
    turn_sin = jnp.take(turn_sin_all, col_pos, axis=1)
    twist_re = cos_part * turn_cos - sin_part * turn_sin
    twist_im = -sin_part * turn_cos - cos_part * turn_sin
    twisted = jnp.stack([twist_re, twist_im]).astype(jnp.bfloat16)
    arranged = to_rows(twisted).reshape(2, block_rows, span, chan_width)
    with_cos = jnp.einsum("bd,kcbh->kdch", span_cos, arranged, preferred_element_type=jnp.float32)
    with_sin = jnp.einsum("bd,kcbh->kdch", span_sin, arranged, preferred_element_type=jnp.float32)
    freq_re = with_cos[0] + with_sin[1]
    freq_im = with_cos[1] - with_sin[0]
    prod_re = freq_re * spectrum[0] - freq_im * spectrum[1]
    prod_im = freq_re * spectrum[1] + freq_im * spectrum[0]
    product = jnp.stack([prod_re, prod_im]).astype(jnp.bfloat16)
    back_cos = jnp.einsum("db,kdch->kcbh", span_cos, product, preferred_element_type=jnp.float32)
    back_sin = jnp.einsum("db,kdch->kcbh", span_sin, product, preferred_element_type=jnp.float32)
    back_re = (back_cos[0] - back_sin[1]) / span
    back_im = (back_cos[1] + back_sin[0]) / span
    back_tc = lax.dynamic_slice_in_dim(turn_cos_all, seq_index * block_rows, block_rows)[:, :, None]
    back_ts = lax.dynamic_slice_in_dim(turn_sin_all, seq_index * block_rows, block_rows)[:, :, None]
    rotated = jnp.stack(
        [back_re * back_tc - back_im * back_ts, back_im * back_tc + back_re * back_ts]
    ).astype(jnp.bfloat16)
    gathered = to_columns(rotated.reshape(2, block_rows, seq_count, col_share)).reshape(2, BLOCK, col_share)
    summed = jnp.dot(block_cos, gathered[0], preferred_element_type=jnp.float32)
    summed = summed - jnp.dot(block_sin, gathered[1], preferred_element_type=jnp.float32)
    ordered = (summed / BLOCK).astype(jnp.bfloat16).reshape(1, BLOCK, col_share)
    conv = to_rows(ordered).reshape(tok_rows, chan_width)
    gated = (conv.astype(jnp.float32) * gate_out.astype(jnp.float32)).astype(jnp.bfloat16)
    partial_sum = jnp.dot(gated, out_weight, preferred_element_type=jnp.float32)
    return lax.psum_scatter(partial_sum.astype(jnp.bfloat16), "chan", scatter_dimension=1, tiled=True)


def shards(values, gate_in, gate_out, spectrum, out_weight):
    seq_count, chan_count = lax.axis_size("seq"), lax.axis_size("chan")
    _, span, block_rows, width = spectrum.shape
    one_lane_block = width == seq_count * LANES and block_rows % 32 == 0
    if span == 2 and chan_count == 4 and seq_count & (seq_count - 1) == 0 and one_lane_block:
        return by_channels(values, gate_in, gate_out, spectrum, out_weight)
    return by_frequencies(values, gate_in, gate_out, spectrum, out_weight)


def solution(mesh):
    placed = (
        P("seq", "chan"),
        P("seq", "chan"),
        P("seq", "chan"),
        P(None, None, "seq", "chan"),
        P("chan", None),
    )
    return jax.shard_map(
        shards, mesh=mesh, in_specs=placed, out_specs=P("seq", "chan"), check_vma=False
    )
```

```python
import functools
import math

import jax
import jax.numpy as jnp
import ml_dtypes
import numpy as np
from jax import lax
from jax.experimental import pallas as pl
from jax.experimental.pallas import tpu as pltpu
from jax.sharding import PartitionSpec as P

BLOCK = 1024
LANES = 128


def angles(first, second, period):
    return (np.arange(first)[:, None] * np.arange(second)[None, :] % period) * (2.0 * math.pi / period)


def rounded(table):
    return jnp.asarray(table.astype(np.float32).astype(ml_dtypes.bfloat16))


def split_rows(rows, span):
    out = lax.broadcasted_iota(jnp.int32, (rows, rows), 0)
    token = lax.broadcasted_iota(jnp.int32, (rows, rows), 1)
    block_rows = rows // span
    return jnp.where(token == (out % block_rows) * span + out // block_rows, 1.0, 0.0).astype(jnp.bfloat16)


def join_rows(rows, span):
    token = lax.broadcasted_iota(jnp.int32, (rows, rows), 0)
    held = lax.broadcasted_iota(jnp.int32, (rows, rows), 1)
    block_rows = rows // span
    return jnp.where(token == (held % block_rows) * span + held // block_rows, 1.0, 0.0).astype(jnp.bfloat16)


def pack_kernel(span, me_ref, values_hbm, gate_hbm, spectrum_hbm, *refs):
    outs, (values_ref, gate_ref, spectrum_ref, sems) = refs[:-4], refs[-4:]
    copies = [
        pltpu.make_async_copy(values_hbm, values_ref, sems.at[0]),
        pltpu.make_async_copy(gate_hbm, gate_ref, sems.at[1]),
    ]
    for part in range(2):
        for d in range(span):
            copies.append(pltpu.make_async_copy(
                spectrum_hbm.at[part, d], spectrum_ref.at[part * span + d], sems.at[2 + part * span + d]
            ))
    for copy in copies:
        copy.start()
    me = me_ref[0]
    rows = values_ref.shape[0]
    block_rows = rows // span
    copies[0].wait()
    copies[1].wait()
    source = (values_ref[...].astype(jnp.float32) * gate_ref[...].astype(jnp.float32)).astype(jnp.bfloat16)
    values_ref[...] = jnp.dot(
        split_rows(rows, span), source, preferred_element_type=jnp.float32
    ).astype(jnp.bfloat16)

    def lanes_of(m):
        return pl.ds(pl.multiple_of((me ^ m) * LANES, LANES), LANES)

    for m, out_ref in enumerate(outs):
        for b in range(span):
            out_ref[2 * span + b] = values_ref[b * block_rows:(b + 1) * block_rows, lanes_of(m)]
    for part in range(2 * span):
        copies[2 + part].wait()
        for m, out_ref in enumerate(outs):
            out_ref[part] = spectrum_ref[part, :, lanes_of(m)].astype(jnp.bfloat16)


def pack(me, values, gate_in, spectrum, shares):
    rows, width = values.shape
    _, span, block_rows, _ = spectrum.shape
    shape = (3 * span, block_rows, LANES)
    vmem, hbm = pl.BlockSpec(memory_space=pltpu.VMEM), pl.BlockSpec(memory_space=pltpu.HBM)
    return pl.pallas_call(
        functools.partial(pack_kernel, span),
        in_specs=[pl.BlockSpec(memory_space=pltpu.SMEM), hbm, hbm, hbm],
        out_specs=[vmem] * shares,
        out_shape=[jax.ShapeDtypeStruct(shape, jnp.bfloat16)] * shares,
        scratch_shapes=[
            pltpu.VMEM((rows, width), jnp.bfloat16),
            pltpu.VMEM((rows, width), jnp.bfloat16),
            pltpu.VMEM((2 * span, block_rows, width), jnp.float32),
            pltpu.SemaphoreType.DMA((2 + 2 * span,)),
        ],
        compiler_params=pltpu.CompilerParams(vmem_limit_bytes=60 << 20),
        name="pack",
    )(me, values, gate_in, spectrum)


def take_kernel(places_ref, weight_hbm, *refs):
    outs, sems = refs[:-1], refs[-1]
    slabs = sems.shape[1]
    depth, cols = outs[0].shape[0] // slabs, outs[0].shape[1]
    copies = [
        pltpu.make_async_copy(
            weight_hbm.at[i * depth:(i + 1) * depth, pl.ds(pl.multiple_of(places_ref[k] * cols, cols), cols)],
            out_ref.at[i * depth:(i + 1) * depth],
            sems.at[k, i],
        )
        for k, out_ref in enumerate(outs)
        for i in range(slabs)
    ]
    for copy in copies:
        copy.start()
    for copy in copies:
        copy.wait()


def take_blocks(places, weight):
    depth, cols = weight.shape[0], weight.shape[1] // 8
    count, slabs = places.shape[0], 4
    return pl.pallas_call(
        take_kernel,
        in_specs=[pl.BlockSpec(memory_space=pltpu.SMEM), pl.BlockSpec(memory_space=pltpu.HBM)],
        out_specs=[pl.BlockSpec(memory_space=pltpu.VMEM)] * count,
        out_shape=[jax.ShapeDtypeStruct((depth, cols), weight.dtype)] * count,
        scratch_shapes=[pltpu.SemaphoreType.DMA((count, slabs))],
        compiler_params=pltpu.CompilerParams(vmem_limit_bytes=48 << 20),
        cost_estimate=pl.CostEstimate(flops=0, bytes_accessed=128 * depth * cols, transcendentals=0),
        name="take_blocks",
    )(places, weight)


def conv_kernel(order, me_ref, *refs):
    shares = len(order)
    data, (cos_ref, sin_ref, turn_cos_ref, turn_sin_ref) = refs[:shares], refs[shares:shares + 4]
    other_ref, re_ref, im_ref, cols_ref, filt_ref = refs[shares + 4:]
    me = me_ref[0]
    rows = data[0].shape[1]
    for m, ref in zip(order, data):
        at = pl.ds(pl.multiple_of((me ^ m) * rows, rows), rows)
        for b in range(2):
            cols_ref[at, b * LANES:(b + 1) * LANES] = ref[4 + b]
        for part in range(4):
            filt_ref[part, at, :] = ref[part]
    step = 2 * rows
    for i in range(shares * rows // step):
        at = slice(i * step, (i + 1) * step)
        first_re = jnp.dot(cos_ref[at, :], cols_ref[...], preferred_element_type=jnp.float32)
        first_sin = jnp.dot(sin_ref[at, :], cols_ref[...], preferred_element_type=jnp.float32)
        tc, ts = turn_cos_ref[at, :], turn_sin_ref[at, :]
        re0, sin0 = first_re[:, :LANES], first_sin[:, :LANES]
        re1, sin1 = first_re[:, LANES:], first_sin[:, LANES:]
        re1, sin1 = re1 * tc - sin1 * ts, sin1 * tc + re1 * ts
        f0r, f0s, f1r, f1s = re0 + re1, sin0 + sin1, re0 - re1, sin0 - sin1
        s0r, s1r, s0i, s1i = (filt_ref[part, at, :].astype(jnp.float32) for part in range(4))
        p0r, p0i = f0r * s0r + f0s * s0i, f0r * s0i - f0s * s0r
        p1r, p1i = f1r * s1r + f1s * s1i, f1r * s1i - f1s * s1r
        b0r, b0i = p0r + p1r, p0i + p1i
        b1r, b1i = p0r - p1r, p0i - p1i
        b1r, b1i = b1r * tc - b1i * ts, b1i * tc + b1r * ts
        re_ref[at, :] = jnp.concatenate([b0r, b1r], axis=1).astype(jnp.bfloat16)
        im_ref[at, :] = jnp.concatenate([b0i, b1i], axis=1).astype(jnp.bfloat16)
    invert(me, 1, cos_ref, sin_ref, re_ref, im_ref, other_ref)


def invert(me, flip, cos_ref, sin_ref, re_ref, im_ref, out_ref):
    chips, _, rows, _ = out_ref.shape
    scale = 1.0 / (2 * 2 * chips * rows)
    for i in range(chips):
        at = pl.ds(pl.multiple_of((me ^ (2 * i + flip)) * rows, rows), rows)
        conv = jnp.dot(cos_ref[at, :], re_ref[...], preferred_element_type=jnp.float32)
        conv = conv - jnp.dot(sin_ref[at, :], im_ref[...], preferred_element_type=jnp.float32)
        conv = (conv * scale).astype(jnp.bfloat16)
        for b in range(2):
            out_ref[i, b] = conv[:, b * LANES:(b + 1) * LANES]


def rest_kernel(me_ref, re_ref, im_ref, cos_ref, sin_ref, out_ref):
    invert(me_ref[0], 0, cos_ref, sin_ref, re_ref, im_ref, out_ref)


def convolve(me, data, order):
    shares = len(data)
    rows = data[0].shape[1]
    block = shares * rows
    angle = angles(block, block, block)
    turn = np.broadcast_to(angles(block, 2, 2 * block)[:, 1:], (block, LANES))
    vmem, smem = pl.BlockSpec(memory_space=pltpu.VMEM), pl.BlockSpec(memory_space=pltpu.SMEM)
    share = jax.ShapeDtypeStruct((shares // 2, 2, rows, LANES), jnp.bfloat16)
    columns = jax.ShapeDtypeStruct((block, 2 * LANES), jnp.bfloat16)
    block_cos, block_sin = rounded(np.cos(angle)), rounded(np.sin(angle))
    other, rotated_re, rotated_im = pl.pallas_call(
        functools.partial(conv_kernel, order),
        in_specs=[smem] + [vmem] * (shares + 4),
        out_specs=[vmem] * 3,
        out_shape=[share, columns, columns],
        scratch_shapes=[
            pltpu.VMEM((block, 2 * LANES), jnp.bfloat16),
            pltpu.VMEM((4, block, LANES), jnp.bfloat16),
        ],
        compiler_params=pltpu.CompilerParams(vmem_limit_bytes=24 << 20),
        cost_estimate=pl.CostEstimate(flops=50 * block * block * LANES, bytes_accessed=8 * block * block, transcendentals=0),
        name="convolve",
    )(
        me, *data, block_cos, block_sin,
        jnp.asarray(np.cos(turn).astype(np.float32)), jnp.asarray(np.sin(turn).astype(np.float32)),
    )
    other = swap(other, "seq", 1)
    mine = pl.pallas_call(
        rest_kernel,
        in_specs=[smem] + [vmem] * 4,
        out_specs=vmem,
        out_shape=share,
        compiler_params=pltpu.CompilerParams(vmem_limit_bytes=24 << 20),
        cost_estimate=pl.CostEstimate(flops=4 * block * block * LANES, bytes_accessed=4 * block * block, transcendentals=0),
        name="convolve_rest",
    )(me, rotated_re, rotated_im, block_cos, block_sin)
    return mine, other


def gate_kernel(chips, me_ref, *refs):
    held, (gate_ref, *outs, conv_ref) = refs[:len(chips)], refs[len(chips):]
    _, span, block_rows, _ = held[0].shape
    rows = span * block_rows
    for flip, ref in zip(chips, held):
        for core in range(2):
            share = me_ref[0] ^ (2 * flip + core)
            conv_ref[:, pl.ds(pl.multiple_of(share * LANES, LANES), LANES)] = ref[core].reshape(rows, LANES)
    conv = jnp.dot(join_rows(rows, span), conv_ref[...], preferred_element_type=jnp.float32)
    gated = (conv * gate_ref[...].astype(jnp.float32)).astype(jnp.bfloat16)
    part = rows // len(outs)
    for p, out_ref in enumerate(outs):
        out_ref[...] = gated[p * part:(p + 1) * part]


def gate(me, held, chips, gate_out, parts):
    rows, width = gate_out.shape
    vmem = pl.BlockSpec(memory_space=pltpu.VMEM)
    return pl.pallas_call(
        functools.partial(gate_kernel, chips),
        in_specs=[pl.BlockSpec(memory_space=pltpu.SMEM)] + [vmem] * (len(held) + 1),
        out_specs=[vmem] * parts,
        out_shape=[jax.ShapeDtypeStruct((rows // parts, width), jnp.bfloat16)] * parts,
        scratch_shapes=[pltpu.VMEM((rows, width), jnp.bfloat16)],
        compiler_params=pltpu.CompilerParams(vmem_limit_bytes=16 << 20),
        name="gate",
    )(me, *held, gate_out)


def own_kernel(me_ref, *refs):
    parts = (len(refs) - 1) // 2
    gated, slabs, out_ref = refs[:parts], refs[parts:-1], refs[-1]
    rows, depth = gated[0].shape[0], slabs[0].shape[0]
    for p, gated_ref in enumerate(gated):
        out_ref[0, p * rows:(p + 1) * rows] = sum(
            jnp.dot(gated_ref[:, i * depth:(i + 1) * depth], slab[...], preferred_element_type=jnp.float32)
            for i, slab in enumerate(slabs)
        )


def own_part(me, gated, weight, blocks):
    parts = len(gated)
    part_rows, depth = gated[0].shape
    cols = weight.shape[1] // 8

    def column(slab, i, me_ref):
        flip = sum((jnp.where(i == place, f, 0) for place, (f, _) in enumerate(blocks)), 0)
        half = sum((jnp.where(i == place, h, 0) for place, (_, h) in enumerate(blocks)), 0)
        return slab, (me_ref[0] ^ flip) * 2 + half

    return pl.pallas_call(
        own_kernel,
        grid_spec=pltpu.PrefetchScalarGridSpec(
            num_scalar_prefetch=1,
            grid=(len(blocks),),
            in_specs=[pl.BlockSpec((part_rows, depth), lambda i, m: (0, 0))] * parts
            + [pl.BlockSpec((depth // parts, cols), functools.partial(column, slab)) for slab in range(parts)],
            out_specs=pl.BlockSpec((1, parts * part_rows, cols), lambda i, m: (i, 0, 0)),
        ),
        out_shape=jax.ShapeDtypeStruct((len(blocks), parts * part_rows, cols), jnp.float32),
        compiler_params=pltpu.CompilerParams(vmem_limit_bytes=40 << 20),
        cost_estimate=pl.CostEstimate(
            flops=2 * parts * part_rows * depth * cols * len(blocks),
            bytes_accessed=2 * depth * cols * len(blocks), transcendentals=0,
        ),
        name="own_part",
    )(me, *gated, *[weight] * parts)


def add_kernel(parts, kept, core_ref, own_ref, *refs):
    moved, refs = refs[:2 * parts], refs[2 * parts:]
    weights, (a_ref, b_ref, held_ref, sems) = refs[:4], refs[4:]
    slabs = sems.shape[1]
    depth = held_ref.shape[1] // slabs

    def copies(side, take_mine):
        source = weights[2 * side] if take_mine else weights[2 * side + 1]
        return [
            pltpu.make_async_copy(
                source.at[i * depth:(i + 1) * depth], held_ref.at[side, i * depth:(i + 1) * depth], sems.at[side, i]
            )
            for i in range(slabs)
        ]

    mine_core = 0 if kept else 1
    for side in range(2):

        @pl.when(core_ref[0] == mine_core)
        def _():
            for copy in copies(side, True):
                copy.start()

        @pl.when(core_ref[0] != mine_core)
        def _():
            for copy in copies(side, False):
                copy.start()

    rows = moved[0].shape[0]
    for side, out_ref in enumerate((a_ref, b_ref)):
        for i, copy in enumerate(copies(side, True)):
            copy.wait()
        for p in range(parts):
            at = slice(p * rows, (p + 1) * rows)
            total = own_ref[side, at] + jnp.dot(
                moved[side * parts + p][...], held_ref[side], preferred_element_type=jnp.float32
            )
            out_ref[at] = total.astype(out_ref.dtype)


def add_moved(core, own, moved_x, moved_y, weights, first, kept, dtype):
    parts = len(moved_x)
    rows, depth = moved_x[0].shape
    cols = own.shape[2]
    whole = pl.BlockSpec((rows, depth), lambda i: (0, 0))
    shape = jax.ShapeDtypeStruct((parts * rows, cols), dtype)
    out = pl.BlockSpec((parts * rows, cols), lambda i: (0, 0))
    return pl.pallas_call(
        functools.partial(add_kernel, parts, kept),
        grid=(1,),
        in_specs=[
            pl.BlockSpec(memory_space=pltpu.SMEM),
            pl.BlockSpec((2, parts * rows, cols), lambda i: (0, first, 0)),
        ]
        + [whole] * (2 * parts)
        + [pl.BlockSpec(memory_space=pl.ANY)] * 4,
        out_specs=[out, out],
        out_shape=[shape, shape],
        scratch_shapes=[pltpu.VMEM((2, depth, cols), jnp.bfloat16), pltpu.SemaphoreType.DMA((2, 4))],
        compiler_params=pltpu.CompilerParams(vmem_limit_bytes=40 << 20),
        cost_estimate=pl.CostEstimate(
            flops=4 * parts * rows * depth * cols, bytes_accessed=4 * depth * cols, transcendentals=0
        ),
        name="add_kept" if kept else "add_sent",
    )(core, own, *moved_x, *moved_y, *weights)


def finish_kernel(kept_a_ref, kept_b_ref, sum_a_ref, sum_b_ref, *refs):
    out_ref = refs[-1]
    cols = kept_a_ref.shape[1]
    out_ref[:, :cols] = (kept_a_ref[...] + sum_a_ref[...].astype(jnp.float32)).astype(out_ref.dtype)
    out_ref[:, cols:] = (kept_b_ref[...] + sum_b_ref[...].astype(jnp.float32)).astype(out_ref.dtype)


def finish(kept_a, kept_b, sum_a, sum_b, part, before):
    rows, cols = sum_a.shape
    total = kept_a.shape[0]
    kept = pl.BlockSpec((rows, cols), lambda i: (part, 0))
    sums = pl.BlockSpec((rows, cols), lambda i: (0, 0))
    earlier = [] if before is None else [before]
    return pl.pallas_call(
        finish_kernel,
        grid=(1,),
        in_specs=[kept, kept, sums, sums] + [pl.BlockSpec(memory_space=pl.ANY)] * len(earlier),
        out_specs=pl.BlockSpec((rows, 2 * cols), lambda i: (part, 0)),
        out_shape=jax.ShapeDtypeStruct((total, 2 * cols), jnp.bfloat16),
        input_output_aliases={4: 0} if earlier else {},
        compiler_params=pltpu.CompilerParams(vmem_limit_bytes=16 << 20),
        name="finish",
    )(kept_a, kept_b, sum_a, sum_b, *earlier)


def swap(data, axis, flip):
    return lax.ppermute(data, axis, [(i, i ^ flip) for i in range(lax.axis_size(axis))])


def by_channels(values, gate_in, gate_out, spectrum, out_weight):
    seq_count = lax.axis_size("seq")
    here = lax.axis_index("seq").astype(jnp.int32)
    me = lax.axis_index("chan").astype(jnp.int32)
    core = here % 2
    parts = 2

    order = tuple(sorted(range(seq_count), key=lambda m: (m == 0, m == 1, m % 2, -m)))
    packed = list(pack(here.reshape(1), values, gate_in, spectrum, seq_count))
    places = jnp.stack([(me ^ (1 + 2 * core)) * 2, (me ^ (2 + core)) * 2 + 1])
    _, places = lax.optimization_barrier((packed, places))
    block_x, block_y = take_blocks(places, out_weight)
    late = [m for m in order if m % 2]
    weight_x, weight_y = swap(block_x, "chan", 1), swap(block_y, "chan", 2)
    data = {m: swap(packed[m], "seq", m) if m else packed[m] for m in order if m % 2 == 0}
    held, data[order[0]] = lax.optimization_barrier(([packed[m] for m in late], data[order[0]]))
    data.update({m: swap(mine, "seq", m) for m, mine in zip(late, held)})
    mine, other = convolve(here.reshape(1), [data[m] for m in order], order)
    held = [jnp.stack([mine[flip], other[flip]]) for flip in range(seq_count // 2)]
    chips = tuple(reversed(range(seq_count // 2)))
    held = [swap(held[flip], "seq", 2 * flip) if flip else held[flip] for flip in chips]
    gated = gate(here.reshape(1), held, chips, gate_out, parts)
    weight_x, weight_y, _ = lax.optimization_barrier((weight_x, weight_y, gated))
    weights = [weight_x, swap(weight_x, "seq", 1), weight_y, swap(weight_y, "seq", 1)]
    own = own_part(me.reshape(1), gated, out_weight, ((2, 0), (1, 1)))
    core = core.reshape(1)
    moved_x, moved_y = [], []
    for p in range(parts):
        mine = gated[p]
        if p:
            mine, own, weights[1] = lax.optimization_barrier((mine, own, weights[1]))
        moved_x.append(swap(mine, "chan", 1))
        moved_y.append(swap(mine, "chan", 2))
    sums_a, sums_b = [], []
    for p in range(parts):
        if p == parts - 1:
            own_kept = own_part(me.reshape(1), gated, out_weight, ((0, 0), (0, 1)))
            own, own_kept = lax.optimization_barrier((own, own_kept))
        sent = add_moved(core, own, moved_x[p:p + 1], moved_y[p:p + 1], weights, p, False, jnp.bfloat16)
        sums_a.append(swap(sent[0], "chan", 2))
        sums_b.append(swap(sent[1], "chan", 1))
    kept_a, kept_b = add_moved(core, own_kept, moved_x, moved_y, weights, 0, True, jnp.float32)
    mixed = None
    for p in range(parts):
        mixed = finish(kept_a, kept_b, sums_a[p], sums_b[p], p, mixed)
    return mixed


def to_columns(data):
    return lax.all_to_all(data, "seq", split_axis=2, concat_axis=1, tiled=True)


def to_rows(data):
    return lax.all_to_all(data, "seq", split_axis=1, concat_axis=2, tiled=True)


def by_frequencies(values, gate_in, gate_out, spectrum, out_weight):
    seq_count = lax.axis_size("seq")
    seq_index = lax.axis_index("seq")
    tok_rows, chan_width = values.shape
    block_rows = BLOCK // seq_count
    span = tok_rows // block_rows
    tokens_all = BLOCK * span
    col_share = span * chan_width // seq_count
    block_cos = rounded(np.cos(angles(BLOCK, BLOCK, BLOCK)))
    block_sin = rounded(np.sin(angles(BLOCK, BLOCK, BLOCK)))
    span_cos = rounded(np.cos(angles(span, span, span)))
    span_sin = rounded(np.sin(angles(span, span, span)))
    turn_all = angles(BLOCK, span, tokens_all)
    turn_cos_all = jnp.asarray(np.cos(turn_all).astype(np.float32))
    turn_sin_all = jnp.asarray(np.sin(turn_all).astype(np.float32))
    source = (values.astype(jnp.float32) * gate_in.astype(jnp.float32)).astype(jnp.bfloat16)
    spread = to_columns(source.reshape(1, block_rows, seq_count, col_share))
    columns = spread.reshape(BLOCK, col_share)
    cos_part = jnp.dot(jnp.transpose(block_cos), columns, preferred_element_type=jnp.float32)
    sin_part = jnp.dot(jnp.transpose(block_sin), columns, preferred_element_type=jnp.float32)
    col_pos = (seq_index * col_share + jnp.arange(col_share, dtype=jnp.int32)) // chan_width
    turn_cos = jnp.take(turn_cos_all, col_pos, axis=1)
    turn_sin = jnp.take(turn_sin_all, col_pos, axis=1)
    twist_re = cos_part * turn_cos - sin_part * turn_sin
    twist_im = -sin_part * turn_cos - cos_part * turn_sin
    twisted = jnp.stack([twist_re, twist_im]).astype(jnp.bfloat16)
    arranged = to_rows(twisted).reshape(2, block_rows, span, chan_width)
    with_cos = jnp.einsum("bd,kcbh->kdch", span_cos, arranged, preferred_element_type=jnp.float32)
    with_sin = jnp.einsum("bd,kcbh->kdch", span_sin, arranged, preferred_element_type=jnp.float32)
    freq_re = with_cos[0] + with_sin[1]
    freq_im = with_cos[1] - with_sin[0]
    prod_re = freq_re * spectrum[0] - freq_im * spectrum[1]
    prod_im = freq_re * spectrum[1] + freq_im * spectrum[0]
    product = jnp.stack([prod_re, prod_im]).astype(jnp.bfloat16)
    back_cos = jnp.einsum("db,kdch->kcbh", span_cos, product, preferred_element_type=jnp.float32)
    back_sin = jnp.einsum("db,kdch->kcbh", span_sin, product, preferred_element_type=jnp.float32)
    back_re = (back_cos[0] - back_sin[1]) / span
    back_im = (back_cos[1] + back_sin[0]) / span
    back_tc = lax.dynamic_slice_in_dim(turn_cos_all, seq_index * block_rows, block_rows)[:, :, None]
    back_ts = lax.dynamic_slice_in_dim(turn_sin_all, seq_index * block_rows, block_rows)[:, :, None]
    rotated = jnp.stack(
        [back_re * back_tc - back_im * back_ts, back_im * back_tc + back_re * back_ts]
    ).astype(jnp.bfloat16)
    gathered = to_columns(rotated.reshape(2, block_rows, seq_count, col_share)).reshape(2, BLOCK, col_share)
    summed = jnp.dot(block_cos, gathered[0], preferred_element_type=jnp.float32)
    summed = summed - jnp.dot(block_sin, gathered[1], preferred_element_type=jnp.float32)
    ordered = (summed / BLOCK).astype(jnp.bfloat16).reshape(1, BLOCK, col_share)
    conv = to_rows(ordered).reshape(tok_rows, chan_width)
    gated = (conv.astype(jnp.float32) * gate_out.astype(jnp.float32)).astype(jnp.bfloat16)
    partial_sum = jnp.dot(gated, out_weight, preferred_element_type=jnp.float32)
    return lax.psum_scatter(partial_sum.astype(jnp.bfloat16), "chan", scatter_dimension=1, tiled=True)


def shards(values, gate_in, gate_out, spectrum, out_weight):
    seq_count, chan_count = lax.axis_size("seq"), lax.axis_size("chan")
    _, span, block_rows, width = spectrum.shape
    one_lane_block = width == seq_count * LANES and block_rows % 32 == 0
    if span == 2 and chan_count == 4 and seq_count & (seq_count - 1) == 0 and one_lane_block:
        return by_channels(values, gate_in, gate_out, spectrum, out_weight)
    return by_frequencies(values, gate_in, gate_out, spectrum, out_weight)


def solution(mesh):
    placed = (
        P("seq", "chan"),
        P("seq", "chan"),
        P("seq", "chan"),
        P(None, None, "seq", "chan"),
        P("chan", None),
    )
    return jax.shard_map(
        shards, mesh=mesh, in_specs=placed, out_specs=P("seq", "chan"), check_vma=False
    )
```

```python
import functools
import math

import jax
import jax.numpy as jnp
import ml_dtypes
import numpy as np
from jax import lax
from jax.experimental import pallas as pl
from jax.experimental.pallas import tpu as pltpu
from jax.sharding import PartitionSpec as P

BLOCK = 1024
LANES = 128


def angles(first, second, period):
    return (np.arange(first)[:, None] * np.arange(second)[None, :] % period) * (2.0 * math.pi / period)


def rounded(table):
    return jnp.asarray(table.astype(np.float32).astype(ml_dtypes.bfloat16))


def split_rows(rows, span):
    out = lax.broadcasted_iota(jnp.int32, (rows, rows), 0)
    token = lax.broadcasted_iota(jnp.int32, (rows, rows), 1)
    block_rows = rows // span
    return jnp.where(token == (out % block_rows) * span + out // block_rows, 1.0, 0.0).astype(jnp.bfloat16)


def join_rows(rows, span):
    token = lax.broadcasted_iota(jnp.int32, (rows, rows), 0)
    held = lax.broadcasted_iota(jnp.int32, (rows, rows), 1)
    block_rows = rows // span
    return jnp.where(token == (held % block_rows) * span + held // block_rows, 1.0, 0.0).astype(jnp.bfloat16)


def pack_kernel(span, me_ref, values_hbm, gate_hbm, spectrum_hbm, *refs):
    outs, (values_ref, gate_ref, spectrum_ref, sems) = refs[:-4], refs[-4:]
    copies = [
        pltpu.make_async_copy(values_hbm, values_ref, sems.at[0]),
        pltpu.make_async_copy(gate_hbm, gate_ref, sems.at[1]),
    ]
    for part in range(2):
        for d in range(span):
            copies.append(pltpu.make_async_copy(
                spectrum_hbm.at[part, d], spectrum_ref.at[part * span + d], sems.at[2 + part * span + d]
            ))
    for copy in copies:
        copy.start()
    me = me_ref[0]
    rows = values_ref.shape[0]
    block_rows = rows // span
    copies[0].wait()
    copies[1].wait()
    source = (values_ref[...].astype(jnp.float32) * gate_ref[...].astype(jnp.float32)).astype(jnp.bfloat16)
    values_ref[...] = jnp.dot(
        split_rows(rows, span), source, preferred_element_type=jnp.float32
    ).astype(jnp.bfloat16)

    def lanes_of(m):
        return pl.ds(pl.multiple_of((me ^ m) * LANES, LANES), LANES)

    for m, out_ref in enumerate(outs):
        for b in range(span):
            out_ref[2 * span + b] = values_ref[b * block_rows:(b + 1) * block_rows, lanes_of(m)]
    for part in range(2 * span):
        copies[2 + part].wait()
        for m, out_ref in enumerate(outs):
            out_ref[part] = spectrum_ref[part, :, lanes_of(m)].astype(jnp.bfloat16)


def pack(me, values, gate_in, spectrum, shares):
    rows, width = values.shape
    _, span, block_rows, _ = spectrum.shape
    shape = (3 * span, block_rows, LANES)
    vmem, hbm = pl.BlockSpec(memory_space=pltpu.VMEM), pl.BlockSpec(memory_space=pltpu.HBM)
    return pl.pallas_call(
        functools.partial(pack_kernel, span),
        in_specs=[pl.BlockSpec(memory_space=pltpu.SMEM), hbm, hbm, hbm],
        out_specs=[vmem] * shares,
        out_shape=[jax.ShapeDtypeStruct(shape, jnp.bfloat16)] * shares,
        scratch_shapes=[
            pltpu.VMEM((rows, width), jnp.bfloat16),
            pltpu.VMEM((rows, width), jnp.bfloat16),
            pltpu.VMEM((2 * span, block_rows, width), jnp.float32),
            pltpu.SemaphoreType.DMA((2 + 2 * span,)),
        ],
        compiler_params=pltpu.CompilerParams(vmem_limit_bytes=60 << 20),
        name="pack",
    )(me, values, gate_in, spectrum)


def take_kernel(places_ref, weight_hbm, *refs):
    outs, sems = refs[:-1], refs[-1]
    slabs = sems.shape[1]
    depth, cols = outs[0].shape[0] // slabs, outs[0].shape[1]
    copies = [
        pltpu.make_async_copy(
            weight_hbm.at[i * depth:(i + 1) * depth, pl.ds(pl.multiple_of(places_ref[k] * cols, cols), cols)],
            out_ref.at[i * depth:(i + 1) * depth],
            sems.at[k, i],
        )
        for k, out_ref in enumerate(outs)
        for i in range(slabs)
    ]
    for copy in copies:
        copy.start()
    for copy in copies:
        copy.wait()


def take_blocks(places, weight):
    depth, cols = weight.shape[0], weight.shape[1] // 8
    count, slabs = places.shape[0], 4
    return pl.pallas_call(
        take_kernel,
        in_specs=[pl.BlockSpec(memory_space=pltpu.SMEM), pl.BlockSpec(memory_space=pltpu.HBM)],
        out_specs=[pl.BlockSpec(memory_space=pltpu.VMEM)] * count,
        out_shape=[jax.ShapeDtypeStruct((depth, cols), weight.dtype)] * count,
        scratch_shapes=[pltpu.SemaphoreType.DMA((count, slabs))],
        compiler_params=pltpu.CompilerParams(vmem_limit_bytes=48 << 20),
        cost_estimate=pl.CostEstimate(flops=0, bytes_accessed=128 * depth * cols, transcendentals=0),
        name="take_blocks",
    )(places, weight)


def conv_kernel(order, me_ref, *refs):
    shares = len(order)
    data, (cos_ref, sin_ref, turn_cos_ref, turn_sin_ref) = refs[:shares], refs[shares:shares + 4]
    other_ref, re_ref, im_ref, cols_ref, filt_ref = refs[shares + 4:]
    me = me_ref[0]
    rows = data[0].shape[1]
    for m, ref in zip(order, data):
        at = pl.ds(pl.multiple_of((me ^ m) * rows, rows), rows)
        for b in range(2):
            cols_ref[at, b * LANES:(b + 1) * LANES] = ref[4 + b]
        for part in range(4):
            filt_ref[part, at, :] = ref[part]
    step = 2 * rows
    for i in range(shares * rows // step):
        at = slice(i * step, (i + 1) * step)
        first_re = jnp.dot(cos_ref[at, :], cols_ref[...], preferred_element_type=jnp.float32)
        first_sin = jnp.dot(sin_ref[at, :], cols_ref[...], preferred_element_type=jnp.float32)
        tc, ts = turn_cos_ref[at, :], turn_sin_ref[at, :]
        re0, im0 = first_re[:, :LANES], -first_sin[:, :LANES]
        re1, im1 = first_re[:, LANES:], -first_sin[:, LANES:]
        re1, im1 = re1 * tc + im1 * ts, im1 * tc - re1 * ts
        f0r, f0i, f1r, f1i = re0 + re1, im0 + im1, re0 - re1, im0 - im1
        s0r, s1r, s0i, s1i = (filt_ref[part, at, :].astype(jnp.float32) for part in range(4))
        p0r, p0i = f0r * s0r - f0i * s0i, f0r * s0i + f0i * s0r
        p1r, p1i = f1r * s1r - f1i * s1i, f1r * s1i + f1i * s1r
        b0r, b0i = 0.5 * (p0r + p1r), 0.5 * (p0i + p1i)
        b1r, b1i = 0.5 * (p0r - p1r), 0.5 * (p0i - p1i)
        b1r, b1i = b1r * tc - b1i * ts, b1i * tc + b1r * ts
        re_ref[at, :] = jnp.concatenate([b0r, b1r], axis=1).astype(jnp.bfloat16)
        im_ref[at, :] = jnp.concatenate([b0i, b1i], axis=1).astype(jnp.bfloat16)
    invert(me, 1, cos_ref, sin_ref, re_ref, im_ref, other_ref)


def invert(me, flip, cos_ref, sin_ref, re_ref, im_ref, out_ref):
    chips, _, rows, _ = out_ref.shape
    scale = 1.0 / (2 * chips * rows)
    for i in range(chips):
        at = pl.ds(pl.multiple_of((me ^ (2 * i + flip)) * rows, rows), rows)
        conv = jnp.dot(cos_ref[at, :], re_ref[...], preferred_element_type=jnp.float32)
        conv = conv - jnp.dot(sin_ref[at, :], im_ref[...], preferred_element_type=jnp.float32)
        conv = (conv * scale).astype(jnp.bfloat16)
        for b in range(2):
            out_ref[i, b] = conv[:, b * LANES:(b + 1) * LANES]


def rest_kernel(me_ref, re_ref, im_ref, cos_ref, sin_ref, out_ref):
    invert(me_ref[0], 0, cos_ref, sin_ref, re_ref, im_ref, out_ref)


def convolve(me, data, order):
    shares = len(data)
    rows = data[0].shape[1]
    block = shares * rows
    angle = angles(block, block, block)
    turn = np.broadcast_to(angles(block, 2, 2 * block)[:, 1:], (block, LANES))
    vmem, smem = pl.BlockSpec(memory_space=pltpu.VMEM), pl.BlockSpec(memory_space=pltpu.SMEM)
    share = jax.ShapeDtypeStruct((shares // 2, 2, rows, LANES), jnp.bfloat16)
    columns = jax.ShapeDtypeStruct((block, 2 * LANES), jnp.bfloat16)
    block_cos, block_sin = rounded(np.cos(angle)), rounded(np.sin(angle))
    other, rotated_re, rotated_im = pl.pallas_call(
        functools.partial(conv_kernel, order),
        in_specs=[smem] + [vmem] * (shares + 4),
        out_specs=[vmem] * 3,
        out_shape=[share, columns, columns],
        scratch_shapes=[
            pltpu.VMEM((block, 2 * LANES), jnp.bfloat16),
            pltpu.VMEM((4, block, LANES), jnp.bfloat16),
        ],
        compiler_params=pltpu.CompilerParams(vmem_limit_bytes=24 << 20),
        cost_estimate=pl.CostEstimate(flops=50 * block * block * LANES, bytes_accessed=8 * block * block, transcendentals=0),
        name="convolve",
    )(
        me, *data, block_cos, block_sin,
        jnp.asarray(np.cos(turn).astype(np.float32)), jnp.asarray(np.sin(turn).astype(np.float32)),
    )
    other = swap(other, "seq", 1)
    mine = pl.pallas_call(
        rest_kernel,
        in_specs=[smem] + [vmem] * 4,
        out_specs=vmem,
        out_shape=share,
        compiler_params=pltpu.CompilerParams(vmem_limit_bytes=24 << 20),
        cost_estimate=pl.CostEstimate(flops=4 * block * block * LANES, bytes_accessed=4 * block * block, transcendentals=0),
        name="convolve_rest",
    )(me, rotated_re, rotated_im, block_cos, block_sin)
    return mine, other


def gate_kernel(chips, me_ref, *refs):
    held, (gate_ref, *outs, conv_ref) = refs[:len(chips)], refs[len(chips):]
    _, span, block_rows, _ = held[0].shape
    rows = span * block_rows
    for flip, ref in zip(chips, held):
        for core in range(2):
            share = me_ref[0] ^ (2 * flip + core)
            conv_ref[:, pl.ds(pl.multiple_of(share * LANES, LANES), LANES)] = ref[core].reshape(rows, LANES)
    conv = jnp.dot(join_rows(rows, span), conv_ref[...], preferred_element_type=jnp.float32)
    gated = (conv * gate_ref[...].astype(jnp.float32)).astype(jnp.bfloat16)
    part = rows // len(outs)
    for p, out_ref in enumerate(outs):
        out_ref[...] = gated[p * part:(p + 1) * part]


def gate(me, held, chips, gate_out, parts):
    rows, width = gate_out.shape
    vmem = pl.BlockSpec(memory_space=pltpu.VMEM)
    return pl.pallas_call(
        functools.partial(gate_kernel, chips),
        in_specs=[pl.BlockSpec(memory_space=pltpu.SMEM)] + [vmem] * (len(held) + 1),
        out_specs=[vmem] * parts,
        out_shape=[jax.ShapeDtypeStruct((rows // parts, width), jnp.bfloat16)] * parts,
        scratch_shapes=[pltpu.VMEM((rows, width), jnp.bfloat16)],
        compiler_params=pltpu.CompilerParams(vmem_limit_bytes=16 << 20),
        name="gate",
    )(me, *held, gate_out)


def own_kernel(me_ref, *refs):
    parts = (len(refs) - 1) // 2
    gated, slabs, out_ref = refs[:parts], refs[parts:-1], refs[-1]
    rows, depth = gated[0].shape[0], slabs[0].shape[0]
    for p, gated_ref in enumerate(gated):
        out_ref[0, p * rows:(p + 1) * rows] = sum(
            jnp.dot(gated_ref[:, i * depth:(i + 1) * depth], slab[...], preferred_element_type=jnp.float32)
            for i, slab in enumerate(slabs)
        )


def own_part(me, gated, weight, blocks):
    parts = len(gated)
    part_rows, depth = gated[0].shape
    cols = weight.shape[1] // 8

    def column(slab, i, me_ref):
        flip = sum((jnp.where(i == place, f, 0) for place, (f, _) in enumerate(blocks)), 0)
        half = sum((jnp.where(i == place, h, 0) for place, (_, h) in enumerate(blocks)), 0)
        return slab, (me_ref[0] ^ flip) * 2 + half

    return pl.pallas_call(
        own_kernel,
        grid_spec=pltpu.PrefetchScalarGridSpec(
            num_scalar_prefetch=1,
            grid=(len(blocks),),
            in_specs=[pl.BlockSpec((part_rows, depth), lambda i, m: (0, 0))] * parts
            + [pl.BlockSpec((depth // parts, cols), functools.partial(column, slab)) for slab in range(parts)],
            out_specs=pl.BlockSpec((1, parts * part_rows, cols), lambda i, m: (i, 0, 0)),
        ),
        out_shape=jax.ShapeDtypeStruct((len(blocks), parts * part_rows, cols), jnp.float32),
        compiler_params=pltpu.CompilerParams(vmem_limit_bytes=40 << 20),
        cost_estimate=pl.CostEstimate(
            flops=2 * parts * part_rows * depth * cols * len(blocks),
            bytes_accessed=2 * depth * cols * len(blocks), transcendentals=0,
        ),
        name="own_part",
    )(me, *gated, *[weight] * parts)


def add_kernel(parts, kept, core_ref, own_ref, *refs):
    moved, refs = refs[:2 * parts], refs[2 * parts:]
    weights, (a_ref, b_ref, held_ref, sems) = refs[:4], refs[4:]
    slabs = sems.shape[1]
    depth = held_ref.shape[1] // slabs

    def copies(side, take_mine):
        source = weights[2 * side] if take_mine else weights[2 * side + 1]
        return [
            pltpu.make_async_copy(
                source.at[i * depth:(i + 1) * depth], held_ref.at[side, i * depth:(i + 1) * depth], sems.at[side, i]
            )
            for i in range(slabs)
        ]

    mine_core = 0 if kept else 1
    for side in range(2):

        @pl.when(core_ref[0] == mine_core)
        def _():
            for copy in copies(side, True):
                copy.start()

        @pl.when(core_ref[0] != mine_core)
        def _():
            for copy in copies(side, False):
                copy.start()

    rows = moved[0].shape[0]
    for side, out_ref in enumerate((a_ref, b_ref)):
        for i, copy in enumerate(copies(side, True)):
            copy.wait()
        for p in range(parts):
            at = slice(p * rows, (p + 1) * rows)
            total = own_ref[side, at] + jnp.dot(
                moved[side * parts + p][...], held_ref[side], preferred_element_type=jnp.float32
            )
            out_ref[at] = total.astype(out_ref.dtype)


def add_moved(core, own, moved_x, moved_y, weights, first, kept, dtype):
    parts = len(moved_x)
    rows, depth = moved_x[0].shape
    cols = own.shape[2]
    whole = pl.BlockSpec((rows, depth), lambda i: (0, 0))
    shape = jax.ShapeDtypeStruct((parts * rows, cols), dtype)
    out = pl.BlockSpec((parts * rows, cols), lambda i: (0, 0))
    return pl.pallas_call(
        functools.partial(add_kernel, parts, kept),
        grid=(1,),
        in_specs=[
            pl.BlockSpec(memory_space=pltpu.SMEM),
            pl.BlockSpec((2, parts * rows, cols), lambda i: (0, first, 0)),
        ]
        + [whole] * (2 * parts)
        + [pl.BlockSpec(memory_space=pl.ANY)] * 4,
        out_specs=[out, out],
        out_shape=[shape, shape],
        scratch_shapes=[pltpu.VMEM((2, depth, cols), jnp.bfloat16), pltpu.SemaphoreType.DMA((2, 4))],
        compiler_params=pltpu.CompilerParams(vmem_limit_bytes=40 << 20),
        cost_estimate=pl.CostEstimate(
            flops=4 * parts * rows * depth * cols, bytes_accessed=4 * depth * cols, transcendentals=0
        ),
        name="add_kept" if kept else "add_sent",
    )(core, own, *moved_x, *moved_y, *weights)


def finish_kernel(kept_ref, sum_ref, *refs):
    out_ref = refs[-1]
    out_ref[...] = (kept_ref[...] + sum_ref[...].astype(jnp.float32)).astype(out_ref.dtype)


def finish(kept, summed, part, side, before):
    rows, cols = summed.shape
    earlier = [] if before is None else [before]
    return pl.pallas_call(
        finish_kernel,
        grid=(1,),
        in_specs=[pl.BlockSpec((rows, cols), lambda i: (part, 0)), pl.BlockSpec((rows, cols), lambda i: (0, 0))]
        + [pl.BlockSpec(memory_space=pl.ANY)] * len(earlier),
        out_specs=pl.BlockSpec((rows, cols), lambda i: (part, side)),
        out_shape=jax.ShapeDtypeStruct((kept.shape[0], 2 * cols), jnp.bfloat16),
        input_output_aliases={2: 0} if earlier else {},
        compiler_params=pltpu.CompilerParams(vmem_limit_bytes=16 << 20),
        name="finish",
    )(kept, summed, *earlier)


def swap(data, axis, flip):
    return lax.ppermute(data, axis, [(i, i ^ flip) for i in range(lax.axis_size(axis))])


def by_channels(values, gate_in, gate_out, spectrum, out_weight):
    seq_count = lax.axis_size("seq")
    here = lax.axis_index("seq").astype(jnp.int32)
    me = lax.axis_index("chan").astype(jnp.int32)
    core = here % 2
    parts = 2

    order = tuple(sorted(range(seq_count), key=lambda m: (m == 0, m == 1, m % 2, -m)))
    packed = list(pack(here.reshape(1), values, gate_in, spectrum, seq_count))
    places = jnp.stack([(me ^ (1 + 2 * core)) * 2, (me ^ (2 + core)) * 2 + 1])
    _, places = lax.optimization_barrier((packed, places))
    block_x, block_y = take_blocks(places, out_weight)
    late = [m for m in order if m % 2]
    weight_x, weight_y = swap(block_x, "chan", 1), swap(block_y, "chan", 2)
    data = {m: swap(packed[m], "seq", m) if m else packed[m] for m in order if m % 2 == 0}
    held, data[order[0]] = lax.optimization_barrier(([packed[m] for m in late], data[order[0]]))
    data.update({m: swap(mine, "seq", m) for m, mine in zip(late, held)})
    mine, other = convolve(here.reshape(1), [data[m] for m in order], order)
    held = [jnp.stack([mine[flip], other[flip]]) for flip in range(seq_count // 2)]
    chips = tuple(reversed(range(seq_count // 2)))
    held = [swap(held[flip], "seq", 2 * flip) if flip else held[flip] for flip in chips]
    gated = gate(here.reshape(1), held, chips, gate_out, parts)
    weight_x, weight_y, _ = lax.optimization_barrier((weight_x, weight_y, gated))
    weights = [weight_x, swap(weight_x, "seq", 1), weight_y, swap(weight_y, "seq", 1)]
    own = own_part(me.reshape(1), gated, out_weight, ((2, 0), (1, 1)))
    core = core.reshape(1)
    moved_x, moved_y = [], []
    for p in range(parts):
        mine = gated[p]
        if p:
            mine, own, weights[1] = lax.optimization_barrier((mine, own, weights[1]))
        moved_x.append(swap(mine, "chan", 1))
        moved_y.append(swap(mine, "chan", 2))
    sums_a, sums_b = [], []
    for p in range(parts):
        if p == parts - 1:
            own_kept = own_part(me.reshape(1), gated, out_weight, ((0, 0), (0, 1)))
            own, own_kept = lax.optimization_barrier((own, own_kept))
        sent = add_moved(core, own, moved_x[p:p + 1], moved_y[p:p + 1], weights, p, False, jnp.bfloat16)
        sums_a.append(swap(sent[0], "chan", 2))
        sums_b.append(swap(sent[1], "chan", 1))
    kept_a, kept_b = add_moved(core, own_kept, moved_x, moved_y, weights, 0, True, jnp.float32)
    mixed = None
    for p in range(parts):
        mixed = finish(kept_a, sums_a[p], p, 0, mixed)
        mixed = finish(kept_b, sums_b[p], p, 1, mixed)
    return mixed


def to_columns(data):
    return lax.all_to_all(data, "seq", split_axis=2, concat_axis=1, tiled=True)


def to_rows(data):
    return lax.all_to_all(data, "seq", split_axis=1, concat_axis=2, tiled=True)


def by_frequencies(values, gate_in, gate_out, spectrum, out_weight):
    seq_count = lax.axis_size("seq")
    seq_index = lax.axis_index("seq")
    tok_rows, chan_width = values.shape
    block_rows = BLOCK // seq_count
    span = tok_rows // block_rows
    tokens_all = BLOCK * span
    col_share = span * chan_width // seq_count
    block_cos = rounded(np.cos(angles(BLOCK, BLOCK, BLOCK)))
    block_sin = rounded(np.sin(angles(BLOCK, BLOCK, BLOCK)))
    span_cos = rounded(np.cos(angles(span, span, span)))
    span_sin = rounded(np.sin(angles(span, span, span)))
    turn_all = angles(BLOCK, span, tokens_all)
    turn_cos_all = jnp.asarray(np.cos(turn_all).astype(np.float32))
    turn_sin_all = jnp.asarray(np.sin(turn_all).astype(np.float32))
    source = (values.astype(jnp.float32) * gate_in.astype(jnp.float32)).astype(jnp.bfloat16)
    spread = to_columns(source.reshape(1, block_rows, seq_count, col_share))
    columns = spread.reshape(BLOCK, col_share)
    cos_part = jnp.dot(jnp.transpose(block_cos), columns, preferred_element_type=jnp.float32)
    sin_part = jnp.dot(jnp.transpose(block_sin), columns, preferred_element_type=jnp.float32)
    col_pos = (seq_index * col_share + jnp.arange(col_share, dtype=jnp.int32)) // chan_width
    turn_cos = jnp.take(turn_cos_all, col_pos, axis=1)
    turn_sin = jnp.take(turn_sin_all, col_pos, axis=1)
    twist_re = cos_part * turn_cos - sin_part * turn_sin
    twist_im = -sin_part * turn_cos - cos_part * turn_sin
    twisted = jnp.stack([twist_re, twist_im]).astype(jnp.bfloat16)
    arranged = to_rows(twisted).reshape(2, block_rows, span, chan_width)
    with_cos = jnp.einsum("bd,kcbh->kdch", span_cos, arranged, preferred_element_type=jnp.float32)
    with_sin = jnp.einsum("bd,kcbh->kdch", span_sin, arranged, preferred_element_type=jnp.float32)
    freq_re = with_cos[0] + with_sin[1]
    freq_im = with_cos[1] - with_sin[0]
    prod_re = freq_re * spectrum[0] - freq_im * spectrum[1]
    prod_im = freq_re * spectrum[1] + freq_im * spectrum[0]
    product = jnp.stack([prod_re, prod_im]).astype(jnp.bfloat16)
    back_cos = jnp.einsum("db,kdch->kcbh", span_cos, product, preferred_element_type=jnp.float32)
    back_sin = jnp.einsum("db,kdch->kcbh", span_sin, product, preferred_element_type=jnp.float32)
    back_re = (back_cos[0] - back_sin[1]) / span
    back_im = (back_cos[1] + back_sin[0]) / span
    back_tc = lax.dynamic_slice_in_dim(turn_cos_all, seq_index * block_rows, block_rows)[:, :, None]
    back_ts = lax.dynamic_slice_in_dim(turn_sin_all, seq_index * block_rows, block_rows)[:, :, None]
    rotated = jnp.stack(
        [back_re * back_tc - back_im * back_ts, back_im * back_tc + back_re * back_ts]
    ).astype(jnp.bfloat16)
    gathered = to_columns(rotated.reshape(2, block_rows, seq_count, col_share)).reshape(2, BLOCK, col_share)
    summed = jnp.dot(block_cos, gathered[0], preferred_element_type=jnp.float32)
    summed = summed - jnp.dot(block_sin, gathered[1], preferred_element_type=jnp.float32)
    ordered = (summed / BLOCK).astype(jnp.bfloat16).reshape(1, BLOCK, col_share)
    conv = to_rows(ordered).reshape(tok_rows, chan_width)
    gated = (conv.astype(jnp.float32) * gate_out.astype(jnp.float32)).astype(jnp.bfloat16)
    partial_sum = jnp.dot(gated, out_weight, preferred_element_type=jnp.float32)
    return lax.psum_scatter(partial_sum.astype(jnp.bfloat16), "chan", scatter_dimension=1, tiled=True)


def shards(values, gate_in, gate_out, spectrum, out_weight):
    seq_count, chan_count = lax.axis_size("seq"), lax.axis_size("chan")
    _, span, block_rows, width = spectrum.shape
    one_lane_block = width == seq_count * LANES and block_rows % 32 == 0
    if span == 2 and chan_count == 4 and seq_count & (seq_count - 1) == 0 and one_lane_block:
        return by_channels(values, gate_in, gate_out, spectrum, out_weight)
    return by_frequencies(values, gate_in, gate_out, spectrum, out_weight)


def solution(mesh):
    placed = (
        P("seq", "chan"),
        P("seq", "chan"),
        P("seq", "chan"),
        P(None, None, "seq", "chan"),
        P("chan", None),
    )
    return jax.shard_map(
        shards, mesh=mesh, in_specs=placed, out_specs=P("seq", "chan"), check_vma=False
    )
```

```python
import functools
import math

import jax
import jax.numpy as jnp
import ml_dtypes
import numpy as np
from jax import lax
from jax.experimental import pallas as pl
from jax.experimental.pallas import tpu as pltpu
from jax.sharding import PartitionSpec as P

BLOCK = 1024
LANES = 128


def angles(first, second, period):
    return (np.arange(first)[:, None] * np.arange(second)[None, :] % period) * (2.0 * math.pi / period)


def rounded(table):
    return jnp.asarray(table.astype(np.float32).astype(ml_dtypes.bfloat16))


def split_rows(rows, span):
    out = lax.broadcasted_iota(jnp.int32, (rows, rows), 0)
    token = lax.broadcasted_iota(jnp.int32, (rows, rows), 1)
    block_rows = rows // span
    return jnp.where(token == (out % block_rows) * span + out // block_rows, 1.0, 0.0).astype(jnp.bfloat16)


def join_rows(rows, span):
    token = lax.broadcasted_iota(jnp.int32, (rows, rows), 0)
    held = lax.broadcasted_iota(jnp.int32, (rows, rows), 1)
    block_rows = rows // span
    return jnp.where(token == (held % block_rows) * span + held // block_rows, 1.0, 0.0).astype(jnp.bfloat16)


def pack_kernel(span, me_ref, values_hbm, gate_hbm, spectrum_hbm, *refs):
    outs, (values_ref, gate_ref, spectrum_ref, sems) = refs[:-4], refs[-4:]
    copies = [
        pltpu.make_async_copy(values_hbm, values_ref, sems.at[0]),
        pltpu.make_async_copy(gate_hbm, gate_ref, sems.at[1]),
    ]
    for part in range(2):
        for d in range(span):
            copies.append(pltpu.make_async_copy(
                spectrum_hbm.at[part, d], spectrum_ref.at[part * span + d], sems.at[2 + part * span + d]
            ))
    for copy in copies:
        copy.start()
    me = me_ref[0]
    rows = values_ref.shape[0]
    block_rows = rows // span
    copies[0].wait()
    copies[1].wait()
    source = (values_ref[...].astype(jnp.float32) * gate_ref[...].astype(jnp.float32)).astype(jnp.bfloat16)
    values_ref[...] = jnp.dot(
        split_rows(rows, span), source, preferred_element_type=jnp.float32
    ).astype(jnp.bfloat16)

    def lanes_of(m):
        return pl.ds(pl.multiple_of((me ^ m) * LANES, LANES), LANES)

    for m, out_ref in enumerate(outs):
        for b in range(span):
            out_ref[2 * span + b] = values_ref[b * block_rows:(b + 1) * block_rows, lanes_of(m)]
    for part in range(2 * span):
        copies[2 + part].wait()
        for m, out_ref in enumerate(outs):
            out_ref[part] = spectrum_ref[part, :, lanes_of(m)].astype(jnp.bfloat16)


def pack(me, values, gate_in, spectrum, shares):
    rows, width = values.shape
    _, span, block_rows, _ = spectrum.shape
    shape = (3 * span, block_rows, LANES)
    vmem, hbm = pl.BlockSpec(memory_space=pltpu.VMEM), pl.BlockSpec(memory_space=pltpu.HBM)
    return pl.pallas_call(
        functools.partial(pack_kernel, span),
        in_specs=[pl.BlockSpec(memory_space=pltpu.SMEM), hbm, hbm, hbm],
        out_specs=[vmem] * shares,
        out_shape=[jax.ShapeDtypeStruct(shape, jnp.bfloat16)] * shares,
        scratch_shapes=[
            pltpu.VMEM((rows, width), jnp.bfloat16),
            pltpu.VMEM((rows, width), jnp.bfloat16),
            pltpu.VMEM((2 * span, block_rows, width), jnp.float32),
            pltpu.SemaphoreType.DMA((2 + 2 * span,)),
        ],
        compiler_params=pltpu.CompilerParams(vmem_limit_bytes=60 << 20),
        name="pack",
    )(me, values, gate_in, spectrum)


def take_kernel(places_ref, weight_hbm, *refs):
    outs, sems = refs[:-1], refs[-1]
    slabs = sems.shape[1]
    depth, cols = outs[0].shape[0] // slabs, outs[0].shape[1]
    copies = [
        pltpu.make_async_copy(
            weight_hbm.at[i * depth:(i + 1) * depth, pl.ds(pl.multiple_of(places_ref[k] * cols, cols), cols)],
            out_ref.at[i * depth:(i + 1) * depth],
            sems.at[k, i],
        )
        for k, out_ref in enumerate(outs)
        for i in range(slabs)
    ]
    for copy in copies:
        copy.start()
    for copy in copies:
        copy.wait()


def take_blocks(places, weight):
    depth, cols = weight.shape[0], weight.shape[1] // 8
    count, slabs = places.shape[0], 4
    return pl.pallas_call(
        take_kernel,
        in_specs=[pl.BlockSpec(memory_space=pltpu.SMEM), pl.BlockSpec(memory_space=pltpu.HBM)],
        out_specs=[pl.BlockSpec(memory_space=pltpu.VMEM)] * count,
        out_shape=[jax.ShapeDtypeStruct((depth, cols), weight.dtype)] * count,
        scratch_shapes=[pltpu.SemaphoreType.DMA((count, slabs))],
        compiler_params=pltpu.CompilerParams(vmem_limit_bytes=48 << 20),
        cost_estimate=pl.CostEstimate(flops=0, bytes_accessed=128 * depth * cols, transcendentals=0),
        name="take_blocks",
    )(places, weight)


def conv_kernel(order, me_ref, *refs):
    shares = len(order)
    data, (cos_ref, sin_ref, turn_cos_ref, turn_sin_ref) = refs[:shares], refs[shares:shares + 4]
    other_ref, re_ref, im_ref, cols_ref, filt_ref = refs[shares + 4:]
    me = me_ref[0]
    rows = data[0].shape[1]
    for m, ref in zip(order, data):
        at = pl.ds(pl.multiple_of((me ^ m) * rows, rows), rows)
        for b in range(2):
            cols_ref[at, b * LANES:(b + 1) * LANES] = ref[4 + b]
        for part in range(4):
            filt_ref[part, at, :] = ref[part]
    step = 2 * rows
    for i in range(shares * rows // step):
        at = slice(i * step, (i + 1) * step)
        first_re = jnp.dot(cos_ref[at, :], cols_ref[...], preferred_element_type=jnp.float32)
        first_sin = jnp.dot(sin_ref[at, :], cols_ref[...], preferred_element_type=jnp.float32)
        tc, ts = turn_cos_ref[at, :], turn_sin_ref[at, :]
        re0, im0 = first_re[:, :LANES], -first_sin[:, :LANES]
        re1, im1 = first_re[:, LANES:], -first_sin[:, LANES:]
        re1, im1 = re1 * tc + im1 * ts, im1 * tc - re1 * ts
        f0r, f0i, f1r, f1i = re0 + re1, im0 + im1, re0 - re1, im0 - im1
        s0r, s1r, s0i, s1i = (filt_ref[part, at, :].astype(jnp.float32) for part in range(4))
        p0r, p0i = f0r * s0r - f0i * s0i, f0r * s0i + f0i * s0r
        p1r, p1i = f1r * s1r - f1i * s1i, f1r * s1i + f1i * s1r
        b0r, b0i = 0.5 * (p0r + p1r), 0.5 * (p0i + p1i)
        b1r, b1i = 0.5 * (p0r - p1r), 0.5 * (p0i - p1i)
        b1r, b1i = b1r * tc - b1i * ts, b1i * tc + b1r * ts
        re_ref[at, :] = jnp.concatenate([b0r, b1r], axis=1).astype(jnp.bfloat16)
        im_ref[at, :] = jnp.concatenate([b0i, b1i], axis=1).astype(jnp.bfloat16)
    invert(me, 1, cos_ref, sin_ref, re_ref, im_ref, other_ref)


def invert(me, flip, cos_ref, sin_ref, re_ref, im_ref, out_ref):
    chips, _, rows, _ = out_ref.shape
    scale = 1.0 / (2 * chips * rows)
    for i in range(chips):
        at = pl.ds(pl.multiple_of((me ^ (2 * i + flip)) * rows, rows), rows)
        conv = jnp.dot(cos_ref[at, :], re_ref[...], preferred_element_type=jnp.float32)
        conv = conv - jnp.dot(sin_ref[at, :], im_ref[...], preferred_element_type=jnp.float32)
        conv = (conv * scale).astype(jnp.bfloat16)
        for b in range(2):
            out_ref[i, b] = conv[:, b * LANES:(b + 1) * LANES]


def rest_kernel(me_ref, re_ref, im_ref, cos_ref, sin_ref, out_ref):
    invert(me_ref[0], 0, cos_ref, sin_ref, re_ref, im_ref, out_ref)


def convolve(me, data, order):
    shares = len(data)
    rows = data[0].shape[1]
    block = shares * rows
    angle = angles(block, block, block)
    turn = np.broadcast_to(angles(block, 2, 2 * block)[:, 1:], (block, LANES))
    vmem, smem = pl.BlockSpec(memory_space=pltpu.VMEM), pl.BlockSpec(memory_space=pltpu.SMEM)
    share = jax.ShapeDtypeStruct((shares // 2, 2, rows, LANES), jnp.bfloat16)
    columns = jax.ShapeDtypeStruct((block, 2 * LANES), jnp.bfloat16)
    block_cos, block_sin = rounded(np.cos(angle)), rounded(np.sin(angle))
    other, rotated_re, rotated_im = pl.pallas_call(
        functools.partial(conv_kernel, order),
        in_specs=[smem] + [vmem] * (shares + 4),
        out_specs=[vmem] * 3,
        out_shape=[share, columns, columns],
        scratch_shapes=[
            pltpu.VMEM((block, 2 * LANES), jnp.bfloat16),
            pltpu.VMEM((4, block, LANES), jnp.bfloat16),
        ],
        compiler_params=pltpu.CompilerParams(vmem_limit_bytes=24 << 20),
        cost_estimate=pl.CostEstimate(flops=50 * block * block * LANES, bytes_accessed=8 * block * block, transcendentals=0),
        name="convolve",
    )(
        me, *data, block_cos, block_sin,
        jnp.asarray(np.cos(turn).astype(np.float32)), jnp.asarray(np.sin(turn).astype(np.float32)),
    )
    other = swap(other, "seq", 1)
    mine = pl.pallas_call(
        rest_kernel,
        in_specs=[smem] + [vmem] * 4,
        out_specs=vmem,
        out_shape=share,
        compiler_params=pltpu.CompilerParams(vmem_limit_bytes=24 << 20),
        cost_estimate=pl.CostEstimate(flops=4 * block * block * LANES, bytes_accessed=4 * block * block, transcendentals=0),
        name="convolve_rest",
    )(me, rotated_re, rotated_im, block_cos, block_sin)
    return mine, other


def gate_kernel(chips, me_ref, *refs):
    held, (gate_ref, *outs, conv_ref) = refs[:len(chips)], refs[len(chips):]
    _, span, block_rows, _ = held[0].shape
    rows = span * block_rows
    for flip, ref in zip(chips, held):
        for core in range(2):
            share = me_ref[0] ^ (2 * flip + core)
            conv_ref[:, pl.ds(pl.multiple_of(share * LANES, LANES), LANES)] = ref[core].reshape(rows, LANES)
    conv = jnp.dot(join_rows(rows, span), conv_ref[...], preferred_element_type=jnp.float32)
    gated = (conv * gate_ref[...].astype(jnp.float32)).astype(jnp.bfloat16)
    part = rows // len(outs)
    for p, out_ref in enumerate(outs):
        out_ref[...] = gated[p * part:(p + 1) * part]


def gate(me, held, chips, gate_out, parts):
    rows, width = gate_out.shape
    vmem = pl.BlockSpec(memory_space=pltpu.VMEM)
    return pl.pallas_call(
        functools.partial(gate_kernel, chips),
        in_specs=[pl.BlockSpec(memory_space=pltpu.SMEM)] + [vmem] * (len(held) + 1),
        out_specs=[vmem] * parts,
        out_shape=[jax.ShapeDtypeStruct((rows // parts, width), jnp.bfloat16)] * parts,
        scratch_shapes=[pltpu.VMEM((rows, width), jnp.bfloat16)],
        compiler_params=pltpu.CompilerParams(vmem_limit_bytes=16 << 20),
        name="gate",
    )(me, *held, gate_out)


def own_kernel(parts, me_ref, *refs):
    gated, slabs, out_ref = refs[:parts], refs[parts:-1], refs[-1]
    rows, depth = gated[0].shape[0], slabs[0].shape[0]
    for p, gated_ref in enumerate(gated):
        out_ref[0, p * rows:(p + 1) * rows] = sum(
            jnp.dot(gated_ref[:, i * depth:(i + 1) * depth], slab[...], preferred_element_type=jnp.float32)
            for i, slab in enumerate(slabs)
        )


def own_part(me, gated, weight, blocks):
    parts, slabs = len(gated), 4
    part_rows, depth = gated[0].shape
    cols = weight.shape[1] // 8

    def column(slab, i, me_ref):
        flip = sum((jnp.where(i == place, f, 0) for place, (f, _) in enumerate(blocks)), 0)
        half = sum((jnp.where(i == place, h, 0) for place, (_, h) in enumerate(blocks)), 0)
        return slab, (me_ref[0] ^ flip) * 2 + half

    return pl.pallas_call(
        functools.partial(own_kernel, parts),
        grid_spec=pltpu.PrefetchScalarGridSpec(
            num_scalar_prefetch=1,
            grid=(len(blocks),),
            in_specs=[pl.BlockSpec((part_rows, depth), lambda i, m: (0, 0))] * parts
            + [pl.BlockSpec((depth // slabs, cols), functools.partial(column, slab)) for slab in range(slabs)],
            out_specs=pl.BlockSpec((1, parts * part_rows, cols), lambda i, m: (i, 0, 0)),
        ),
        out_shape=jax.ShapeDtypeStruct((len(blocks), parts * part_rows, cols), jnp.float32),
        compiler_params=pltpu.CompilerParams(vmem_limit_bytes=40 << 20),
        cost_estimate=pl.CostEstimate(
            flops=2 * parts * part_rows * depth * cols * len(blocks),
            bytes_accessed=2 * depth * cols * len(blocks), transcendentals=0,
        ),
        name="own_part",
    )(me, *gated, *[weight] * slabs)


def add_kernel(parts, kept, core_ref, own_ref, *refs):
    moved, refs = refs[:2 * parts], refs[2 * parts:]
    weights, (a_ref, b_ref, held_ref, sems) = refs[:4], refs[4:]
    slabs = sems.shape[1]
    depth = held_ref.shape[1] // slabs

    def copies(side, take_mine):
        source = weights[2 * side] if take_mine else weights[2 * side + 1]
        return [
            pltpu.make_async_copy(
                source.at[i * depth:(i + 1) * depth], held_ref.at[side, i * depth:(i + 1) * depth], sems.at[side, i]
            )
            for i in range(slabs)
        ]

    mine_core = 0 if kept else 1
    for side in range(2):

        @pl.when(core_ref[0] == mine_core)
        def _():
            for copy in copies(side, True):
                copy.start()

        @pl.when(core_ref[0] != mine_core)
        def _():
            for copy in copies(side, False):
                copy.start()

    rows = moved[0].shape[0]
    for side, out_ref in enumerate((a_ref, b_ref)):
        for i, copy in enumerate(copies(side, True)):
            copy.wait()
        for p in range(parts):
            at = slice(p * rows, (p + 1) * rows)
            total = own_ref[side, at] + jnp.dot(
                moved[side * parts + p][...], held_ref[side], preferred_element_type=jnp.float32
            )
            out_ref[at] = total.astype(out_ref.dtype)


def add_moved(core, own, moved_x, moved_y, weights, first, kept, dtype):
    parts = len(moved_x)
    rows, depth = moved_x[0].shape
    cols = own.shape[2]
    whole = pl.BlockSpec((rows, depth), lambda i: (0, 0))
    shape = jax.ShapeDtypeStruct((parts * rows, cols), dtype)
    out = pl.BlockSpec((parts * rows, cols), lambda i: (0, 0))
    return pl.pallas_call(
        functools.partial(add_kernel, parts, kept),
        grid=(1,),
        in_specs=[
            pl.BlockSpec(memory_space=pltpu.SMEM),
            pl.BlockSpec((2, parts * rows, cols), lambda i: (0, first, 0)),
        ]
        + [whole] * (2 * parts)
        + [pl.BlockSpec(memory_space=pl.ANY)] * 4,
        out_specs=[out, out],
        out_shape=[shape, shape],
        scratch_shapes=[pltpu.VMEM((2, depth, cols), jnp.bfloat16), pltpu.SemaphoreType.DMA((2, 4))],
        compiler_params=pltpu.CompilerParams(vmem_limit_bytes=40 << 20),
        cost_estimate=pl.CostEstimate(
            flops=4 * parts * rows * depth * cols, bytes_accessed=4 * depth * cols, transcendentals=0
        ),
        name="add_kept" if kept else "add_sent",
    )(core, own, *moved_x, *moved_y, *weights)


def finish_kernel(kept_a_ref, kept_b_ref, sum_a_ref, sum_b_ref, *refs):
    out_ref = refs[-1]
    cols = kept_a_ref.shape[1]
    out_ref[:, :cols] = (kept_a_ref[...] + sum_a_ref[...].astype(jnp.float32)).astype(out_ref.dtype)
    out_ref[:, cols:] = (kept_b_ref[...] + sum_b_ref[...].astype(jnp.float32)).astype(out_ref.dtype)


def finish(kept_a, kept_b, sum_a, sum_b, part, before):
    rows, cols = sum_a.shape
    total = kept_a.shape[0]
    kept = pl.BlockSpec((rows, cols), lambda i: (part, 0))
    sums = pl.BlockSpec((rows, cols), lambda i: (0, 0))
    earlier = [] if before is None else [before]
    return pl.pallas_call(
        finish_kernel,
        grid=(1,),
        in_specs=[kept, kept, sums, sums] + [pl.BlockSpec(memory_space=pl.ANY)] * len(earlier),
        out_specs=pl.BlockSpec((rows, 2 * cols), lambda i: (part, 0)),
        out_shape=jax.ShapeDtypeStruct((total, 2 * cols), jnp.bfloat16),
        input_output_aliases={4: 0} if earlier else {},
        compiler_params=pltpu.CompilerParams(vmem_limit_bytes=16 << 20),
        name="finish",
    )(kept_a, kept_b, sum_a, sum_b, *earlier)


def swap(data, axis, flip):
    return lax.ppermute(data, axis, [(i, i ^ flip) for i in range(lax.axis_size(axis))])


def by_channels(values, gate_in, gate_out, spectrum, out_weight):
    seq_count = lax.axis_size("seq")
    here = lax.axis_index("seq").astype(jnp.int32)
    me = lax.axis_index("chan").astype(jnp.int32)
    core = here % 2
    parts = 2

    order = tuple(sorted(range(seq_count), key=lambda m: (m == 0, m == 1, m % 2, -m)))
    packed = list(pack(here.reshape(1), values, gate_in, spectrum, seq_count))
    places = jnp.stack([(me ^ (1 + 2 * core)) * 2, (me ^ (2 + core)) * 2 + 1])
    _, places = lax.optimization_barrier((packed, places))
    block_x, block_y = take_blocks(places, out_weight)
    late = [m for m in order if m % 2]
    weight_x, weight_y = swap(block_x, "chan", 1), swap(block_y, "chan", 2)
    data = {m: swap(packed[m], "seq", m) if m else packed[m] for m in order if m % 2 == 0}
    held, data[order[0]] = lax.optimization_barrier(([packed[m] for m in late], data[order[0]]))
    data.update({m: swap(mine, "seq", m) for m, mine in zip(late, held)})
    mine, other = convolve(here.reshape(1), [data[m] for m in order], order)
    held = [jnp.stack([mine[flip], other[flip]]) for flip in range(seq_count // 2)]
    chips = tuple(reversed(range(seq_count // 2)))
    held = [swap(held[flip], "seq", 2 * flip) if flip else held[flip] for flip in chips]
    gated = gate(here.reshape(1), held, chips, gate_out, parts)
    weight_x, weight_y, _ = lax.optimization_barrier((weight_x, weight_y, gated))
    weights = [weight_x, swap(weight_x, "seq", 1), weight_y, swap(weight_y, "seq", 1)]
    own = own_part(me.reshape(1), gated, out_weight, ((2, 0), (1, 1)))
    core = core.reshape(1)
    moved_x, moved_y = [], []
    for p in range(parts):
        mine = gated[p]
        if p:
            mine, own, weights[1] = lax.optimization_barrier((mine, own, weights[1]))
        moved_x.append(swap(mine, "chan", 1))
        moved_y.append(swap(mine, "chan", 2))
    sums_a, sums_b = [], []
    for p in range(parts):
        if p == parts - 1:
            own_kept = own_part(me.reshape(1), gated, out_weight, ((0, 0), (0, 1)))
            own, own_kept = lax.optimization_barrier((own, own_kept))
        sent = add_moved(core, own, moved_x[p:p + 1], moved_y[p:p + 1], weights, p, False, jnp.bfloat16)
        sums_a.append(swap(sent[0], "chan", 2))
        sums_b.append(swap(sent[1], "chan", 1))
    kept_a, kept_b = add_moved(core, own_kept, moved_x, moved_y, weights, 0, True, jnp.float32)
    mixed = None
    for p in range(parts):
        mixed = finish(kept_a, kept_b, sums_a[p], sums_b[p], p, mixed)
    return mixed


def to_columns(data):
    return lax.all_to_all(data, "seq", split_axis=2, concat_axis=1, tiled=True)


def to_rows(data):
    return lax.all_to_all(data, "seq", split_axis=1, concat_axis=2, tiled=True)


def by_frequencies(values, gate_in, gate_out, spectrum, out_weight):
    seq_count = lax.axis_size("seq")
    seq_index = lax.axis_index("seq")
    tok_rows, chan_width = values.shape
    block_rows = BLOCK // seq_count
    span = tok_rows // block_rows
    tokens_all = BLOCK * span
    col_share = span * chan_width // seq_count
    block_cos = rounded(np.cos(angles(BLOCK, BLOCK, BLOCK)))
    block_sin = rounded(np.sin(angles(BLOCK, BLOCK, BLOCK)))
    span_cos = rounded(np.cos(angles(span, span, span)))
    span_sin = rounded(np.sin(angles(span, span, span)))
    turn_all = angles(BLOCK, span, tokens_all)
    turn_cos_all = jnp.asarray(np.cos(turn_all).astype(np.float32))
    turn_sin_all = jnp.asarray(np.sin(turn_all).astype(np.float32))
    source = (values.astype(jnp.float32) * gate_in.astype(jnp.float32)).astype(jnp.bfloat16)
    spread = to_columns(source.reshape(1, block_rows, seq_count, col_share))
    columns = spread.reshape(BLOCK, col_share)
    cos_part = jnp.dot(jnp.transpose(block_cos), columns, preferred_element_type=jnp.float32)
    sin_part = jnp.dot(jnp.transpose(block_sin), columns, preferred_element_type=jnp.float32)
    col_pos = (seq_index * col_share + jnp.arange(col_share, dtype=jnp.int32)) // chan_width
    turn_cos = jnp.take(turn_cos_all, col_pos, axis=1)
    turn_sin = jnp.take(turn_sin_all, col_pos, axis=1)
    twist_re = cos_part * turn_cos - sin_part * turn_sin
    twist_im = -sin_part * turn_cos - cos_part * turn_sin
    twisted = jnp.stack([twist_re, twist_im]).astype(jnp.bfloat16)
    arranged = to_rows(twisted).reshape(2, block_rows, span, chan_width)
    with_cos = jnp.einsum("bd,kcbh->kdch", span_cos, arranged, preferred_element_type=jnp.float32)
    with_sin = jnp.einsum("bd,kcbh->kdch", span_sin, arranged, preferred_element_type=jnp.float32)
    freq_re = with_cos[0] + with_sin[1]
    freq_im = with_cos[1] - with_sin[0]
    prod_re = freq_re * spectrum[0] - freq_im * spectrum[1]
    prod_im = freq_re * spectrum[1] + freq_im * spectrum[0]
    product = jnp.stack([prod_re, prod_im]).astype(jnp.bfloat16)
    back_cos = jnp.einsum("db,kdch->kcbh", span_cos, product, preferred_element_type=jnp.float32)
    back_sin = jnp.einsum("db,kdch->kcbh", span_sin, product, preferred_element_type=jnp.float32)
    back_re = (back_cos[0] - back_sin[1]) / span
    back_im = (back_cos[1] + back_sin[0]) / span
    back_tc = lax.dynamic_slice_in_dim(turn_cos_all, seq_index * block_rows, block_rows)[:, :, None]
    back_ts = lax.dynamic_slice_in_dim(turn_sin_all, seq_index * block_rows, block_rows)[:, :, None]
    rotated = jnp.stack(
        [back_re * back_tc - back_im * back_ts, back_im * back_tc + back_re * back_ts]
    ).astype(jnp.bfloat16)
    gathered = to_columns(rotated.reshape(2, block_rows, seq_count, col_share)).reshape(2, BLOCK, col_share)
    summed = jnp.dot(block_cos, gathered[0], preferred_element_type=jnp.float32)
    summed = summed - jnp.dot(block_sin, gathered[1], preferred_element_type=jnp.float32)
    ordered = (summed / BLOCK).astype(jnp.bfloat16).reshape(1, BLOCK, col_share)
    conv = to_rows(ordered).reshape(tok_rows, chan_width)
    gated = (conv.astype(jnp.float32) * gate_out.astype(jnp.float32)).astype(jnp.bfloat16)
    partial_sum = jnp.dot(gated, out_weight, preferred_element_type=jnp.float32)
    return lax.psum_scatter(partial_sum.astype(jnp.bfloat16), "chan", scatter_dimension=1, tiled=True)


def shards(values, gate_in, gate_out, spectrum, out_weight):
    seq_count, chan_count = lax.axis_size("seq"), lax.axis_size("chan")
    _, span, block_rows, width = spectrum.shape
    one_lane_block = width == seq_count * LANES and block_rows % 32 == 0
    if span == 2 and chan_count == 4 and seq_count & (seq_count - 1) == 0 and one_lane_block:
        return by_channels(values, gate_in, gate_out, spectrum, out_weight)
    return by_frequencies(values, gate_in, gate_out, spectrum, out_weight)


def solution(mesh):
    placed = (
        P("seq", "chan"),
        P("seq", "chan"),
        P("seq", "chan"),
        P(None, None, "seq", "chan"),
        P("chan", None),
    )
    return jax.shard_map(
        shards, mesh=mesh, in_specs=placed, out_specs=P("seq", "chan"), check_vma=False
    )
```
